32 devices in a mesh: image: 2 (over x), dom: 4 (over y, core), band: 4 (over z).
Axes of the slice: x: 2, y: 2, z: 4, core: 2. Of those that a mesh axis runs over, the one named last changes fastest.
Arguments:
- y_cur: float32 [8192, 2048], P(('image', 'dom'), 'band'), parts along dimension 0, may hold values from -6 to 6
- y_prev: float32 [8192, 2048], P(('image', 'dom'), 'band'), parts along dimension 0, may hold values from -3 to 3
- connect: int32 [4096, 8], P('dom'), may hold values from 0 to 2047, as said below
- face_map: int32 [4096], P('dom'), may hold values from 0 to 1023, as said below
- elem_scale: float32 [4096], P('dom'), may hold values from 0.5 to 2
- potential: float32 [8192], P(('image', 'dom')), parts along dimension 0, may hold values from 0 to 2
Outputs:
- y_next: float32 [8192, 2048], P(('image', 'dom'), 'band'), parts along dimension 0
- margin: float32 [4096, 2048], P(('image', 'band'), 'dom'), parts along dimension 0
- projected: float32 [4096, 2048], P(('image', 'band'), 'dom'), parts along dimension 0
The draws below stay inside these ranges and needn't reach their ends.
There are 2 independent parts, one for each index of `image`. The reference program is written for one: setup_inputs(seed, part) draws one part's arguments, and reference() takes and returns one part's arrays. A program takes and returns all parts, laid end to end along the dimension named above; an argument that names none is the same for every part. Nothing has to cross between parts.
Inputs may be any that keep to these rules, and one draw needn't show every extreme that they name: `connect`: each domain's 1024 nodes lie on one plane at positions q = 32 * j + k of a periodic 32 * 32 grid. Its 1024 elements, in arbitrary order, are the cells (j, k) between that plane and the next domain's plane (after the last domain comes the first). Corner 4 * a + 2 * b + c (a, b, c each 0 or 1) sits at position ((j + b) mod 32) * 32 + (k + c) mod 32; its entry is the local index of the domain's own node there when a = 0, and 1024 + that position on the next domain's plane when a = 1. `face_map`: each domain's 1024 entries list, for positions q = 0 to 1023 in order, the local index of the domain's node at position q: a permutation of 0 to 1023.
All inputs are finite; a program needn't handle non-finite values.
Results may differ from the reference program's by a relative error of at most 0.0003.
Values sent between devices are 32-bit elements; how exact they have to be, the bound alone decides.
No kernel may reach another device: no remote copies, remote signals or barrier semaphores. Data moves between devices by JAX's collectives and lax.ppermute only.
A program may use at most 128 MiB of HBM per device.

```python
import math
import jax
import jax.numpy as jnp
import numpy as np
from jax import lax

STATES = 2048
SIDE = 32
NODE_DEV = 1024
NODES = 4096
ELEMS = 4096


def grid_tables(key):
    node_dev = SIDE * SIDE
    domains = NODES // node_dev
    keys = jax.random.split(key, 2 * domains)
    perms = jax.vmap(lambda single: jax.random.permutation(single, node_dev))(keys[:domains])
    orders = jax.vmap(lambda single: jax.random.permutation(single, node_dev))(keys[domains:])
    return (perms.astype(jnp.int32), orders.astype(jnp.int32))


def draw_connect(key, part):
    perms, orders = grid_tables(key)
    node_dev = SIDE * SIDE
    cells = jnp.arange(node_dev, dtype=jnp.int32)
    grid_row = cells // SIDE
    grid_col = cells % SIDE
    corners = []
    for corner in range(8):
        normal_step = corner // 4
        row_step = corner // 2 % 2
        col_step = corner % 2
        place = (grid_row + row_step) % SIDE * SIDE + (grid_col + col_step) % SIDE
        if normal_step == 0:
            corners.append(perms[:, place])
        else:
            corners.append(jnp.broadcast_to(node_dev + place, perms.shape))
    table = jnp.stack(corners, axis=-1)
    table = jax.vmap(lambda cell_table, order: cell_table[order])(table, orders)
    return table.reshape(-1, 8).astype(jnp.int32)


def draw_face_map(key, part):
    perms, orders = grid_tables(key)
    return perms.reshape(-1).astype(jnp.int32)


def draw_y_cur(key, part):
    key = jax.random.fold_in(key, 7)
    keys = jax.random.split(key, 3)
    noise = 0.5 * jax.random.normal(keys[0], (NODES, STATES), jnp.float32)
    spatial = 0.5 * jax.random.normal(keys[1], (4, NODES), jnp.float32)
    mixing = 0.5 * jax.random.normal(keys[2], (4, STATES), jnp.float32)
    total = noise
    for member in range(4):
        total = total + spatial[member][:, None] * mixing[member][None, :]
    return jnp.clip(total, -6.0, 6.0)


def levels(rng, shape, cuts, smallest, largest):
    loudness = 1.0
    for axis_at, parts in cuts:
        steps = jax.random.uniform(jax.random.fold_in(jax.random.fold_in(rng, 6), axis_at), (parts,), jnp.float32, smallest / len(cuts), largest / len(cuts))
        loudness = loudness * jnp.repeat(jnp.exp(steps), shape[axis_at] // parts).reshape((-1,) + (1,) * (len(shape) - 1 - axis_at))
    return loudness


def normal_values(stream_key, extent, scale, limit, shards=(), kind=jnp.bfloat16):
    values = jax.random.normal(stream_key, extent, jnp.float32) * scale
    if len(shards) > 0:
        values = levels(stream_key, extent, shards, -0.22, 0.18) * values
    return jnp.clip(values, min=-limit, max=limit).astype(kind)


def setup_inputs(seed: int = 0, part: int = 0) -> dict:
    arg_keys = jax.random.split(jax.random.key(seed), 7)
    own_keys = jax.random.split(jax.random.fold_in(arg_keys[6], part), 7)
    y_cur = draw_y_cur(jax.random.fold_in(jax.random.fold_in(arg_keys[6], part), 71), part)
    y_prev = normal_values(own_keys[1], (NODES, STATES), 0.5, 3.0, ((0, 4), (1, 4)), jnp.float32)
    connect = draw_connect(jax.random.fold_in(arg_keys[6], 71), part)
    face_map = draw_face_map(jax.random.fold_in(arg_keys[6], 71), part)
    elem_scale = jnp.clip(jnp.exp(math.log(2.0) - 1.3862944 * jax.random.uniform(arg_keys[4], (ELEMS,), jnp.float32) ** levels(arg_keys[4], (ELEMS,), ((0, 4),), -0.2, 0.2)), 0.5, 2.0)
    potential = jnp.clip(2.0 * jax.random.uniform(own_keys[5], (NODES,), jnp.float32) ** levels(own_keys[5], (NODES,), ((0, 4),), -0.2, 0.2), 0.0, 2.0)
    return dict(y_cur=y_cur, y_prev=y_prev, connect=connect, face_map=face_map, elem_scale=elem_scale, potential=potential)


cheb_low = 1.0
cheb_high = 9.0


def element_matrix():
    stiff_line = np.array([[1.0, -1.0], [-1.0, 1.0]])
    mass_line = np.array([[1.0 / 3.0, 1.0 / 6.0], [1.0 / 6.0, 1.0 / 3.0]])
    total = np.kron(stiff_line, np.kron(mass_line, mass_line))
    total = total + np.kron(mass_line, np.kron(stiff_line, mass_line))
    total = total + np.kron(mass_line, np.kron(mass_line, stiff_line))
    return jnp.asarray(total, dtype=jnp.float32)


def global_nodes(connect, face_map):
    domains = NODES // NODE_DEV
    local = connect.reshape(domains, NODE_DEV, 8)
    faces = face_map.reshape(domains, NODE_DEV)
    next_faces = jnp.roll(faces, -1, axis=0)
    base = (jnp.arange(domains, dtype=jnp.int32) * NODE_DEV)[:, None, None]
    next_base = jnp.roll(base, -1, axis=0)
    halo_place = jnp.clip(local - NODE_DEV, 0, NODE_DEV - 1).astype(jnp.int32)
    halo_local = jax.vmap(lambda table, index: table[index])(next_faces, halo_place)
    joined = jnp.where(local < NODE_DEV, base + local, next_base + halo_local)
    return joined.reshape(-1, 8).astype(jnp.int32)


def apply_h(field, nodes, elem_scale, potential, stiff):
    width = min(STATES, 128)
    count = STATES // width

    def one_block(block):
        picked = block[nodes]
        local = jnp.einsum("ab,ebs->eas", stiff, picked, precision=lax.Precision.HIGHEST)
        local = local * elem_scale[:, None, None]
        summed = jnp.zeros_like(block).at[nodes.reshape(-1)].add(local.reshape(-1, width))
        return 0.5 * summed + potential[:, None] * block

    blocks = field.reshape(NODES, count, width).transpose(1, 0, 2)
    result = lax.map(one_block, blocks)
    return result.transpose(1, 0, 2).reshape(NODES, STATES)


def reference(y_cur, y_prev, connect, face_map, elem_scale, potential):
    stiff = element_matrix()
    nodes = global_nodes(connect, face_map)
    centre = 0.5 * (cheb_high + cheb_low)
    half_width = 0.5 * (cheb_high - cheb_low)
    applied = apply_h(y_cur, nodes, elem_scale, potential, stiff)
    y_next = (2.0 / half_width) * (applied - centre * y_cur) - y_prev
    applied_next = apply_h(y_next, nodes, elem_scale, potential, stiff)
    weight = 1.0 / NODES
    margin = weight * jnp.dot(y_next.T, y_next, precision=lax.Precision.HIGHEST, preferred_element_type=jnp.float32)
    projected = weight * jnp.dot(applied_next.T, y_next, precision=lax.Precision.HIGHEST, preferred_element_type=jnp.float32)
    return y_next, margin, projected
```

```python
import functools

import jax
import jax.numpy as jnp
import numpy as np
from jax import lax
from jax.experimental import pallas as pl
from jax.experimental.pallas import tpu as pltpu
from jax.sharding import PartitionSpec as P

SIDE = 32
CHUNK = 128
BLOCK = 128
WINDOW = 256
MARGIN = (WINDOW - BLOCK) // 2

cheb_low = 1.0
cheb_high = 9.0
centre = 0.5 * (cheb_high + cheb_low)
half_width = 0.5 * (cheb_high - cheb_low)

OFFSETS = [(dj, dk) for dj in (-1, 0, 1) for dk in (-1, 0, 1)]
PARAMS = pltpu.CompilerParams(vmem_limit_bytes=48 * 1024 * 1024)


def cost(flops, bytes_accessed):
    return pl.CostEstimate(flops=flops, bytes_accessed=bytes_accessed, transcendentals=0)


def element_table():
    stiff_line = np.array([[1.0, -1.0], [-1.0, 1.0]])
    mass_line = np.array([[1.0 / 3.0, 1.0 / 6.0], [1.0 / 6.0, 1.0 / 3.0]])
    total = np.kron(stiff_line, np.kron(mass_line, mass_line))
    total = total + np.kron(mass_line, np.kron(stiff_line, mass_line))
    total = total + np.kron(mass_line, np.kron(mass_line, stiff_line))
    return total.astype(np.float32)


def halves(x):
    high = x.astype(jnp.bfloat16)
    low = (x - high.astype(jnp.float32)).astype(jnp.bfloat16)
    return high, low


def dot(a, b):
    return lax.dot_general(a, b, (((1,), (0,)), ((), ())), preferred_element_type=jnp.float32)


def to_grid_kernel(map_ref, x_ref, *refs):
    outs, (high_ref, low_ref) = refs[:-2], refs[-2:]

    @pl.when(pl.program_id(0) == 0)
    def _():
        high_ref[...], low_ref[...] = halves(x_ref[...])

    rows, nodes = map_ref.shape[0], x_ref.shape[0]
    place = lax.broadcasted_iota(jnp.int32, (rows, nodes), 1)
    pick = jnp.where(place == map_ref[...], 1.0, 0.0).astype(jnp.bfloat16)
    moved = dot(pick, high_ref[...]) + dot(pick, low_ref[...])
    for at, out_ref in enumerate(outs):
        out_ref[...] = moved[:, at * CHUNK : (at + 1) * CHUNK]


def to_grid(face_map, x):
    nodes, states = x.shape
    rows = 256
    count = states // CHUNK
    return pl.pallas_call(
        to_grid_kernel,
        grid=(nodes // rows,),
        in_specs=[
            pl.BlockSpec((rows, 1), lambda i: (i, 0)),
            pl.BlockSpec((nodes, states), lambda i: (0, 0)),
        ],
        out_specs=[pl.BlockSpec((rows, CHUNK), lambda i: (i, 0))] * count,
        out_shape=[jax.ShapeDtypeStruct((nodes, CHUNK), jnp.float32)] * count,
        scratch_shapes=[pltpu.VMEM((nodes, states), jnp.bfloat16)] * 2,
        compiler_params=PARAMS,
        cost_estimate=cost(4 * nodes * nodes * states, 8 * nodes * states),
        name="to_grid",
    )(face_map.reshape(nodes, 1), x)


def from_grid_kernel(map_ref, *refs):
    ins, out_ref, high_ref, low_ref = refs[:-3], refs[-3], refs[-2], refs[-1]
    step = pl.program_id(0)

    @pl.when(step == 0)
    def _():
        for at, x_ref in enumerate(ins):
            columns = slice(at * CHUNK, (at + 1) * CHUNK)
            high_ref[:, columns], low_ref[:, columns] = halves(x_ref[...])

    rows, nodes = out_ref.shape[0], high_ref.shape[0]
    node = lax.broadcasted_iota(jnp.int32, (rows, nodes), 0) + step * rows
    pick = jnp.where(node == map_ref[...], 1.0, 0.0).astype(jnp.bfloat16)
    out_ref[...] = dot(pick, high_ref[...]) + dot(pick, low_ref[...])


def from_grid(face_map, chunks):
    nodes = chunks[0].shape[0]
    states = CHUNK * len(chunks)
    rows = 256
    return pl.pallas_call(
        from_grid_kernel,
        grid=(nodes // rows,),
        in_specs=[pl.BlockSpec((1, nodes), lambda i: (0, 0))]
        + [pl.BlockSpec((nodes, CHUNK), lambda i: (0, 0))] * len(chunks),
        out_specs=pl.BlockSpec((rows, states), lambda i: (i, 0)),
        out_shape=jax.ShapeDtypeStruct((nodes, states), jnp.float32),
        scratch_shapes=[pltpu.VMEM((nodes, states), jnp.bfloat16)] * 2,
        compiler_params=PARAMS,
        cost_estimate=cost(4 * nodes * nodes * states, 8 * nodes * states),
        name="from_grid",
    )(face_map.reshape(1, nodes), *chunks)


def plane_terms(scale, stiff, layer):
    terms = []
    for dj, dk in OFFSETS:
        total = 0.0
        for b in (0, 1):
            for c in (0, 1):
                if b + dj in (0, 1) and c + dk in (0, 1):
                    weight = float(stiff[2 * b + c, 4 * layer + 2 * (b + dj) + c + dk])
                    total = total + weight * jnp.roll(scale, (b, c), axis=(0, 1))
        terms.append(total)
    return terms


def coefficients(own, before, potential, stiff):
    own, before, potential = (x.reshape(SIDE, SIDE) for x in (own, before, potential))
    here = [0.5 * (a + b) for a, b in zip(plane_terms(own, stiff, 0), plane_terms(before, stiff, 0))]
    here[4] = here[4] + potential
    after = [0.5 * a for a in plane_terms(own, stiff, 1)]
    back = [0.5 * a for a in plane_terms(before, stiff, 1)]
    rows = jnp.stack([x.reshape(-1) for x in here + after + back])
    return jnp.pad(rows, ((0, 32 - rows.shape[0]), (0, 0)))


def bands_kernel(terms_ref, high_ref, low_ref):
    terms = terms_ref[...].T
    row = lax.broadcasted_iota(jnp.int32, (BLOCK, WINDOW), 0)
    column = lax.broadcasted_iota(jnp.int32, (BLOCK, WINDOW), 1)
    dj = (column >> 5) - MARGIN // SIDE - (row >> 5)
    dk = (column - row) & (SIDE - 1)
    dk = jnp.where(dk == SIDE - 1, -1, dk)
    near = (dj >= -1) & (dj <= 1) & (dk <= 1)
    which = jnp.where(near, (dj + 1) * 3 + dk + 1, -1)
    for plane in range(3):
        total = jnp.zeros((BLOCK, WINDOW), jnp.float32)
        for at in range(9):
            term = terms[:, plane * 9 + at : plane * 9 + at + 1]
            total = jnp.where(which == at, term, total)
        high_ref[plane, 0], low_ref[plane, 0] = halves(total)


def bands(terms):
    nodes = terms.shape[1]
    count = nodes // BLOCK
    shape = jax.ShapeDtypeStruct((3, count, BLOCK, WINDOW), jnp.bfloat16)
    spec = pl.BlockSpec((3, 1, BLOCK, WINDOW), lambda i: (0, i, 0, 0))
    return pl.pallas_call(
        bands_kernel,
        grid=(count,),
        in_specs=[pl.BlockSpec((32, BLOCK), lambda i: (0, i))],
        out_specs=[spec, spec],
        out_shape=[shape, shape],
        compiler_params=PARAMS,
        cost_estimate=cost(60 * nodes * WINDOW, 12 * nodes * WINDOW),
        name="bands",
    )(terms)


def apply_kernel(filtered, high_ref, low_ref, own_ref, after_ref, before_ref, *refs):
    wide_high, wide_low = refs[-2:]
    step = pl.program_id(0)
    nodes = own_ref.shape[0]

    @pl.when(step == 0)
    def _():
        for plane, ref in enumerate((own_ref, after_ref, before_ref)):
            high, low = halves(ref[...])
            for wide, part in ((wide_high, high), (wide_low, low)):
                wide[plane, pl.ds(MARGIN, nodes), :] = part
                wide[plane, pl.ds(0, MARGIN), :] = part[nodes - MARGIN :]
                wide[plane, pl.ds(MARGIN + nodes, MARGIN), :] = part[:MARGIN]

    per_step = high_ref.shape[1]
    for at in range(per_step):
        block = step * per_step + at
        first = pl.multiple_of(block * BLOCK, BLOCK)
        total = None
        for plane in range(3):
            high = wide_high[plane, pl.ds(first, WINDOW), :]
            low = wide_low[plane, pl.ds(first, WINDOW), :]
            term = dot(high_ref[plane, at], high) + dot(high_ref[plane, at], low)
            term = term + dot(low_ref[plane, at], high)
            total = term if total is None else total + term
        rows = pl.ds(at * BLOCK, BLOCK)
        if filtered:
            last_ref, out_ref, turned_high, turned_low = refs[:4]
            mine = own_ref[pl.ds(first, BLOCK), :]
            total = (2.0 / half_width) * (total - centre * mine) - last_ref[rows, :]
            out_ref[rows, :] = total
        else:
            turned_high, turned_low = refs[:2]
        turned_high[:, rows], turned_low[:, rows] = halves(total.T)


def apply_h(band_high, band_low, own, after, before, last=None):
    nodes, width = own.shape
    per_step = 2
    rows = per_step * BLOCK
    filtered = last is not None
    whole = pl.BlockSpec((nodes, width), lambda i: (0, 0))
    part = pl.BlockSpec((rows, width), lambda i: (i, 0))
    turned = pl.BlockSpec((width, rows), lambda i: (0, i))
    band = pl.BlockSpec((3, per_step, BLOCK, WINDOW), lambda i: (0, i, 0, 0))
    turned_shape = jax.ShapeDtypeStruct((width, nodes), jnp.bfloat16)
    plain_shape = jax.ShapeDtypeStruct((nodes, width), jnp.float32)
    return pl.pallas_call(
        functools.partial(apply_kernel, filtered),
        grid=(nodes // rows,),
        in_specs=[band, band, whole, whole, whole] + [part] * filtered,
        out_specs=[part] * filtered + [turned, turned],
        out_shape=[plain_shape] * filtered + [turned_shape, turned_shape],
        scratch_shapes=[pltpu.VMEM((3, nodes + 2 * MARGIN, width), jnp.bfloat16)] * 2,
        compiler_params=PARAMS,
        cost_estimate=cost(18 * nodes * WINDOW * width, 20 * nodes * width),
        name="apply_h",
    )(band_high, band_low, own, after, before, *([last] if filtered else []))


def product_kernel(summed, left_high, left_low, more_high, more_low, *refs):
    count = len(refs) - 3
    pieces, out_ref, high_ref, low_ref = refs[:count], refs[-3], refs[-2], refs[-1]
    step = pl.program_id(0)

    @pl.when(step == 0)
    def _():
        done = 0
        for at in range(0, count, summed):
            piece = pieces[at][...]
            for other in range(1, summed):
                piece = piece + pieces[at + other][...]
            columns = slice(done, done + piece.shape[1])
            done += piece.shape[1]
            high_ref[:, columns], low_ref[:, columns] = halves(piece)

    def rows_of(left, left_rest):
        total = dot(left[...], high_ref[...]) + dot(left[...], low_ref[...])
        out_ref[...] = total + dot(left_rest[...], high_ref[...])

    @pl.when(step < pl.num_programs(0) // 2)
    def _():
        rows_of(left_high, left_low)

    @pl.when(step >= pl.num_programs(0) // 2)
    def _():
        rows_of(more_high, more_low)


def products(y_turned, h_turned, pieces, summed=1):
    states, nodes = y_turned[0].shape
    rows = 256 if states % 256 == 0 else states
    steps = states // rows
    width = sum(piece.shape[1] for piece in pieces) // summed
    first = pl.BlockSpec((rows, nodes), lambda i: (jnp.minimum(i, steps - 1), 0))
    second = pl.BlockSpec((rows, nodes), lambda i: (jnp.maximum(i - steps, 0), 0))
    return pl.pallas_call(
        functools.partial(product_kernel, summed),
        grid=(2 * steps,),
        in_specs=[first, first, second, second]
        + [pl.BlockSpec(piece.shape, lambda i: (0, 0)) for piece in pieces],
        out_specs=pl.BlockSpec((rows, width), lambda i: (i, 0)),
        out_shape=jax.ShapeDtypeStruct((2 * states, width), jnp.float32),
        scratch_shapes=[pltpu.VMEM((nodes, width), jnp.bfloat16)] * 2,
        compiler_params=PARAMS,
        cost_estimate=cost(12 * states * nodes * width, 8 * nodes * states + 4 * nodes * width),
        name="products",
    )(*y_turned, *h_turned, *pieces)


def ring(axis, distance):
    size = lax.axis_size(axis)
    return [((i - distance) % size, i) for i in range(size)]


def around(block):
    after = lax.ppermute(block, "dom", ring("dom", -1))
    before = lax.ppermute(block, "dom", ring("dom", 1))
    return after, before


def line(block, step):
    last = lax.axis_size("band") - 1
    up = lax.ppermute(block[0], "band", [(i, i + 1) for i in range(step - 1, last)])
    down = lax.ppermute(block[1], "band", [(i + 1, i) for i in range(0, last - step + 1)])
    return up, down


def summed_over_dom(piece, bands_of):
    size = lax.axis_size("band")
    cores, chips = [], []
    for at, target in enumerate(bands_of):
        if target is None:
            continue
        for chip in (0, 2):
            to = chip + target % 2
            cores.append(((to ^ 1) * size + at, to * size + at))
        chips.append(((target ^ 2) * size + at, target * size + at))
    both = piece + lax.ppermute(piece, ("dom", "band"), cores)
    return both, lax.ppermute(both, ("dom", "band"), chips)


def on_device(y_cur, y_prev, connect, face_map, elem_scale, potential):
    stiff = element_table()
    nodes, states = y_cur.shape
    count = states // CHUNK
    domains, widths = lax.axis_size("dom"), lax.axis_size("band")
    place = jnp.arange(nodes, dtype=jnp.int32)
    cell_place = connect[:, 4] - nodes
    own = jnp.sum(jnp.where(cell_place[:, None] == place[None, :], elem_scale[:, None], 0.0), axis=0)
    before = lax.ppermute(own, "dom", ring("dom", 1))
    at_grid = jnp.sum(jnp.where(place[:, None] == face_map[None, :], potential[:, None], 0.0), axis=0)

    current = to_grid(face_map, y_cur)
    current_around = [around(chunk) for chunk in current]
    band = bands(coefficients(own, before, at_grid, stiff))
    last = to_grid(face_map, y_prev)

    following, turned, next_around, first_step = [], [], [], []
    for at in range(count):
        chunk, high, low = apply_h(*band, current[at], *current_around[at], last[at])
        following.append(chunk)
        turned.append((high, low))
        next_around.append(around(chunk))
        if domains == 4 and widths == 4:
            first_step.append(line((chunk, chunk), 1))
    y_turned = [jnp.concatenate([pair[i] for pair in turned]) for i in (0, 1)]
    y_next = from_grid(face_map, following)
    turned = [apply_h(*band, following[at], *next_around[at]) for at in range(count)]
    h_turned = [jnp.concatenate([pair[i] for pair in turned]) for i in (0, 1)]
    weight = 1.0 / (nodes * domains)

    if not (domains == 4 and widths == 4):
        piece = lax.all_gather(jnp.concatenate(following, axis=1), "band", axis=1, tiled=True)
        block = products(y_turned, h_turned, [piece])
        parts = [
            weight * lax.psum_scatter(half, "dom", scatter_dimension=1, tiled=True)
            for half in (block[:states], block[states:])
        ]
        return (y_next, *parts)

    second_step = [line(pair, 2) for pair in first_step]
    third_step = [line(pair, 3) for pair in second_step]
    bands_at = range(widths)

    def inside(value):
        return value if 0 <= value < widths else None

    own_block = products(y_turned, h_turned, following)
    up_block = products(y_turned, h_turned, [pair[0] for pair in first_step])
    down_block = products(y_turned, h_turned, [pair[1] for pair in first_step])
    second_block = products(y_turned, h_turned, [x for pair in second_step for x in pair], 2)
    third_blocks = [products(y_turned, h_turned, list(pair), 2) for pair in third_step]
    far = [3 - b if b in (0, 3) else None for b in bands_at]
    groups = [
        ([own_block], [b for b in bands_at]),
        ([up_block], [inside(b - 1) for b in bands_at]),
        ([down_block], [inside(b + 1) for b in bands_at]),
        ([second_block], [b ^ 2 for b in bands_at]),
        (third_blocks, far),
    ]
    me, level = lax.axis_index("dom"), lax.axis_index("band")
    total = 0.0
    for blocks, bands_of in groups:
        mine = jnp.array([-1 if b is None else b for b in bands_of], jnp.int32)[level] == me
        sums = [summed_over_dom(block, bands_of) for block in blocks]
        kept = [jnp.where(mine, both, 0.0) + arrived for both, arrived in sums]
        total = total + (kept[0] if len(kept) == 1 else jnp.concatenate(kept, axis=1))
    total = weight * total
    return (y_next, total[:states], total[states:])


def solution(mesh):
    placed = (
        P(("image", "dom"), "band"),
        P(("image", "dom"), "band"),
        P("dom", None),
        P("dom"),
        P("dom"),
        P(("image", "dom")),
    )
    return jax.shard_map(
        on_device,
        mesh=mesh,
        in_specs=placed,
        out_specs=(
            P(("image", "dom"), "band"),
            P(("image", "band"), "dom"),
            P(("image", "band"), "dom"),
        ),
        check_vma=False,
    )
```

```python
import functools

import jax
import jax.numpy as jnp
import numpy as np
from jax import lax
from jax.experimental import pallas as pl
from jax.experimental.pallas import tpu as pltpu
from jax.sharding import PartitionSpec as P

SIDE = 32
STATES_DEV = 512
BLOCK = 128
WINDOW = 256
MARGIN = (WINDOW - BLOCK) // 2

cheb_low = 1.0
cheb_high = 9.0
centre = 0.5 * (cheb_high + cheb_low)
half_width = 0.5 * (cheb_high - cheb_low)

OFFSETS = [(dj, dk) for dj in (-1, 0, 1) for dk in (-1, 0, 1)]
PARAMS = pltpu.CompilerParams(vmem_limit_bytes=32 * 1024 * 1024)


COST = pl.CostEstimate(flops=1, bytes_accessed=1, transcendentals=0)


def element_table():
    stiff_line = np.array([[1.0, -1.0], [-1.0, 1.0]])
    mass_line = np.array([[1.0 / 3.0, 1.0 / 6.0], [1.0 / 6.0, 1.0 / 3.0]])
    total = np.kron(stiff_line, np.kron(mass_line, mass_line))
    total = total + np.kron(mass_line, np.kron(stiff_line, mass_line))
    total = total + np.kron(mass_line, np.kron(mass_line, stiff_line))
    return total.astype(np.float32)


def halves(x):
    high = x.astype(jnp.bfloat16)
    low = (x - high.astype(jnp.float32)).astype(jnp.bfloat16)
    return high, low


def dot(a, b):
    return lax.dot_general(a, b, (((1,), (0,)), ((), ())), preferred_element_type=jnp.float32)


def call(kernel, after, *, in_specs, name, into=(), **options):
    count = len(in_specs)
    extra = [*[array for _, array in into], *after]

    def body(*refs):
        kernel(*refs[:count], *refs[count + len(extra) :])

    made = pl.pallas_call(
        body,
        in_specs=[*in_specs, *[pl.BlockSpec(memory_space=pl.ANY)] * len(extra)],
        input_output_aliases={count + at: out for at, (out, _) in enumerate(into)},
        compiler_params=PARAMS,
        cost_estimate=COST,
        name=name,
        **options,
    )
    return lambda *args: made(*args, *extra)


def join_kernel(left_ref, right_ref, out_ref, *passed):
    width = left_ref.shape[1]
    out_ref[:, :width] = left_ref[...]
    out_ref[:, width:] = right_ref[...]


def join(left, right, after, passed=()):
    nodes, width = left.shape
    rows = 256
    part = pl.BlockSpec((rows, width), lambda i: (i, 0))
    return call(
        join_kernel,
        after,
        into=[(1 + at, x) for at, x in enumerate(passed)],
        grid=(nodes // rows,),
        in_specs=[part, part],
        out_specs=[pl.BlockSpec((rows, 2 * width), lambda i: (i, 0))]
        + [pl.BlockSpec(memory_space=pl.ANY)] * len(passed),
        out_shape=[jax.ShapeDtypeStruct((nodes, 2 * width), left.dtype)]
        + [jax.ShapeDtypeStruct(x.shape, x.dtype) for x in passed],
        name="join",
    )(left, right)


def to_grid_kernel(offsets, map_ref, x_ref, *refs):
    whole_ref, outs, (high_ref, low_ref) = refs[0], refs[1:-2], refs[-2:]
    step = pl.program_id(0)

    @pl.when(step == 0)
    def _():
        high_ref[...], low_ref[...] = halves(x_ref[...])

    rows, nodes = whole_ref.shape[0], x_ref.shape[0]
    place = lax.broadcasted_iota(jnp.int32, (BLOCK, nodes), 1)
    for at in range(rows // BLOCK):
        row = map_ref[pl.ds(step * (rows // BLOCK) + at, 1), :]
        column = jnp.broadcast_to(row, (BLOCK, BLOCK)).T
        column = jnp.concatenate([column] * (nodes // BLOCK), axis=1)
        pick = jnp.where(place == column, 1.0, 0.0).astype(jnp.bfloat16)
        moved = dot(pick, high_ref[...]) + dot(pick, low_ref[...])
        out = slice(at * BLOCK, (at + 1) * BLOCK)
        whole_ref[out, :] = moved
        for first, out_ref in zip(offsets, outs):
            out_ref[out, :] = moved[:, first : first + out_ref.shape[1]]


def to_grid(face_map, x, first, width, widths=(), after=()):
    nodes = x.shape[0]
    rows = 512
    offsets = tuple(sum(widths[:at]) for at in range(len(widths)))
    sizes = (width, *widths)
    at = first // width
    return call(
        functools.partial(to_grid_kernel, offsets),
        after,
        grid=(nodes // rows,),
        in_specs=[
            pl.BlockSpec((nodes // BLOCK, BLOCK), lambda i: (0, 0)),
            pl.BlockSpec((nodes, width), lambda i: (0, at)),
        ],
        out_specs=[pl.BlockSpec((rows, size), lambda i: (i, 0)) for size in sizes],
        out_shape=[jax.ShapeDtypeStruct((nodes, size), jnp.float32) for size in sizes],
        scratch_shapes=[pltpu.VMEM((nodes, width), jnp.bfloat16)] * 2,
        name="to_grid",
    )(face_map.reshape(nodes // BLOCK, BLOCK), x)


def from_grid_kernel(map_ref, *refs):
    pieces, (out_ref, high_ref, low_ref) = refs[:-3], refs[-3:]
    step = pl.program_id(0)

    @pl.when(step == 0)
    def _():
        split_columns([[x] for x in pieces], high_ref, low_ref, 0)

    rows, nodes = out_ref.shape[0], high_ref.shape[0]
    node = lax.broadcasted_iota(jnp.int32, (rows, nodes), 0) + step * rows
    pick = jnp.where(node == map_ref[...], 1.0, 0.0).astype(jnp.bfloat16)
    out_ref[...] = dot(pick, high_ref[...]) + dot(pick, low_ref[...])


def from_grid(face_map, pieces, at, states, so_far=None, after=()):
    nodes = pieces[0].shape[0]
    width = sum(x.shape[1] for x in pieces)
    rows = 256
    return call(
        from_grid_kernel,
        after,
        into=[(0, so_far)] if at else [],
        grid=(nodes // rows,),
        in_specs=[pl.BlockSpec((1, nodes), lambda i: (0, 0))]
        + [pl.BlockSpec(x.shape, lambda i: (0, 0)) for x in pieces],
        out_specs=pl.BlockSpec((rows, width), lambda i: (i, at)),
        out_shape=jax.ShapeDtypeStruct((nodes, states), jnp.float32),
        scratch_shapes=[pltpu.VMEM((nodes, width), jnp.bfloat16)] * 2,
        name="from_grid",
    )(face_map.reshape(1, nodes), *pieces)


def plane_terms(shifted, stiff, layer):
    terms = []
    for dj, dk in OFFSETS:
        total = None
        for b in (0, 1):
            for c in (0, 1):
                if b + dj in (0, 1) and c + dk in (0, 1):
                    weight = float(stiff[2 * b + c, 4 * layer + 2 * (b + dj) + c + dk])
                    term = weight * shifted[b][c]
                    total = term if total is None else total + term
        terms.append(total)
    return terms


def write_terms(stiff, odd, own_ref, before_ref, potential_ref, terms_ref):
    nodes = own_ref.shape[1]
    column = lax.broadcasted_iota(jnp.int32, (8, nodes), 1) & (SIDE - 1)
    here, layers = None, []
    for ref in (own_ref, before_ref):
        scale = jnp.broadcast_to(0.5 * ref[...], (8, nodes))
        back = jnp.where(column == 0, pltpu.roll(scale, nodes - SIDE + 1, 1), pltpu.roll(scale, 1, 1))
        shifted = [[x, pltpu.roll(x, SIDE, 1)] for x in (scale, back)]
        shifted = [[shifted[c][b] for c in (0, 1)] for b in (0, 1)]
        mine = plane_terms(shifted, stiff, 0)
        here = mine if here is None else [a + b for a, b in zip(here, mine)]
        layers.append(plane_terms(shifted, stiff, 1))
    here[4] = here[4] + potential_ref[...]
    after, back = layers
    paired = [jnp.where(odd, b, a) for a, b in zip(after, back)]
    far = [jnp.where(odd, a, b) for a, b in zip(after, back)]
    for at, term in enumerate(here + paired + far):
        terms_ref[at : at + 1, :] = term[:1]


def write_bands(terms, out_ref):
    row = lax.broadcasted_iota(jnp.int32, (SIDE, BLOCK), 0)
    lane = lax.broadcasted_iota(jnp.int32, (SIDE, BLOCK), 1)
    turn = (lane - row) & (SIDE - 1)
    for line in range(BLOCK // SIDE):
        rows = slice(line * SIDE, (line + 1) * SIDE)
        rest = slice(BLOCK + rows.start, BLOCK + rows.stop)
        masks = {}
        for dj, dk in OFFSETS:
            tile, group = divmod(line + MARGIN // SIDE + dj, BLOCK // SIDE)
            masks[dj, dk] = tile, (turn == dk % SIDE) & ((lane >> 5) == group)
        for plane in range(3):
            totals = [jnp.zeros((SIDE, BLOCK), jnp.float32) for _ in range(WINDOW // BLOCK)]
            for at, offset in enumerate(OFFSETS):
                term = terms[rows, plane * 9 + at : plane * 9 + at + 1]
                tile, mask = masks[offset]
                totals[tile] = jnp.where(mask, term, totals[tile])
            for tile, total in enumerate(totals):
                columns = slice(tile * BLOCK, (tile + 1) * BLOCK)
                out_ref[plane, 0, rows, columns], out_ref[plane, 0, rest, columns] = halves(total)


def prepare_kernel(stiff, odd_ref, own_ref, before_ref, potential_ref, map_ref, prev_ref, *refs):
    band_ref, last_ref, terms_ref, high_ref, low_ref = refs
    step = pl.program_id(0)
    nodes = prev_ref.shape[0]

    @pl.when(step == 0)
    def _():
        write_terms(stiff, odd_ref[0] == 1, own_ref, before_ref, potential_ref, terms_ref)
        split_columns([[prev_ref]], high_ref, low_ref, 0)

    write_bands(terms_ref[:, pl.ds(pl.multiple_of(step * BLOCK, BLOCK), BLOCK)].T, band_ref)
    place = lax.broadcasted_iota(jnp.int32, (BLOCK, nodes), 1)
    column = jnp.broadcast_to(map_ref[pl.ds(step, 1), :], (BLOCK, BLOCK)).T
    column = jnp.concatenate([column] * (nodes // BLOCK), axis=1)
    pick = jnp.where(place == column, 1.0, 0.0).astype(jnp.bfloat16)
    last_ref[...] = dot(pick, high_ref[...]) + dot(pick, low_ref[...])


def prepare(stiff, odd, own, before, potential, face_map, y_prev, after):
    nodes, states = y_prev.shape
    row = pl.BlockSpec((1, nodes), lambda i: (0, 0))
    return call(
        functools.partial(prepare_kernel, stiff),
        after,
        grid=(nodes // BLOCK,),
        in_specs=[pl.BlockSpec(memory_space=pltpu.SMEM), row, row, row]
        + [pl.BlockSpec((nodes // BLOCK, BLOCK), lambda i: (0, 0))]
        + [pl.BlockSpec((nodes, states), lambda i: (0, 0))],
        out_specs=[
            pl.BlockSpec((3, 1, 2 * BLOCK, WINDOW), lambda i: (0, i, 0, 0)),
            pl.BlockSpec((BLOCK, states), lambda i: (i, 0)),
        ],
        out_shape=[
            jax.ShapeDtypeStruct((3, nodes // BLOCK, 2 * BLOCK, WINDOW), jnp.bfloat16),
            jax.ShapeDtypeStruct((nodes, states), jnp.float32),
        ],
        scratch_shapes=[pltpu.VMEM((32, nodes), jnp.float32)]
        + [pltpu.VMEM((nodes, states), jnp.bfloat16)] * 2,
        name="prepare",
    )(
        odd,
        *[x.reshape(1, nodes) for x in (own, before, potential)],
        face_map.reshape(nodes // BLOCK, BLOCK),
        y_prev,
    )


def apply_kernel(filtered, band_ref, own_ref, paired_ref, far_ref, *refs):
    wide = refs[-1]
    step = pl.program_id(0)
    nodes, width = own_ref.shape

    @pl.when(step == 0)
    def _():
        for plane, ref in enumerate((own_ref, paired_ref, far_ref)):
            for columns, part in zip((slice(0, width), slice(width, 2 * width)), halves(ref[...])):
                wide[plane, pl.ds(MARGIN, nodes), columns] = part
                wide[plane, pl.ds(0, MARGIN), columns] = part[nodes - MARGIN :]
                wide[plane, pl.ds(MARGIN + nodes, MARGIN), columns] = part[:MARGIN]

    per_step = band_ref.shape[1]
    for at in range(per_step):
        block = step * per_step + at
        first = pl.multiple_of(block * BLOCK, BLOCK)
        total = None
        for plane in range(3):
            term = dot(band_ref[plane, at], wide[plane, pl.ds(first, WINDOW), :])
            total = term if total is None else total + term
        total = total[:BLOCK] + total[BLOCK:]
        total = total[:, :width] + total[:, width:]
        rows = pl.ds(at * BLOCK, BLOCK)
        if filtered:
            last_ref, out_ref, joined_ref, turned_high, turned_low = refs[:5]
            mine = own_ref[pl.ds(first, BLOCK), :]
            total = (2.0 / half_width) * (total - centre * mine) - last_ref[rows, :]
            out_ref[rows, :] = total
            joined_ref[rows, :] = total
        else:
            turned_high, turned_low = refs[:2]
        turned_high[:, rows], turned_low[:, rows] = halves(total.T)


def apply_specs(nodes, width):
    per_step = 2
    rows = per_step * BLOCK
    return dict(
        grid=(nodes // rows,),
        scratch_shapes=[pltpu.VMEM((3, nodes + 2 * MARGIN, 2 * width), jnp.bfloat16)],
        name="apply_h",
    ), pl.BlockSpec((3, per_step, 2 * BLOCK, WINDOW), lambda i: (0, i, 0, 0)), rows


def next_degree(band, own, paired, far, last, half, at, so_far, after):
    nodes, width = far.shape
    states = own.shape[1]
    options, band_spec, rows = apply_specs(nodes, width)
    inside = at % (half // width)
    column = pl.BlockSpec((nodes, width), lambda i: (0, at))
    part = pl.BlockSpec((rows, width), lambda i: (i, at))
    turned = pl.BlockSpec((width, rows), lambda i: (at, i))
    turned_shape = jax.ShapeDtypeStruct((states, nodes), jnp.bfloat16)
    into = [(out, so_far[out - 1]) for out in (1, 2, 3) if (inside if out == 1 else at)]
    return call(
        functools.partial(apply_kernel, True),
        after,
        into=into,
        in_specs=[band_spec, column, column, pl.BlockSpec((nodes, width), lambda i: (0, 0)), part],
        out_specs=[
            pl.BlockSpec((rows, width), lambda i: (i, 0)),
            pl.BlockSpec((rows, width), lambda i: (i, inside)),
            turned,
            turned,
        ],
        out_shape=[
            jax.ShapeDtypeStruct((nodes, width), jnp.float32),
            jax.ShapeDtypeStruct((nodes, half), jnp.float32),
            turned_shape,
            turned_shape,
        ],
        **options,
    )(band, own, paired, far, last)


def applied_next(band, own, paired, far, states, at, so_far, after=()):
    nodes, width = far.shape
    options, band_spec, rows = apply_specs(nodes, width)
    whole = pl.BlockSpec((nodes, width), lambda i: (0, 0))
    turned = pl.BlockSpec((width, rows), lambda i: (at, i))
    turned_shape = jax.ShapeDtypeStruct((states, nodes), jnp.bfloat16)
    return call(
        functools.partial(apply_kernel, False),
        after,
        into=[(out, so_far[out]) for out in (0, 1) if at],
        in_specs=[band_spec, whole, whole, whole],
        out_specs=[turned, turned],
        out_shape=[turned_shape, turned_shape],
        **options,
    )(band, own, paired, far)


def split_columns(pieces, high_ref, low_ref, first):
    for group in pieces:
        piece = group[0][...]
        for other in group[1:]:
            piece = piece + other[...]
        columns = slice(first, first + piece.shape[1])
        first += piece.shape[1]
        high_ref[:, columns], low_ref[:, columns] = halves(piece)


def rows_product(left_high, left_low, high_ref, low_ref):
    total = dot(left_high[...], high_ref[...]) + dot(left_high[...], low_ref[...])
    return total + dot(left_low[...], high_ref[...])


def sorted_kernel(count, keep_ref, left_high, left_low, *refs):
    own, first = [[x] for x in refs[:count]], [[x] for x in refs[count:-4]]
    kept_ref, sent_ref, high_ref, low_ref = refs[-4:]
    width = kept_ref.shape[1]

    @pl.when((pl.program_id(0) == 0) & (keep_ref[0] == 1))
    def _():
        split_columns(own, high_ref, low_ref, 0)
        split_columns(first, high_ref, low_ref, width)

    @pl.when((pl.program_id(0) == 0) & (keep_ref[0] != 1))
    def _():
        split_columns(own, high_ref, low_ref, width)
        split_columns(first, high_ref, low_ref, 0)

    total = rows_product(left_high, left_low, high_ref, low_ref)
    kept_ref[...] = total[:, :width]
    sent_ref[...] = total[:, width:]


def sorted_products(keep, turned, own, first, after=()):
    states, nodes = turned[0].shape
    rows = 256
    width = sum(piece.shape[1] for piece in own)
    left = pl.BlockSpec((rows, nodes), lambda i: (i, 0))
    out = pl.BlockSpec((rows, width), lambda i: (i, 0))
    shape = jax.ShapeDtypeStruct((states, width), jnp.float32)
    return call(
        functools.partial(sorted_kernel, len(own)),
        after,
        grid=(states // rows,),
        in_specs=[pl.BlockSpec(memory_space=pltpu.SMEM), left, left]
        + [pl.BlockSpec(piece.shape, lambda i: (0, 0)) for piece in (*own, *first)],
        out_specs=[out, out],
        out_shape=[shape, shape],
        scratch_shapes=[pltpu.VMEM((nodes, 2 * width), jnp.bfloat16)] * 2,
        name="sorted_products",
    )(keep, *turned, *own, *first)


def both_kernel(summed, left_high, left_low, more_high, more_low, *refs):
    pieces, (out_ref, high_ref, low_ref) = refs[:-3], refs[-3:]
    step, half = pl.program_id(0), pl.num_programs(0) // 2

    @pl.when(step == 0)
    def _():
        groups = [pieces[at : at + summed] for at in range(0, len(pieces), summed)]
        split_columns(groups, high_ref, low_ref, 0)

    @pl.when(step < half)
    def _():
        out_ref[...] = rows_product(left_high, left_low, high_ref, low_ref)

    @pl.when(step >= half)
    def _():
        out_ref[...] = rows_product(more_high, more_low, high_ref, low_ref)


def both_products(y_turned, h_turned, pieces, summed=1, after=()):
    states, nodes = y_turned[0].shape
    rows = 256
    steps = states // rows
    width = sum(piece.shape[1] for piece in pieces) // summed
    first = pl.BlockSpec((rows, nodes), lambda i: (jnp.minimum(i, steps - 1), 0))
    second = pl.BlockSpec((rows, nodes), lambda i: (jnp.maximum(i - steps, 0), 0))
    return call(
        functools.partial(both_kernel, summed),
        after,
        grid=(2 * steps,),
        in_specs=[first, first, second, second]
        + [pl.BlockSpec(piece.shape, lambda i: (0, 0)) for piece in pieces],
        out_specs=pl.BlockSpec((rows, width), lambda i: (i, 0)),
        out_shape=jax.ShapeDtypeStruct((2 * states, width), jnp.float32),
        scratch_shapes=[pltpu.VMEM((nodes, width), jnp.bfloat16)] * 2,
        name="both_products",
    )(*y_turned, *h_turned, *pieces)


def finish_kernel(weight, count, states, flag_ref, base_ref, *refs):
    sums, arrived = refs[:count], refs[count : 2 * count]
    margin_ref, projected_ref = refs[2 * count :]
    mine = jnp.where(flag_ref[0] == 1, 1.0, 0.0)
    for half, out_ref in enumerate((margin_ref, projected_ref)):
        rows = slice(half * states, (half + 1) * states)
        first = 0
        for block, other in zip(sums, arrived):
            columns = slice(first, first + block.shape[1])
            first += block.shape[1]
            total = base_ref[rows, columns] + mine * block[rows, :] + other[rows, :]
            out_ref[:, columns] = weight * total


def finish(weight, flag, base, sums, arrived):
    states = base.shape[0] // 2
    shape = jax.ShapeDtypeStruct((states, base.shape[1]), jnp.float32)
    return call(
        functools.partial(finish_kernel, weight, len(sums), states),
        (),
        in_specs=[pl.BlockSpec(memory_space=pltpu.SMEM)]
        + [pl.BlockSpec(memory_space=pltpu.VMEM)] * (1 + 2 * len(sums)),
        out_specs=[pl.BlockSpec(memory_space=pltpu.VMEM)] * 2,
        out_shape=[shape, shape],
        name="finish",
    )(flag, base, *sums, *arrived)


def exchange(block, axis, pairs):
    return lax.ppermute(block, axis, pairs + [(b, a) for a, b in pairs])


def paired(block):
    return exchange(block, "dom", [(i, i + 1) for i in range(0, lax.axis_size("dom"), 2)])


def crossed(block):
    size = lax.axis_size("dom")
    return exchange(block, "dom", [(i, (i + 1) % size) for i in range(1, size, 2)])


def to_owner(block, owners, step):
    size = len(owners)
    route = []
    for band, owner in enumerate(owners):
        for to in (owner, owner ^ 2) if step == 1 else (owner,):
            route.append(((to ^ step) * size + band, to * size + band))
    return lax.ppermute(block, ("dom", "band"), route)


def on_device(y_cur, y_prev, connect, face_map, elem_scale, potential):
    stiff = element_table()
    nodes, states = y_cur.shape
    domains, band_count = lax.axis_size("dom"), lax.axis_size("band")
    me, level = lax.axis_index("dom"), lax.axis_index("band")
    swaps = domains == 4 and band_count == 4 and states == STATES_DEV
    half = states // 2
    quarter = states // 4 if swaps else half
    place = jnp.arange(nodes, dtype=jnp.int32)
    cell_place = connect[:, 4] - nodes
    own = jnp.sum(jnp.where(cell_place[:, None] == place[None, :], elem_scale[:, None], 0.0), axis=0)
    before = lax.ppermute(own, "dom", [(i, (i + 1) % domains) for i in range(domains)])
    at_grid = jnp.sum(jnp.where(place[:, None] == face_map[None, :], potential[:, None], 0.0), axis=0)
    odd = (me % 2).astype(jnp.int32).reshape(1)
    weight = 1.0 / (nodes * domains)

    current, *chunks = to_grid(face_map, y_cur, 0, states, (quarter,) * (states // quarter), after=(own,))
    current_paired = paired(current)
    far = [crossed(chunk) for chunk in chunks]
    band, last = prepare(stiff, odd, own, before, at_grid, face_map, y_prev, (current,))

    following, pair_step, joined, middle_step = [], [], [], []
    so_far, waited = [None] * 3, ()
    for at, piece in enumerate(far):
        sources = (band, current, current_paired, piece, last, half, at)
        chunk, *so_far = next_degree(*sources, so_far, waited)
        following.append(chunk)
        waited = (chunk, *pair_step[at - 1 : at]) if at else (chunk,)
        if (at + 1) * quarter % half == 0:
            joined.append(so_far[0])
        if swaps:
            pair_step.append(exchange(chunk, "band", [(0, 1), (2, 3)]))
            if at == 1:
                middle_step.append(exchange(joined[0], "band", [(1, 2)]))
    y_turned = so_far[1:]

    if not swaps:
        y_next = from_grid(face_map, joined, 0, states)
        h_turned = [None] * 2
        for at, piece in enumerate(joined):
            h_turned = applied_next(band, piece, paired(piece), crossed(piece), states, at, h_turned)
        piece = lax.all_gather(jnp.concatenate(joined, axis=1), "band", axis=1, tiled=True)
        block = both_products(y_turned, h_turned, [piece])
        parts = [
            weight * lax.psum_scatter(rows, "dom", scatter_dimension=1, tiled=True)
            for rows in (block[:states], block[states:])
        ]
        return (y_next, *parts)

    outward = [(2, 3), (1, 0)]
    core, chip, upper = me % 2, me // 2, level // 2
    keep = jnp.where(core == level % 2, 1, 0).astype(jnp.int32).reshape(1)
    near_route = [
        (((b // 2 * 2 + c) ^ 2) * 4 + b, (b // 2 * 2 + c) * 4 + b) for b in range(4) for c in (0, 1)
    ]

    def near(rows, after):
        first, sent = sorted_products(keep, rows, following, pair_step, after)
        kept = first + paired(sent)
        return kept, lax.ppermute(kept, ("dom", "band"), near_route), first

    second_out = [lax.ppermute(middle_step[0], "band", outward)]
    near_paired = paired(joined[0])
    waited = (following[3], middle_step[0], *pair_step[2:], near_paired)
    far_pair, later = join(*pair_step[:2], waited, (joined[1],))
    middle_step.append(exchange(later, "band", [(1, 2)]))
    third_middle = [exchange(far_pair, "band", [(1, 2)])]
    sources = (joined[0], near_paired, crossed(joined[0]))
    h_turned = applied_next(band, *sources, states, 0, None, (far_pair,))
    near_margin = near(y_turned, (h_turned[0],))
    (far_pair,) = join(*pair_step[2:], (near_margin[2], second_out[0], middle_step[1]))
    second_out.append(lax.ppermute(middle_step[1], "band", outward))
    third_middle.append(exchange(far_pair, "band", [(1, 2)]))
    sources = (later, paired(later), crossed(later))
    h_turned = applied_next(band, *sources, states, 1, h_turned, (far_pair,))
    near_projected = near(h_turned, (near_margin[0],))
    waited = (near_projected[2], second_out[1], third_middle[0])
    y_next = from_grid(face_map, [joined[0]], 0, states, None, waited)

    second_owner, third_owner = [2, 2, 1, 1], [3, 3, 0, 0]
    pieces = [x for pair in zip(middle_step, second_out) for x in pair]
    second = both_products(y_turned, h_turned, pieces, 2, (y_next, near_projected[0]))
    y_next = from_grid(face_map, [later], 1, states, y_next, (second, third_middle[1]))
    third_pieces = [third_middle[0], third_middle[1][:, :quarter], third_middle[1][:, quarter:]]
    third_out = [lax.ppermute(x, "band", outward) for x in third_pieces]
    waited = (y_next, near_margin[1])
    second = second + to_owner(second, second_owner, 1)
    second_far = to_owner(second, second_owner, 2)

    is_near, is_second = chip == upper, core == upper
    third, third_far = [], []
    for at, pair in enumerate(zip(third_pieces, third_out)):
        block = both_products(y_turned, h_turned, list(pair), 2, waited)
        waited = (block, second, near_projected[1]) if at == 0 else (block, third[0], second_far)
        block = block + to_owner(block, third_owner, 1)
        third.append(block)
        third_far.append(to_owner(block, third_owner, 2))
    near_rows = jnp.concatenate([sum(near_margin[:2]), sum(near_projected[:2])])
    base = jnp.where(is_near, near_rows, jnp.where(is_second, second + second_far, 0.0))
    flag = jnp.where(is_near | is_second, 0, 1).astype(jnp.int32).reshape(1)
    return (y_next, *finish(weight, flag, base, third, third_far))


def solution(mesh):
    placed = (
        P(("image", "dom"), "band"),
        P(("image", "dom"), "band"),
        P("dom", None),
        P("dom"),
        P("dom"),
        P(("image", "dom")),
    )
    return jax.shard_map(
        on_device,
        mesh=mesh,
        in_specs=placed,
        out_specs=(
            P(("image", "dom"), "band"),
            P(("image", "band"), "dom"),
            P(("image", "band"), "dom"),
        ),
        check_vma=False,
    )
```

```python
import functools

import jax
import jax.numpy as jnp
import numpy as np
from jax import lax
from jax.experimental import pallas as pl
from jax.experimental.pallas import tpu as pltpu
from jax.sharding import PartitionSpec as P

SIDE = 32
STATES_DEV = 512
BLOCK = 128
WINDOW = 256
MARGIN = (WINDOW - BLOCK) // 2

cheb_low = 1.0
cheb_high = 9.0
centre = 0.5 * (cheb_high + cheb_low)
half_width = 0.5 * (cheb_high - cheb_low)

OFFSETS = [(dj, dk) for dj in (-1, 0, 1) for dk in (-1, 0, 1)]
PARAMS = pltpu.CompilerParams(vmem_limit_bytes=32 * 1024 * 1024)


COST = pl.CostEstimate(flops=10**12, bytes_accessed=1, transcendentals=0)


def element_table():
    stiff_line = np.array([[1.0, -1.0], [-1.0, 1.0]])
    mass_line = np.array([[1.0 / 3.0, 1.0 / 6.0], [1.0 / 6.0, 1.0 / 3.0]])
    total = np.kron(stiff_line, np.kron(mass_line, mass_line))
    total = total + np.kron(mass_line, np.kron(stiff_line, mass_line))
    total = total + np.kron(mass_line, np.kron(mass_line, stiff_line))
    return total.astype(np.float32)


def halves(x):
    high = x.astype(jnp.bfloat16)
    low = (x - high.astype(jnp.float32)).astype(jnp.bfloat16)
    return high, low


def dot(a, b):
    return lax.dot_general(a, b, (((1,), (0,)), ((), ())), preferred_element_type=jnp.float32)


def corner(x):
    rows = 32 // x.dtype.itemsize
    return pl.BlockSpec((rows, 128), lambda *_: (0, 0))


def call(kernel, after, *, in_specs, out_specs, out_shape, name, into=(), passed=(), **options):
    count = len(in_specs)
    extra = [*[array for _, array in into], *passed, *after]
    aliases = {count + at: out for at, (out, _) in enumerate(into)}
    outs = len(out_shape) if isinstance(out_shape, (list, tuple)) else 1
    if passed:
        out_specs = [*out_specs, *map(corner, passed)]
        out_shape = [*out_shape, *[jax.ShapeDtypeStruct(x.shape, x.dtype) for x in passed]]
        aliases |= {count + len(into) + at: outs + at for at in range(len(passed))}

    def body(*refs):
        rest = refs[count + len(extra) :]
        kernel(*refs[:count], *rest[:outs], *rest[outs + len(passed) :])
        first = count + len(into)
        for x_ref, out_ref in zip(refs[first : first + len(passed)], rest[outs : outs + len(passed)]):
            out_ref[...] = x_ref[...]

    made = pl.pallas_call(
        body,
        in_specs=[*in_specs, *map(corner, extra)],
        out_specs=out_specs,
        out_shape=out_shape,
        input_output_aliases=aliases,
        compiler_params=PARAMS,
        cost_estimate=COST,
        name=name,
        **options,
    )
    return lambda *args: made(*args, *extra)


def gate(arrays, after):
    return call(lambda: None, after, passed=arrays, grid=(1,), in_specs=[], out_specs=[], out_shape=[], name="gate")()


def plus_kernel(left_ref, right_ref, out_ref):
    out_ref[...] = left_ref[...] + right_ref[...]


def plus(left, right, after, passed=()):
    rows = min(512, left.shape[0])
    part = pl.BlockSpec((rows, left.shape[1]), lambda i: (i, 0))
    return call(
        plus_kernel,
        after,
        grid=(left.shape[0] // rows,),
        in_specs=[part, part],
        out_specs=[part],
        out_shape=[jax.ShapeDtypeStruct(left.shape, left.dtype)],
        passed=passed,
        name="plus",
    )(left, right)


def to_grid_kernel(map_ref, x_ref, out_ref, whole_ref, high_ref, low_ref):
    step = pl.program_id(0)

    @pl.when(step == 0)
    def _():
        high_ref[...], low_ref[...] = halves(x_ref[...])

    rows, nodes = out_ref.shape[0], x_ref.shape[0]
    place = lax.broadcasted_iota(jnp.int32, (BLOCK, nodes), 1)
    for at in range(rows // BLOCK):
        row = map_ref[pl.ds(step * (rows // BLOCK) + at, 1), :]
        column = jnp.broadcast_to(row, (BLOCK, BLOCK)).T
        column = jnp.concatenate([column] * (nodes // BLOCK), axis=1)
        pick = jnp.where(place == column, 1.0, 0.0).astype(jnp.bfloat16)
        moved = dot(pick, high_ref[...]) + dot(pick, low_ref[...])
        out = slice(at * BLOCK, (at + 1) * BLOCK)
        out_ref[out, :] = moved
        whole_ref[out, :] = moved


def to_grid(face_map, x, at, width, so_far, after):
    nodes, states = x.shape
    rows = 512
    return call(
        to_grid_kernel,
        after,
        into=[(1, so_far)] if at else [],
        grid=(nodes // rows,),
        in_specs=[
            pl.BlockSpec((nodes // BLOCK, BLOCK), lambda i: (0, 0)),
            pl.BlockSpec((nodes, width), lambda i: (0, at)),
        ],
        out_specs=[pl.BlockSpec((rows, width), lambda i: (i, 0)), pl.BlockSpec((rows, width), lambda i: (i, at))],
        out_shape=[
            jax.ShapeDtypeStruct((nodes, width), jnp.float32),
            jax.ShapeDtypeStruct((nodes, states), jnp.float32),
        ],
        scratch_shapes=[pltpu.VMEM((nodes, width), jnp.bfloat16)] * 2,
        name="to_grid",
    )(face_map.reshape(nodes // BLOCK, BLOCK), x)


def from_grid_kernel(map_ref, x_ref, out_ref, again_ref, half_ref, high_ref, low_ref):
    step = pl.program_id(0)

    @pl.when(step == 0)
    def _():
        high_ref[...], low_ref[...] = halves(x_ref[...])

    rows, nodes = out_ref.shape[0], high_ref.shape[0]
    node = lax.broadcasted_iota(jnp.int32, (rows, nodes), 0) + step * rows
    pick = jnp.where(node == map_ref[...], 1.0, 0.0).astype(jnp.bfloat16)
    out_ref[...] = dot(pick, high_ref[...]) + dot(pick, low_ref[...])
    again = x_ref[pl.ds(pl.multiple_of(step * rows, rows), rows), :]
    again_ref[...] = again
    half_ref[...] = again[:, half_ref.shape[1] :]


def from_grid(face_map, x, after=(), passed=()):
    nodes, states = x.shape
    rows = 256
    part = pl.BlockSpec((rows, states), lambda i: (i, 0))
    return call(
        from_grid_kernel,
        after,
        passed=passed,
        grid=(nodes // rows,),
        in_specs=[pl.BlockSpec((1, nodes), lambda i: (0, 0)), pl.BlockSpec((nodes, states), lambda i: (0, 0))],
        out_specs=[part, part, pl.BlockSpec((rows, states // 2), lambda i: (i, 0))],
        out_shape=[jax.ShapeDtypeStruct((nodes, size), jnp.float32) for size in (states, states, states // 2)],
        scratch_shapes=[pltpu.VMEM((nodes, states), jnp.bfloat16)] * 2,
        name="from_grid",
    )(face_map.reshape(1, nodes), x)


def plane_terms(shifted, stiff, layer):
    terms = []
    for dj, dk in OFFSETS:
        total = None
        for b in (0, 1):
            for c in (0, 1):
                if b + dj in (0, 1) and c + dk in (0, 1):
                    weight = float(stiff[2 * b + c, 4 * layer + 2 * (b + dj) + c + dk])
                    term = weight * shifted[b][c]
                    total = term if total is None else total + term
        terms.append(total)
    return terms


def write_terms(stiff, odd, own_ref, before_ref, potential_ref, terms_ref):
    nodes = own_ref.shape[1]
    column = lax.broadcasted_iota(jnp.int32, (8, nodes), 1) & (SIDE - 1)
    here, layers = None, []
    for ref in (own_ref, before_ref):
        scale = jnp.broadcast_to(0.5 * ref[...], (8, nodes))
        back = jnp.where(column == 0, pltpu.roll(scale, nodes - SIDE + 1, 1), pltpu.roll(scale, 1, 1))
        shifted = [[x, pltpu.roll(x, SIDE, 1)] for x in (scale, back)]
        shifted = [[shifted[c][b] for c in (0, 1)] for b in (0, 1)]
        mine = plane_terms(shifted, stiff, 0)
        here = mine if here is None else [a + b for a, b in zip(here, mine)]
        layers.append(plane_terms(shifted, stiff, 1))
    here[4] = here[4] + potential_ref[...]
    after, back = layers
    paired = [jnp.where(odd, b, a) for a, b in zip(after, back)]
    far = [jnp.where(odd, a, b) for a, b in zip(after, back)]
    for at, term in enumerate(here + paired + far):
        terms_ref[at : at + 1, :] = term[:1]


def write_bands(terms, out_ref):
    row = lax.broadcasted_iota(jnp.int32, (SIDE, BLOCK), 0)
    lane = lax.broadcasted_iota(jnp.int32, (SIDE, BLOCK), 1)
    turn = (lane - row) & (SIDE - 1)
    for line in range(BLOCK // SIDE):
        rows = slice(line * SIDE, (line + 1) * SIDE)
        rest = slice(BLOCK + rows.start, BLOCK + rows.stop)
        masks = {}
        for dj, dk in OFFSETS:
            tile, group = divmod(line + MARGIN // SIDE + dj, BLOCK // SIDE)
            masks[dj, dk] = tile, (turn == dk % SIDE) & ((lane >> 5) == group)
        for plane in range(3):
            totals = [jnp.zeros((SIDE, BLOCK), jnp.float32) for _ in range(WINDOW // BLOCK)]
            for at, offset in enumerate(OFFSETS):
                term = terms[rows, plane * 9 + at : plane * 9 + at + 1]
                tile, mask = masks[offset]
                totals[tile] = jnp.where(mask, term, totals[tile])
            for tile, total in enumerate(totals):
                columns = slice(tile * BLOCK, (tile + 1) * BLOCK)
                out_ref[plane, 0, rows, columns], out_ref[plane, 0, rest, columns] = halves(total)


def prepare_kernel(stiff, odd_ref, own_ref, before_ref, potential_ref, map_ref, prev_ref, *refs):
    band_ref, last_ref, terms_ref, high_ref, low_ref = refs
    step = pl.program_id(0)
    nodes = prev_ref.shape[0]

    @pl.when(step == 0)
    def _():
        write_terms(stiff, odd_ref[0] == 1, own_ref, before_ref, potential_ref, terms_ref)
        split_columns([[prev_ref]], high_ref, low_ref, 0)

    write_bands(terms_ref[:, pl.ds(pl.multiple_of(step * BLOCK, BLOCK), BLOCK)].T, band_ref)
    place = lax.broadcasted_iota(jnp.int32, (BLOCK, nodes), 1)
    column = jnp.broadcast_to(map_ref[pl.ds(step, 1), :], (BLOCK, BLOCK)).T
    column = jnp.concatenate([column] * (nodes // BLOCK), axis=1)
    pick = jnp.where(place == column, 1.0, 0.0).astype(jnp.bfloat16)
    last_ref[...] = dot(pick, high_ref[...]) + dot(pick, low_ref[...])


def prepare(stiff, odd, own, before, potential, face_map, y_prev, after):
    nodes, states = y_prev.shape
    row = pl.BlockSpec((1, nodes), lambda i: (0, 0))
    return call(
        functools.partial(prepare_kernel, stiff),
        after,
        grid=(nodes // BLOCK,),
        in_specs=[pl.BlockSpec(memory_space=pltpu.SMEM), row, row, row]
        + [pl.BlockSpec((nodes // BLOCK, BLOCK), lambda i: (0, 0))]
        + [pl.BlockSpec((nodes, states), lambda i: (0, 0))],
        out_specs=[
            pl.BlockSpec((3, 1, 2 * BLOCK, WINDOW), lambda i: (0, i, 0, 0)),
            pl.BlockSpec((BLOCK, states), lambda i: (i, 0)),
        ],
        out_shape=[
            jax.ShapeDtypeStruct((3, nodes // BLOCK, 2 * BLOCK, WINDOW), jnp.bfloat16),
            jax.ShapeDtypeStruct((nodes, states), jnp.float32),
        ],
        scratch_shapes=[pltpu.VMEM((32, nodes), jnp.float32)]
        + [pltpu.VMEM((nodes, states), jnp.bfloat16)] * 2,
        name="prepare",
    )(
        odd,
        *[x.reshape(1, nodes) for x in (own, before, potential)],
        face_map.reshape(nodes // BLOCK, BLOCK),
        y_prev,
    )


def apply_kernel(filtered, pieces, band_ref, own_ref, paired_ref, *refs):
    far_refs, refs, wide = refs[:pieces], refs[pieces:], refs[-1]
    step = pl.program_id(0)
    nodes, width = own_ref.shape

    @pl.when(step == 0)
    def _():
        sources = [(0, 0, own_ref), (1, 0, paired_ref)]
        sources += [(2, at * width // pieces, ref) for at, ref in enumerate(far_refs)]
        for plane, first, ref in sources:
            for start, part in zip((first, width + first), halves(ref[...])):
                columns = slice(start, start + part.shape[1])
                wide[plane, pl.ds(MARGIN, nodes), columns] = part
                wide[plane, pl.ds(0, MARGIN), columns] = part[nodes - MARGIN :]
                wide[plane, pl.ds(MARGIN + nodes, MARGIN), columns] = part[:MARGIN]

    per_step = band_ref.shape[1]
    for at in range(per_step):
        block = step * per_step + at
        first = pl.multiple_of(block * BLOCK, BLOCK)
        total = None
        for plane in range(3):
            term = dot(band_ref[plane, at], wide[plane, pl.ds(first, WINDOW), :])
            total = term if total is None else total + term
        total = total[:BLOCK] + total[BLOCK:]
        total = total[:, :width] + total[:, width:]
        rows = pl.ds(at * BLOCK, BLOCK)
        if filtered:
            last_ref, out_ref, whole_ref, turned_high, turned_low = refs[:5]
            mine = own_ref[pl.ds(first, BLOCK), :]
            total = (2.0 / half_width) * (total - centre * mine) - last_ref[rows, :]
            out_ref[rows, :] = total
            whole_ref[rows, :] = total
        else:
            turned_high, turned_low = refs[:2]
        turned_high[:, rows], turned_low[:, rows] = halves(total.T)


def apply_specs(nodes, width):
    per_step = 2
    rows = per_step * BLOCK
    return dict(
        grid=(nodes // rows,),
        scratch_shapes=[pltpu.VMEM((3, nodes + 2 * MARGIN, 2 * width), jnp.bfloat16)],
        name="apply_h",
    ), pl.BlockSpec((3, per_step, 2 * BLOCK, WINDOW), lambda i: (0, i, 0, 0)), rows


def next_degree(band, own, paired, far, last, at, so_far, after):
    nodes, width = far.shape
    states = own.shape[1]
    options, band_spec, rows = apply_specs(nodes, width)
    column = pl.BlockSpec((nodes, width), lambda i: (0, at))
    part = pl.BlockSpec((rows, width), lambda i: (i, at))
    turned = pl.BlockSpec((width, rows), lambda i: (at, i))
    turned_shape = jax.ShapeDtypeStruct((states, nodes), jnp.bfloat16)
    return call(
        functools.partial(apply_kernel, True, 1),
        after,
        into=[(out, so_far[out - 1]) for out in (1, 2, 3) if at],
        in_specs=[band_spec, column, column, pl.BlockSpec((nodes, width), lambda i: (0, 0)), part],
        out_specs=[pl.BlockSpec((rows, width), lambda i: (i, 0)), part, turned, turned],
        out_shape=[
            jax.ShapeDtypeStruct((nodes, width), jnp.float32),
            jax.ShapeDtypeStruct((nodes, states), jnp.float32),
            turned_shape,
            turned_shape,
        ],
        **options,
    )(band, own, paired, far, last)


def applied_next(band, own, paired, far, after=()):
    nodes, states = own.shape
    options, band_spec, rows = apply_specs(nodes, states)
    whole = pl.BlockSpec((nodes, states), lambda i: (0, 0))
    turned = pl.BlockSpec((states, rows), lambda i: (0, i))
    turned_shape = jax.ShapeDtypeStruct((states, nodes), jnp.bfloat16)
    return call(
        functools.partial(apply_kernel, False, len(far)),
        after,
        in_specs=[band_spec, whole, whole] + [pl.BlockSpec(x.shape, lambda i: (0, 0)) for x in far],
        out_specs=[turned, turned],
        out_shape=[turned_shape, turned_shape],
        **options,
    )(band, own, paired, *far)


def split_columns(pieces, high_ref, low_ref, first):
    for group in pieces:
        piece = group[0][...]
        for other in group[1:]:
            piece = piece + other[...]
        columns = slice(first, first + piece.shape[1])
        first += piece.shape[1]
        high_ref[:, columns], low_ref[:, columns] = halves(piece)


def rows_product(left_high, left_low, high_ref, low_ref):
    total = dot(left_high[...], high_ref[...]) + dot(left_high[...], low_ref[...])
    return total + dot(left_low[...], high_ref[...])


def sorted_kernel(count, keep_ref, left_high, left_low, *refs):
    own, first = [[x] for x in refs[:count]], [[x] for x in refs[count:-4]]
    kept_ref, sent_ref, high_ref, low_ref = refs[-4:]
    width = kept_ref.shape[1]

    @pl.when((pl.program_id(0) == 0) & (keep_ref[0] == 1))
    def _():
        split_columns(own, high_ref, low_ref, 0)
        split_columns(first, high_ref, low_ref, width)

    @pl.when((pl.program_id(0) == 0) & (keep_ref[0] != 1))
    def _():
        split_columns(own, high_ref, low_ref, width)
        split_columns(first, high_ref, low_ref, 0)

    total = rows_product(left_high, left_low, high_ref, low_ref)
    kept_ref[...] = total[:, :width]
    sent_ref[...] = total[:, width:]


def sorted_products(keep, turned, own, first, at, so_far, after=(), passed=()):
    states, nodes = turned[0].shape
    rows = 256
    steps = states // rows
    width = sum(piece.shape[1] for piece in own)
    left = pl.BlockSpec((rows, nodes), lambda i: (i, 0))
    out = pl.BlockSpec((rows, width), lambda i: (i + at * steps, 0))
    shape = jax.ShapeDtypeStruct((2 * states, width), jnp.float32)
    return call(
        functools.partial(sorted_kernel, len(own)),
        after,
        into=list(enumerate(so_far)) if at else [],
        passed=passed,
        grid=(steps,),
        in_specs=[pl.BlockSpec(memory_space=pltpu.SMEM), left, left]
        + [pl.BlockSpec(piece.shape, lambda i: (0, 0)) for piece in (*own, *first)],
        out_specs=[out, out],
        out_shape=[shape, shape],
        scratch_shapes=[pltpu.VMEM((nodes, 2 * width), jnp.bfloat16)] * 2,
        name="sorted_products",
    )(keep, *turned, *own, *first)


def both_kernel(summed, left_high, left_low, more_high, more_low, *refs):
    pieces, (out_ref, high_ref, low_ref) = refs[:-3], refs[-3:]
    step, half = pl.program_id(0), pl.num_programs(0) // 2

    @pl.when(step == 0)
    def _():
        groups = [pieces[at : at + summed] for at in range(0, len(pieces), summed)]
        split_columns(groups, high_ref, low_ref, 0)

    @pl.when(step < half)
    def _():
        out_ref[...] = rows_product(left_high, left_low, high_ref, low_ref)

    @pl.when(step >= half)
    def _():
        out_ref[...] = rows_product(more_high, more_low, high_ref, low_ref)


def both_products(y_turned, h_turned, pieces, summed=1, after=(), passed=()):
    states, nodes = y_turned[0].shape
    rows = 256
    steps = states // rows
    width = sum(piece.shape[1] for piece in pieces) // summed
    first = pl.BlockSpec((rows, nodes), lambda i: (jnp.minimum(i, steps - 1), 0))
    second = pl.BlockSpec((rows, nodes), lambda i: (jnp.maximum(i - steps, 0), 0))
    return call(
        functools.partial(both_kernel, summed),
        after,
        grid=(2 * steps,),
        in_specs=[first, first, second, second]
        + [pl.BlockSpec(piece.shape, lambda i: (0, 0)) for piece in pieces],
        out_specs=[pl.BlockSpec((rows, width), lambda i: (i, 0))],
        out_shape=[jax.ShapeDtypeStruct((2 * states, width), jnp.float32)],
        passed=passed,
        scratch_shapes=[pltpu.VMEM((nodes, width), jnp.bfloat16)] * 2,
        name="both_products",
    )(*y_turned, *h_turned, *pieces)


def pair_kernel(keep_ref, left_high, left_low, more_high, more_low, block_ref, piece_ref, other_ref, *refs):
    kept_ref, sent_ref, high_ref, low_ref = refs
    step, half = pl.program_id(0), pl.num_programs(0) // 2

    @pl.when(step == 0)
    def _():
        split_columns([[piece_ref, other_ref]], high_ref, low_ref, 0)

    def write(total):
        keeps = keep_ref[0] == 1
        kept_ref[...] = jnp.where(keeps, block_ref[...], total)
        sent_ref[...] = jnp.where(keeps, total, block_ref[...])

    @pl.when(step < half)
    def _():
        write(rows_product(left_high, left_low, high_ref, low_ref))

    @pl.when(step >= half)
    def _():
        write(rows_product(more_high, more_low, high_ref, low_ref))


def pair_products(keep, y_turned, h_turned, block, piece, other, after):
    states, nodes = y_turned[0].shape
    rows = 256
    steps = states // rows
    width = piece.shape[1]
    first = pl.BlockSpec((rows, nodes), lambda i: (jnp.minimum(i, steps - 1), 0))
    second = pl.BlockSpec((rows, nodes), lambda i: (jnp.maximum(i - steps, 0), 0))
    whole = pl.BlockSpec((nodes, width), lambda i: (0, 0))
    out = pl.BlockSpec((rows, width), lambda i: (i, 0))
    return call(
        pair_kernel,
        after,
        grid=(2 * steps,),
        in_specs=[pl.BlockSpec(memory_space=pltpu.SMEM), first, first, second, second, out, whole, whole],
        out_specs=[out, out],
        out_shape=[jax.ShapeDtypeStruct((2 * states, width), jnp.float32)] * 2,
        scratch_shapes=[pltpu.VMEM((nodes, width), jnp.bfloat16)] * 2,
        name="pair_products",
    )(keep, *y_turned, *h_turned, block, piece, other)


def near_kernel(flags_ref, mine_ref, arrived_ref, out_ref):
    out_ref[...] = jnp.where(flags_ref[0] == 1, 1.0, 0.0) * (mine_ref[...] + arrived_ref[...])


def near_rows(flags, mine, arrived, after):
    whole = pl.BlockSpec(mine.shape, lambda i: (0, 0))
    return call(
        near_kernel,
        after,
        grid=(1,),
        in_specs=[pl.BlockSpec(memory_space=pltpu.SMEM), whole, whole],
        out_specs=whole,
        out_shape=jax.ShapeDtypeStruct(mine.shape, jnp.float32),
        name="near_rows",
    )(flags, mine, arrived)


def mark(after):
    shape = jax.ShapeDtypeStruct((8, 128), jnp.float32)

    def kernel(out_ref):
        out_ref[...] = jnp.zeros_like(out_ref)

    return call(kernel, after, in_specs=[], grid=(1,), out_specs=corner(shape), out_shape=shape, name="mark")()


def finish_kernel(weight, flags_ref, base_ref, one_ref, one_far, two_ref, two_far, *outs):
    one, two = [jnp.where(flags_ref[band] == 1, 1.0, 0.0) for band in (1, 2)]
    states = outs[0].shape[0]
    for half, out_ref in enumerate(outs):
        rows = slice(half * states, (half + 1) * states)
        total = base_ref[rows, :] + one * (one_ref[rows, :] + one_far[rows, :])
        out_ref[...] = weight * (total + two * (two_ref[rows, :] + two_far[rows, :]))


def finish(weight, at, flags, base, one, one_far, two, two_far, so_far, after):
    rows, width = one.shape
    states = rows // 2
    whole = pl.BlockSpec((rows, width), lambda i: (0, 0))
    part = pl.BlockSpec((states, width), lambda i: (0, at))
    shape = jax.ShapeDtypeStruct((states, base.shape[1]), jnp.float32)
    return call(
        functools.partial(finish_kernel, weight),
        after,
        into=[(out, x) for out, x in enumerate(so_far)],
        grid=(1,),
        in_specs=[pl.BlockSpec(memory_space=pltpu.SMEM), pl.BlockSpec((rows, width), lambda i: (0, at))]
        + [whole] * 4,
        out_specs=[part, part],
        out_shape=[shape, shape],
        name="finish",
    )(flags, base, one, one_far, two, two_far)


def exchange(block, axis, pairs):
    return lax.ppermute(block, axis, pairs + [(b, a) for a, b in pairs])


def paired(block):
    return exchange(block, "dom", [(i, i + 1) for i in range(0, lax.axis_size("dom"), 2)])


def crossed(block):
    size = lax.axis_size("dom")
    return exchange(block, "dom", [(i, (i + 1) % size) for i in range(1, size, 2)])


def to_owner(block, owners, step):
    size = len(owners)
    route = []
    for band, owner in enumerate(owners):
        for to in (owner, owner ^ 2) if step == 1 else (owner,):
            route.append(((to ^ step) * size + band, to * size + band))
    return lax.ppermute(block, ("dom", "band"), route)


def on_device(y_cur, y_prev, connect, face_map, elem_scale, potential):
    stiff = element_table()
    nodes, states = y_cur.shape
    domains, band_count = lax.axis_size("dom"), lax.axis_size("band")
    me, level = lax.axis_index("dom"), lax.axis_index("band")
    swaps = domains == 4 and band_count == 4 and states == STATES_DEV
    half = states // 2
    place = jnp.arange(nodes, dtype=jnp.int32)
    cell_place = connect[:, 4] - nodes
    own = jnp.sum(jnp.where(cell_place[:, None] == place[None, :], elem_scale[:, None], 0.0), axis=0)
    before = lax.ppermute(own, "dom", [(i, (i + 1) % domains) for i in range(domains)])
    at_grid = jnp.sum(jnp.where(place[:, None] == face_map[None, :], potential[:, None], 0.0), axis=0)
    odd = (me % 2).astype(jnp.int32).reshape(1)
    weight = 1.0 / (nodes * domains)

    far, current, waited = [], None, ()
    for at in (0, 1):
        chunk, current = to_grid(face_map, y_cur, at, half, current, waited)
        far.append(crossed(chunk))
        waited = (chunk,)
    current_paired = paired(current)
    band, last = prepare(stiff, odd, own, before, at_grid, face_map, y_prev, (current,))

    following, so_far, waited = [], [None] * 3, ()
    for at, piece in enumerate(far):
        chunk, *so_far = next_degree(band, current, current_paired, piece, last, at, so_far, waited)
        following.append(chunk)
        waited = (chunk,)
    whole, *y_turned = so_far
    next_far = [crossed(following[0])]

    if not swaps:
        y_next, again, other = from_grid(face_map, whole)
        next_far.append(crossed(other))
        h_turned = applied_next(band, whole, paired(again), next_far)
        piece = lax.all_gather(whole, "band", axis=1, tiled=True)
        (block,) = both_products(y_turned, h_turned, [piece])
        parts = [
            weight * lax.psum_scatter(rows, "dom", scatter_dimension=1, tiled=True)
            for rows in (block[:states], block[states:])
        ]
        return (y_next, *parts)

    outward = [(2, 3), (1, 0)]
    core, chip, upper = me % 2, me // 2, level // 2
    keep = jnp.where(core == level % 2, 1, 0).astype(jnp.int32).reshape(1)
    near_route = [
        (((b // 2 * 2 + c) ^ 2) * 4 + b, (b // 2 * 2 + c) * 4 + b) for b in range(4) for c in (0, 1)
    ]
    near_across = lambda x: lax.ppermute(x, ("dom", "band"), near_route)
    second_owner, third_owner = [2, 2, 1, 1], [3, 3, 0, 0]

    ends, middle = [(0, 1), (2, 3)], [(1, 2)]
    first = [exchange(x, "band", ends) for x in following]
    second_middle = [exchange(x, "band", middle) for x in following]
    waited = (first[0], second_middle[0], next_far[0])
    y_next, again, other, second_middle[0] = from_grid(face_map, whole, waited, second_middle[:1])
    next_far.append(crossed(other))
    second_out = [lax.ppermute(second_middle[0], "band", outward)]
    whole_paired = paired(again)
    (first[0],) = gate(first[:1], (mark((y_next,)), whole_paired, second_middle[1]))
    third_middle = [exchange(first[0], "band", middle)]
    *near, second_middle[1] = sorted_products(keep, y_turned, following, first, 0, (), (), second_middle[1:])
    second_out.append(lax.ppermute(second_middle[1], "band", outward))
    h_turned = applied_next(band, whole, whole_paired, next_far, (near[0],))
    (first[1],) = gate(first[1:], (h_turned[0], third_middle[0]))
    third_middle.append(exchange(first[1], "band", middle))
    kept, sent, third_middle[0] = sorted_products(keep, h_turned, following, first, 1, near, (), third_middle[:1])
    third_out = [lax.ppermute(third_middle[0], "band", outward)]
    sent = paired(sent)

    blocks = [*both_products(y_turned, h_turned, [second_middle[0], second_out[0]], 2, (kept,))]
    cores = [to_owner(blocks[0], second_owner, 1)]
    (near,) = plus(kept, sent, (blocks[0],))
    near_far = near_across(near)
    blocks += both_products(y_turned, h_turned, [second_middle[1], second_out[1]], 2, (near, third_middle[1]))
    second, third_middle[1] = plus(blocks[0], cores[0], (blocks[1],), third_middle[1:])
    second_far = to_owner(second, second_owner, 2)
    third_out.append(lax.ppermute(third_middle[1], "band", outward))
    keep = jnp.where(core == upper, 1, 0).astype(jnp.int32).reshape(1)
    pieces = (blocks[1], third_middle[0], third_out[0])
    kept, sent = pair_products(keep, y_turned, h_turned, *pieces, (second,))
    sent = paired(sent)
    (pair,) = plus(kept, sent, (mark((kept,)),))
    pair_route = [
        (((2 - b // 2 * 2 + c) ^ 2) * 4 + b, (2 - b // 2 * 2 + c) * 4 + b) for b in range(4) for c in (0, 1)
    ]
    pair_far = lax.ppermute(pair, ("dom", "band"), pair_route)
    (block,) = both_products(y_turned, h_turned, [third_middle[1], third_out[1]], 2, (pair,))
    cores.append(to_owner(block, third_owner, 1))
    is_near, is_second = chip == upper, core == upper
    flags = jnp.stack([is_near, ~is_near & is_second, ~is_near & ~is_second]).astype(jnp.int32)
    base = near_rows(flags, near, near_far, (block, second_far))
    (third,) = plus(block, cores[1], (base,))
    third_far = to_owner(third, third_owner, 2)
    pieces = (second, second_far, pair, pair_far, third, third_far)
    outs = finish(weight, 0, flags, base, *pieces[:4], (), (third,))
    return (y_next, *finish(weight, 1, flags, base, *pieces[2:], outs, ()))


def solution(mesh):
    placed = (
        P(("image", "dom"), "band"),
        P(("image", "dom"), "band"),
        P("dom", None),
        P("dom"),
        P("dom"),
        P(("image", "dom")),
    )
    return jax.shard_map(
        on_device,
        mesh=mesh,
        in_specs=placed,
        out_specs=(
            P(("image", "dom"), "band"),
            P(("image", "band"), "dom"),
            P(("image", "band"), "dom"),
        ),
        check_vma=False,
    )
```

```python
import functools

import jax
import jax.numpy as jnp
import numpy as np
from jax import lax
from jax.experimental import pallas as pl
from jax.experimental.pallas import tpu as pltpu
from jax.sharding import PartitionSpec as P

SIDE = 32
STATES_DEV = 512
BLOCK = 128
WINDOW = 256
MARGIN = (WINDOW - BLOCK) // 2

cheb_low = 1.0
cheb_high = 9.0
centre = 0.5 * (cheb_high + cheb_low)
half_width = 0.5 * (cheb_high - cheb_low)

OFFSETS = [(dj, dk) for dj in (-1, 0, 1) for dk in (-1, 0, 1)]
PARAMS = pltpu.CompilerParams(vmem_limit_bytes=32 * 1024 * 1024)


COST = pl.CostEstimate(flops=10**12, bytes_accessed=1, transcendentals=0)


def element_table():
    stiff_line = np.array([[1.0, -1.0], [-1.0, 1.0]])
    mass_line = np.array([[1.0 / 3.0, 1.0 / 6.0], [1.0 / 6.0, 1.0 / 3.0]])
    total = np.kron(stiff_line, np.kron(mass_line, mass_line))
    total = total + np.kron(mass_line, np.kron(stiff_line, mass_line))
    total = total + np.kron(mass_line, np.kron(mass_line, stiff_line))
    return total.astype(np.float32)


def halves(x):
    high = x.astype(jnp.bfloat16)
    low = (x - high.astype(jnp.float32)).astype(jnp.bfloat16)
    return high, low


def dot(a, b):
    return lax.dot_general(a, b, (((1,), (0,)), ((), ())), preferred_element_type=jnp.float32)


def corner(x):
    rows = 32 // x.dtype.itemsize
    return pl.BlockSpec((rows, 128), lambda *_: (0, 0))


def call(kernel, after, *, in_specs, out_specs, out_shape, name, into=(), passed=(), **options):
    count = len(in_specs)
    extra = [*[array for _, array in into], *after, *passed]
    aliases = {count + at: out for at, (out, _) in enumerate(into)}
    outs = len(out_shape) if isinstance(out_shape, (list, tuple)) else 1
    if passed:
        out_specs = [*out_specs, *map(corner, passed)]
        out_shape = [*out_shape, *[jax.ShapeDtypeStruct(x.shape, x.dtype) for x in passed]]
        aliases |= {count + len(extra) - len(passed) + at: outs + at for at in range(len(passed))}

    def body(*refs):
        rest = refs[count + len(extra) :]
        kernel(*refs[:count], *rest[:outs], *rest[outs + len(passed) :])
        first = count + len(extra) - len(passed)
        for x_ref, out_ref in zip(refs[first : first + len(passed)], rest[outs : outs + len(passed)]):
            out_ref[...] = x_ref[...]

    made = pl.pallas_call(
        body,
        in_specs=[*in_specs, *map(corner, extra)],
        out_specs=out_specs,
        out_shape=out_shape,
        input_output_aliases=aliases,
        compiler_params=PARAMS,
        cost_estimate=COST,
        name=name,
        **options,
    )
    return lambda *args: made(*args, *extra)


def gate(arrays, after):
    return call(lambda: None, after, passed=arrays, grid=(1,), in_specs=[], out_specs=[], out_shape=[], name="gate")()


def plus_kernel(left_ref, right_ref, out_ref):
    out_ref[...] = left_ref[...] + right_ref[...]


def plus(left, right, after, passed=()):
    rows = min(512, left.shape[0])
    part = pl.BlockSpec((rows, left.shape[1]), lambda i: (i, 0))
    return call(
        plus_kernel,
        after,
        grid=(left.shape[0] // rows,),
        in_specs=[part, part],
        out_specs=[part],
        out_shape=[jax.ShapeDtypeStruct(left.shape, left.dtype)],
        passed=passed,
        name="plus",
    )(left, right)


def to_grid_kernel(map_ref, x_ref, out_ref, whole_ref, high_ref, low_ref):
    step = pl.program_id(0)

    @pl.when(step == 0)
    def _():
        high_ref[...], low_ref[...] = halves(x_ref[...])

    rows, nodes = out_ref.shape[0], x_ref.shape[0]
    place = lax.broadcasted_iota(jnp.int32, (BLOCK, nodes), 1)
    for at in range(rows // BLOCK):
        row = map_ref[pl.ds(step * (rows // BLOCK) + at, 1), :]
        column = jnp.broadcast_to(row, (BLOCK, BLOCK)).T
        column = jnp.concatenate([column] * (nodes // BLOCK), axis=1)
        pick = jnp.where(place == column, 1.0, 0.0).astype(jnp.bfloat16)
        moved = dot(pick, high_ref[...]) + dot(pick, low_ref[...])
        out = slice(at * BLOCK, (at + 1) * BLOCK)
        out_ref[out, :] = moved
        whole_ref[out, :] = moved


def to_grid(face_map, x, at, width, so_far, after):
    nodes, states = x.shape
    rows = 512
    return call(
        to_grid_kernel,
        after,
        into=[(1, so_far)] if at else [],
        grid=(nodes // rows,),
        in_specs=[
            pl.BlockSpec((nodes // BLOCK, BLOCK), lambda i: (0, 0)),
            pl.BlockSpec((nodes, width), lambda i: (0, at)),
        ],
        out_specs=[pl.BlockSpec((rows, width), lambda i: (i, 0)), pl.BlockSpec((rows, width), lambda i: (i, at))],
        out_shape=[
            jax.ShapeDtypeStruct((nodes, width), jnp.float32),
            jax.ShapeDtypeStruct((nodes, states), jnp.float32),
        ],
        scratch_shapes=[pltpu.VMEM((nodes, width), jnp.bfloat16)] * 2,
        name="to_grid",
    )(face_map.reshape(nodes // BLOCK, BLOCK), x)


def from_grid_kernel(map_ref, x_ref, out_ref, again_ref, half_ref, high_ref, low_ref):
    step = pl.program_id(0)

    @pl.when(step == 0)
    def _():
        high_ref[...], low_ref[...] = halves(x_ref[...])

    rows, nodes = out_ref.shape[0], high_ref.shape[0]
    node = lax.broadcasted_iota(jnp.int32, (rows, nodes), 0) + step * rows
    pick = jnp.where(node == map_ref[...], 1.0, 0.0).astype(jnp.bfloat16)
    out_ref[...] = dot(pick, high_ref[...]) + dot(pick, low_ref[...])
    again = x_ref[pl.ds(pl.multiple_of(step * rows, rows), rows), :]
    again_ref[...] = again
    half_ref[...] = again[:, half_ref.shape[1] :]


def from_grid(face_map, x, after=(), passed=()):
    nodes, states = x.shape
    rows = 256
    part = pl.BlockSpec((rows, states), lambda i: (i, 0))
    return call(
        from_grid_kernel,
        after,
        passed=passed,
        grid=(nodes // rows,),
        in_specs=[pl.BlockSpec((1, nodes), lambda i: (0, 0)), pl.BlockSpec((nodes, states), lambda i: (0, 0))],
        out_specs=[part, part, pl.BlockSpec((rows, states // 2), lambda i: (i, 0))],
        out_shape=[jax.ShapeDtypeStruct((nodes, size), jnp.float32) for size in (states, states, states // 2)],
        scratch_shapes=[pltpu.VMEM((nodes, states), jnp.bfloat16)] * 2,
        name="from_grid",
    )(face_map.reshape(1, nodes), x)


def plane_terms(shifted, stiff, layer):
    terms = []
    for dj, dk in OFFSETS:
        total = None
        for b in (0, 1):
            for c in (0, 1):
                if b + dj in (0, 1) and c + dk in (0, 1):
                    weight = float(stiff[2 * b + c, 4 * layer + 2 * (b + dj) + c + dk])
                    term = weight * shifted[b][c]
                    total = term if total is None else total + term
        terms.append(total)
    return terms


def write_terms(stiff, odd, own_ref, before_ref, potential_ref, terms_ref):
    nodes = own_ref.shape[1]
    column = lax.broadcasted_iota(jnp.int32, (8, nodes), 1) & (SIDE - 1)
    here, layers = None, []
    for ref in (own_ref, before_ref):
        scale = jnp.broadcast_to(0.5 * ref[...], (8, nodes))
        back = jnp.where(column == 0, pltpu.roll(scale, nodes - SIDE + 1, 1), pltpu.roll(scale, 1, 1))
        shifted = [[x, pltpu.roll(x, SIDE, 1)] for x in (scale, back)]
        shifted = [[shifted[c][b] for c in (0, 1)] for b in (0, 1)]
        mine = plane_terms(shifted, stiff, 0)
        here = mine if here is None else [a + b for a, b in zip(here, mine)]
        layers.append(plane_terms(shifted, stiff, 1))
    here[4] = here[4] + potential_ref[...]
    after, back = layers
    paired = [jnp.where(odd, b, a) for a, b in zip(after, back)]
    far = [jnp.where(odd, a, b) for a, b in zip(after, back)]
    for at, term in enumerate(here + paired + far):
        terms_ref[at : at + 1, :] = term[:1]


def write_bands(terms, out_ref):
    row = lax.broadcasted_iota(jnp.int32, (SIDE, BLOCK), 0)
    lane = lax.broadcasted_iota(jnp.int32, (SIDE, BLOCK), 1)
    turn = (lane - row) & (SIDE - 1)
    for line in range(BLOCK // SIDE):
        rows = slice(line * SIDE, (line + 1) * SIDE)
        rest = slice(BLOCK + rows.start, BLOCK + rows.stop)
        masks = {}
        for dj, dk in OFFSETS:
            tile, group = divmod(line + MARGIN // SIDE + dj, BLOCK // SIDE)
            masks[dj, dk] = tile, (turn == dk % SIDE) & ((lane >> 5) == group)
        for plane in range(3):
            totals = [jnp.zeros((SIDE, BLOCK), jnp.float32) for _ in range(WINDOW // BLOCK)]
            for at, offset in enumerate(OFFSETS):
                term = terms[rows, plane * 9 + at : plane * 9 + at + 1]
                tile, mask = masks[offset]
                totals[tile] = jnp.where(mask, term, totals[tile])
            for tile, total in enumerate(totals):
                columns = slice(tile * BLOCK, (tile + 1) * BLOCK)
                out_ref[plane, 0, rows, columns], out_ref[plane, 0, rest, columns] = halves(total)


def prepare_kernel(stiff, odd_ref, own_ref, before_ref, potential_ref, map_ref, prev_ref, *refs):
    band_ref, last_ref, terms_ref, high_ref, low_ref = refs
    step = pl.program_id(0)
    nodes = prev_ref.shape[0]

    @pl.when(step == 0)
    def _():
        write_terms(stiff, odd_ref[0] == 1, own_ref, before_ref, potential_ref, terms_ref)
        split_columns([[prev_ref]], high_ref, low_ref, 0)

    write_bands(terms_ref[:, pl.ds(pl.multiple_of(step * BLOCK, BLOCK), BLOCK)].T, band_ref)
    place = lax.broadcasted_iota(jnp.int32, (BLOCK, nodes), 1)
    column = jnp.broadcast_to(map_ref[pl.ds(step, 1), :], (BLOCK, BLOCK)).T
    column = jnp.concatenate([column] * (nodes // BLOCK), axis=1)
    pick = jnp.where(place == column, 1.0, 0.0).astype(jnp.bfloat16)
    last_ref[...] = dot(pick, high_ref[...]) + dot(pick, low_ref[...])


def prepare(stiff, odd, own, before, potential, face_map, y_prev, after):
    nodes, states = y_prev.shape
    row = pl.BlockSpec((1, nodes), lambda i: (0, 0))
    return call(
        functools.partial(prepare_kernel, stiff),
        after,
        grid=(nodes // BLOCK,),
        in_specs=[pl.BlockSpec(memory_space=pltpu.SMEM), row, row, row]
        + [pl.BlockSpec((nodes // BLOCK, BLOCK), lambda i: (0, 0))]
        + [pl.BlockSpec((nodes, states), lambda i: (0, 0))],
        out_specs=[
            pl.BlockSpec((3, 1, 2 * BLOCK, WINDOW), lambda i: (0, i, 0, 0)),
            pl.BlockSpec((BLOCK, states), lambda i: (i, 0)),
        ],
        out_shape=[
            jax.ShapeDtypeStruct((3, nodes // BLOCK, 2 * BLOCK, WINDOW), jnp.bfloat16),
            jax.ShapeDtypeStruct((nodes, states), jnp.float32),
        ],
        scratch_shapes=[pltpu.VMEM((32, nodes), jnp.float32)]
        + [pltpu.VMEM((nodes, states), jnp.bfloat16)] * 2,
        name="prepare",
    )(
        odd,
        *[x.reshape(1, nodes) for x in (own, before, potential)],
        face_map.reshape(nodes // BLOCK, BLOCK),
        y_prev,
    )


def fill(wide, plane, ref, start, width):
    nodes = ref.shape[0]
    for first, part in zip((start, width + start), halves(ref[...])):
        columns = slice(first, first + part.shape[1])
        wide[plane, pl.ds(MARGIN, nodes), columns] = part
        wide[plane, pl.ds(0, MARGIN), columns] = part[nodes - MARGIN :]
        wide[plane, pl.ds(MARGIN + nodes, MARGIN), columns] = part[:MARGIN]


def applied_rows(band_ref, at, wide, first):
    total = None
    for plane in range(band_ref.shape[0]):
        term = dot(band_ref[plane, at], wide[plane, pl.ds(first, WINDOW), :])
        total = term if total is None else total + term
    total = total[:BLOCK] + total[BLOCK:]
    width = total.shape[1] // 2
    return total[:, :width] + total[:, width:]


def on_chip_kernel(filtered, band_ref, own_ref, paired_ref, *refs):
    last_ref, (out_ref, wide) = refs[0], refs[-2:]
    step = pl.program_id(0)
    width = own_ref.shape[1]

    @pl.when(step == 0)
    def _():
        for plane, ref in enumerate((own_ref, paired_ref)):
            fill(wide, plane, ref, 0, width)

    per_step = band_ref.shape[1]
    for at in range(per_step):
        first = pl.multiple_of((step * per_step + at) * BLOCK, BLOCK)
        total = applied_rows(band_ref, at, wide, first)
        rows = pl.ds(at * BLOCK, BLOCK)
        if filtered:
            total = (2.0 / half_width) * (total - centre * own_ref[pl.ds(first, BLOCK), :]) - last_ref[rows, :]
        out_ref[rows, :] = total


def across_kernel(filtered, pieces, band_ref, part_ref, *refs):
    far_refs, outs, wide = refs[:pieces], refs[pieces:-1], refs[-1]
    step = pl.program_id(0)
    width = part_ref.shape[1]

    @pl.when(step == 0)
    def _():
        for at, ref in enumerate(far_refs):
            fill(wide, 0, ref, at * width // pieces, width)

    per_step = band_ref.shape[1]
    for at in range(per_step):
        first = pl.multiple_of((step * per_step + at) * BLOCK, BLOCK)
        total = applied_rows(band_ref, at, wide, first)
        rows = pl.ds(at * BLOCK, BLOCK)
        if filtered:
            total = (2.0 / half_width) * total
        total = part_ref[rows, :] + total
        for out_ref in outs[:-2]:
            out_ref[rows, :] = total
        for out_ref, half in zip(outs[-2:], halves(total.T)):
            out_ref[:, rows] = half


PER_STEP = 2


def on_chip(band, own, paired, last, after=()):
    nodes, states = own.shape
    rows = PER_STEP * BLOCK
    whole = pl.BlockSpec((nodes, states), lambda i: (0, 0))
    part = pl.BlockSpec((rows, states), lambda i: (i, 0))
    return call(
        functools.partial(on_chip_kernel, last is not None),
        after,
        grid=(nodes // rows,),
        in_specs=[pl.BlockSpec((2, PER_STEP, 2 * BLOCK, WINDOW), lambda i: (0, i, 0, 0)), whole, whole]
        + [part] * (last is not None),
        out_specs=part,
        out_shape=jax.ShapeDtypeStruct((nodes, states), jnp.float32),
        scratch_shapes=[pltpu.VMEM((2, nodes + 2 * MARGIN, 2 * states), jnp.bfloat16)],
        name="on_chip",
    )(band, own, paired, *([] if last is None else [last]))


def across_specs(nodes, width):
    rows = PER_STEP * BLOCK
    return dict(
        grid=(nodes // rows,),
        scratch_shapes=[pltpu.VMEM((1, nodes + 2 * MARGIN, 2 * width), jnp.bfloat16)],
        name="across",
    ), pl.BlockSpec((1, PER_STEP, 2 * BLOCK, WINDOW), lambda i: (2, i, 0, 0))


def next_degree(band, terms, far, at, so_far, after):
    nodes, width = far.shape
    states = terms.shape[1]
    rows = PER_STEP * BLOCK
    options, band_spec = across_specs(nodes, width)
    part = pl.BlockSpec((rows, width), lambda i: (i, at))
    turned = pl.BlockSpec((width, rows), lambda i: (at, i))
    turned_shape = jax.ShapeDtypeStruct((states, nodes), jnp.bfloat16)
    return call(
        functools.partial(across_kernel, True, 1),
        after,
        into=[(out, so_far[out - 1]) for out in (1, 2, 3) if at],
        in_specs=[band_spec, part, pl.BlockSpec((nodes, width), lambda i: (0, 0))],
        out_specs=[pl.BlockSpec((rows, width), lambda i: (i, 0)), part, turned, turned],
        out_shape=[
            jax.ShapeDtypeStruct((nodes, width), jnp.float32),
            jax.ShapeDtypeStruct((nodes, states), jnp.float32),
            turned_shape,
            turned_shape,
        ],
        **options,
    )(band, terms, far)


def applied_next(band, terms, far, after=()):
    nodes, states = terms.shape
    rows = PER_STEP * BLOCK
    options, band_spec = across_specs(nodes, states)
    turned = pl.BlockSpec((states, rows), lambda i: (0, i))
    turned_shape = jax.ShapeDtypeStruct((states, nodes), jnp.bfloat16)
    return call(
        functools.partial(across_kernel, False, len(far)),
        after,
        in_specs=[band_spec, pl.BlockSpec((rows, states), lambda i: (i, 0))]
        + [pl.BlockSpec(x.shape, lambda i: (0, 0)) for x in far],
        out_specs=[turned, turned],
        out_shape=[turned_shape, turned_shape],
        **options,
    )(band, terms, *far)


def split_columns(pieces, high_ref, low_ref, first):
    for group in pieces:
        piece = group[0][...]
        for other in group[1:]:
            piece = piece + other[...]
        columns = slice(first, first + piece.shape[1])
        first += piece.shape[1]
        high_ref[:, columns], low_ref[:, columns] = halves(piece)


def rows_product(left_high, left_low, high_ref, low_ref):
    total = dot(left_high[...], high_ref[...]) + dot(left_high[...], low_ref[...])
    return total + dot(left_low[...], high_ref[...])


def sorted_kernel(count, keep_ref, left_high, left_low, *refs):
    own, first = [[x] for x in refs[:count]], [[x] for x in refs[count:-4]]
    kept_ref, sent_ref, high_ref, low_ref = refs[-4:]
    width = kept_ref.shape[1]

    @pl.when((pl.program_id(0) == 0) & (keep_ref[0] == 1))
    def _():
        split_columns(own, high_ref, low_ref, 0)
        split_columns(first, high_ref, low_ref, width)

    @pl.when((pl.program_id(0) == 0) & (keep_ref[0] != 1))
    def _():
        split_columns(own, high_ref, low_ref, width)
        split_columns(first, high_ref, low_ref, 0)

    total = rows_product(left_high, left_low, high_ref, low_ref)
    kept_ref[...] = total[:, :width]
    sent_ref[...] = total[:, width:]


def sorted_products(keep, turned, own, first, at, so_far, after=(), passed=()):
    states, nodes = turned[0].shape
    rows = 256
    steps = states // rows
    width = sum(piece.shape[1] for piece in own)
    left = pl.BlockSpec((rows, nodes), lambda i: (i, 0))
    out = pl.BlockSpec((rows, width), lambda i: (i + at * steps, 0))
    shape = jax.ShapeDtypeStruct((2 * states, width), jnp.float32)
    return call(
        functools.partial(sorted_kernel, len(own)),
        after,
        into=list(enumerate(so_far)) if at else [],
        passed=passed,
        grid=(steps,),
        in_specs=[pl.BlockSpec(memory_space=pltpu.SMEM), left, left]
        + [pl.BlockSpec(piece.shape, lambda i: (0, 0)) for piece in (*own, *first)],
        out_specs=[out, out],
        out_shape=[shape, shape],
        scratch_shapes=[pltpu.VMEM((nodes, 2 * width), jnp.bfloat16)] * 2,
        name="sorted_products",
    )(keep, *turned, *own, *first)


def both_kernel(summed, left_high, left_low, more_high, more_low, *refs):
    pieces, (out_ref, high_ref, low_ref) = refs[:-3], refs[-3:]
    step, half = pl.program_id(0), pl.num_programs(0) // 2

    @pl.when(step == 0)
    def _():
        groups = [pieces[at : at + summed] for at in range(0, len(pieces), summed)]
        split_columns(groups, high_ref, low_ref, 0)

    @pl.when(step < half)
    def _():
        out_ref[...] = rows_product(left_high, left_low, high_ref, low_ref)

    @pl.when(step >= half)
    def _():
        out_ref[...] = rows_product(more_high, more_low, high_ref, low_ref)


def both_products(y_turned, h_turned, pieces, summed=1, after=(), passed=()):
    states, nodes = y_turned[0].shape
    rows = 256
    steps = states // rows
    width = sum(piece.shape[1] for piece in pieces) // summed
    first = pl.BlockSpec((rows, nodes), lambda i: (jnp.minimum(i, steps - 1), 0))
    second = pl.BlockSpec((rows, nodes), lambda i: (jnp.maximum(i - steps, 0), 0))
    return call(
        functools.partial(both_kernel, summed),
        after,
        grid=(2 * steps,),
        in_specs=[first, first, second, second]
        + [pl.BlockSpec(piece.shape, lambda i: (0, 0)) for piece in pieces],
        out_specs=[pl.BlockSpec((rows, width), lambda i: (i, 0))],
        out_shape=[jax.ShapeDtypeStruct((2 * states, width), jnp.float32)],
        passed=passed,
        scratch_shapes=[pltpu.VMEM((nodes, width), jnp.bfloat16)] * 2,
        name="both_products",
    )(*y_turned, *h_turned, *pieces)


def pair_kernel(keep_ref, left_high, left_low, more_high, more_low, block_ref, piece_ref, other_ref, *refs):
    kept_ref, sent_ref, high_ref, low_ref = refs
    step, half = pl.program_id(0), pl.num_programs(0) // 2

    @pl.when(step == 0)
    def _():
        split_columns([[piece_ref, other_ref]], high_ref, low_ref, 0)

    def write(total):
        keeps = keep_ref[0] == 1
        kept_ref[...] = jnp.where(keeps, block_ref[...], total)
        sent_ref[...] = jnp.where(keeps, total, block_ref[...])

    @pl.when(step < half)
    def _():
        write(rows_product(left_high, left_low, high_ref, low_ref))

    @pl.when(step >= half)
    def _():
        write(rows_product(more_high, more_low, high_ref, low_ref))


def pair_products(keep, y_turned, h_turned, block, piece, other, after):
    states, nodes = y_turned[0].shape
    rows = 256
    steps = states // rows
    width = piece.shape[1]
    first = pl.BlockSpec((rows, nodes), lambda i: (jnp.minimum(i, steps - 1), 0))
    second = pl.BlockSpec((rows, nodes), lambda i: (jnp.maximum(i - steps, 0), 0))
    whole = pl.BlockSpec((nodes, width), lambda i: (0, 0))
    out = pl.BlockSpec((rows, width), lambda i: (i, 0))
    return call(
        pair_kernel,
        after,
        grid=(2 * steps,),
        in_specs=[pl.BlockSpec(memory_space=pltpu.SMEM), first, first, second, second, out, whole, whole],
        out_specs=[out, out],
        out_shape=[jax.ShapeDtypeStruct((2 * states, width), jnp.float32)] * 2,
        scratch_shapes=[pltpu.VMEM((nodes, width), jnp.bfloat16)] * 2,
        name="pair_products",
    )(keep, *y_turned, *h_turned, block, piece, other)


def near_kernel(flags_ref, mine_ref, arrived_ref, out_ref):
    out_ref[...] = jnp.where(flags_ref[0] == 1, 1.0, 0.0) * (mine_ref[...] + arrived_ref[...])


def near_rows(flags, mine, arrived, after):
    whole = pl.BlockSpec(mine.shape, lambda i: (0, 0))
    return call(
        near_kernel,
        after,
        grid=(1,),
        in_specs=[pl.BlockSpec(memory_space=pltpu.SMEM), whole, whole],
        out_specs=whole,
        out_shape=jax.ShapeDtypeStruct(mine.shape, jnp.float32),
        name="near_rows",
    )(flags, mine, arrived)


def mark(after):
    shape = jax.ShapeDtypeStruct((8, 128), jnp.float32)

    def kernel(out_ref):
        out_ref[...] = jnp.zeros_like(out_ref)

    return call(kernel, after, in_specs=[], grid=(1,), out_specs=corner(shape), out_shape=shape, name="mark")()


def most_kernel(weight, flags_ref, base_ref, one_ref, one_far, two_ref, two_far, *refs):
    third_refs, outs, rest_ref = refs[:-3], refs[-3:-1], refs[-1]
    one, two = [jnp.where(flags_ref[band] == 1, 1.0, 0.0) for band in (1, 2)]
    states, width = outs[0].shape
    for half, out_ref in enumerate(outs):
        rows = slice(half * states, (half + 1) * states)
        total = base_ref[rows, :width] + one * (one_ref[rows, :] + one_far[rows, :])
        pair = two_ref[rows, :] + two_far[rows, :]
        out_ref[...] = weight * (total + two * pair)
        rest = base_ref[rows, width:] + one * pair
        third = jnp.concatenate([x[rows, :] for x in third_refs], axis=1)
        rest_ref[rows, :] = weight * (rest + two * third)


def finish_most(weight, flags, base, one, one_far, two, two_far, *third):
    rows, width = one.shape
    states = rows // 2
    whole = pl.BlockSpec((rows, width), lambda i: (0, 0))
    shape = jax.ShapeDtypeStruct((states, base.shape[1]), jnp.float32)
    return call(
        functools.partial(most_kernel, weight),
        (),
        grid=(1,),
        in_specs=[pl.BlockSpec(memory_space=pltpu.SMEM), pl.BlockSpec(base.shape, lambda i: (0, 0))]
        + [whole] * 4
        + [pl.BlockSpec(x.shape, lambda i: (0, 0)) for x in third],
        out_specs=[pl.BlockSpec((states, width), lambda i: (0, 0))] * 2 + [whole],
        out_shape=[shape, shape, jax.ShapeDtypeStruct((rows, width), jnp.float32)],
        name="finish_most",
    )(flags, base, one, one_far, two, two_far, *third)


def finish_kernel(weight, upper_ref, lower_ref, *refs):
    far_refs, outs = refs[:-2], refs[-2:]
    far_refs = far_refs[: len(far_refs) // 2], far_refs[len(far_refs) // 2 :]
    for rest_ref, far, out_ref in zip((upper_ref, lower_ref), far_refs, outs):
        arrived = jnp.concatenate([x[...] for x in far], axis=1)
        out_ref[...] = rest_ref[...] + weight * arrived


def finish(weight, outs, rest, far):
    states, width = outs[0].shape
    steps, half = 2, width // 2
    rows = states // steps
    upper = lambda size: pl.BlockSpec((rows, size), lambda i: (i, 0))
    lower = lambda size: pl.BlockSpec((rows, size), lambda i: (i + steps, 0))
    return call(
        functools.partial(finish_kernel, weight),
        (),
        into=list(enumerate(outs)),
        grid=(steps,),
        in_specs=[upper(half), lower(half)]
        + [upper(x.shape[1]) for x in far]
        + [lower(x.shape[1]) for x in far],
        out_specs=[pl.BlockSpec((rows, half), lambda i: (i, 1))] * 2,
        out_shape=[jax.ShapeDtypeStruct((states, width), jnp.float32)] * 2,
        name="finish",
    )(rest, rest, *far, *far)


def exchange(block, axis, pairs):
    return lax.ppermute(block, axis, pairs + [(b, a) for a, b in pairs])


def paired(block):
    return exchange(block, "dom", [(i, i + 1) for i in range(0, lax.axis_size("dom"), 2)])


def crossed(block):
    size = lax.axis_size("dom")
    return exchange(block, "dom", [(i, (i + 1) % size) for i in range(1, size, 2)])


def to_owner(block, owners, step):
    size = len(owners)
    route = []
    for band, owner in enumerate(owners):
        for to in (owner, owner ^ 2) if step == 1 else (owner,):
            route.append(((to ^ step) * size + band, to * size + band))
    return lax.ppermute(block, ("dom", "band"), route)


def on_device(y_cur, y_prev, connect, face_map, elem_scale, potential):
    stiff = element_table()
    nodes, states = y_cur.shape
    domains, band_count = lax.axis_size("dom"), lax.axis_size("band")
    me, level = lax.axis_index("dom"), lax.axis_index("band")
    swaps = domains == 4 and band_count == 4 and states == STATES_DEV
    half = states // 2
    place = jnp.arange(nodes, dtype=jnp.int32)
    cell_place = connect[:, 4] - nodes
    own = jnp.sum(jnp.where(cell_place[:, None] == place[None, :], elem_scale[:, None], 0.0), axis=0)
    before = lax.ppermute(own, "dom", [(i, (i + 1) % domains) for i in range(domains)])
    at_grid = jnp.sum(jnp.where(place[:, None] == face_map[None, :], potential[:, None], 0.0), axis=0)
    odd = (me % 2).astype(jnp.int32).reshape(1)
    weight = 1.0 / (nodes * domains)

    far, current, waited = [], None, ()
    for at in (0, 1):
        chunk, current = to_grid(face_map, y_cur, at, half, current, waited)
        far.append(crossed(chunk))
        waited = (chunk,)
    current_paired = paired(current)
    band, last = prepare(stiff, odd, own, before, at_grid, face_map, y_prev, (current,))

    terms = on_chip(band, current, current_paired, last)
    following, so_far, waited = [], [None] * 3, ()
    for at, piece in enumerate(far):
        chunk, *so_far = next_degree(band, terms, piece, at, so_far, waited)
        following.append(chunk)
        waited = (chunk,)
    whole, *y_turned = so_far
    next_far = [crossed(following[0])]

    if not swaps:
        y_next, again, other = from_grid(face_map, whole)
        next_far.append(crossed(other))
        h_turned = applied_next(band, on_chip(band, whole, paired(again), None), next_far)
        piece = lax.all_gather(whole, "band", axis=1, tiled=True)
        (block,) = both_products(y_turned, h_turned, [piece])
        parts = [
            weight * lax.psum_scatter(rows, "dom", scatter_dimension=1, tiled=True)
            for rows in (block[:states], block[states:])
        ]
        return (y_next, *parts)

    outward = [(2, 3), (1, 0)]
    core, chip, upper = me % 2, me // 2, level // 2
    keep = jnp.where(core == level % 2, 1, 0).astype(jnp.int32).reshape(1)
    near_route = [
        (((b // 2 * 2 + c) ^ 2) * 4 + b, (b // 2 * 2 + c) * 4 + b) for b in range(4) for c in (0, 1)
    ]
    near_across = lambda x: lax.ppermute(x, ("dom", "band"), near_route)
    second_owner, third_owner = [2, 2, 1, 1], [3, 3, 0, 0]

    ends, middle = [(0, 1), (2, 3)], [(1, 2)]
    first = [exchange(x, "band", ends) for x in following]
    second_middle = [exchange(x, "band", middle) for x in following]
    waited = (first[0], next_far[0])
    y_next, again, other, second_middle[0] = from_grid(face_map, whole, waited, second_middle[:1])
    next_far.append(crossed(other))
    second_out = [lax.ppermute(second_middle[0], "band", outward)]
    whole_paired = paired(again)
    (first[0],) = gate(first[:1], (mark((y_next,)), whole_paired, second_middle[1]))
    third_middle = [exchange(first[0], "band", middle)]
    *near, second_middle[1] = sorted_products(keep, y_turned, following, first, 0, (), (), second_middle[1:])
    second_out.append(lax.ppermute(second_middle[1], "band", outward))
    h_turned = applied_next(band, on_chip(band, whole, whole_paired, None, near[:1]), next_far)
    (first[1],) = gate(first[1:], (h_turned[0], third_middle[0]))
    third_middle.append(exchange(first[1], "band", middle))
    kept, sent, third_middle[0] = sorted_products(keep, h_turned, following, first, 1, near, (), third_middle[:1])
    third_out = [lax.ppermute(third_middle[0], "band", outward)]
    sent = paired(sent)

    blocks = [*both_products(y_turned, h_turned, [second_middle[0], second_out[0]], 2, (kept,))]
    cores = [to_owner(blocks[0], second_owner, 1)]
    (near,) = plus(kept, sent, (blocks[0],))
    near_far = near_across(near)
    pieces = [second_middle[1], second_out[1]]
    block, third_middle[1] = both_products(y_turned, h_turned, pieces, 2, (near,), third_middle[1:])
    blocks.append(block)
    tails = [third_middle[1][:, : half // 2], third_middle[1][:, half // 2 :]]
    (second,) = plus(blocks[0], cores[0], (blocks[1],))
    second_far = to_owner(second, second_owner, 2)
    tails_out = [lax.ppermute(tails[0], "band", outward)]
    keep = jnp.where(core == upper, 1, 0).astype(jnp.int32).reshape(1)
    pieces = (blocks[1], third_middle[0], third_out[0])
    kept, sent = pair_products(keep, y_turned, h_turned, *pieces, (second,))
    sent = paired(sent)
    (tails[1],) = gate(tails[1:], (kept, second_far))
    tails_out.append(lax.ppermute(tails[1], "band", outward))
    (pair,) = plus(kept, sent, tails[1:])
    pair_route = [
        (((2 - b // 2 * 2 + c) ^ 2) * 4 + b, (2 - b // 2 * 2 + c) * 4 + b) for b in range(4) for c in (0, 1)
    ]
    pair_far = lax.ppermute(pair, ("dom", "band"), pair_route)
    blocks, waited = [], (pair,)
    for piece in zip(tails, tails_out):
        blocks += both_products(y_turned, h_turned, list(piece), 2, waited)
        waited = blocks[-1:]
    cores = [to_owner(block, third_owner, 1) for block in blocks]
    third = [*plus(blocks[0], cores[0], blocks[1:])]
    third += plus(blocks[1], cores[1], third)
    third_far = [to_owner(block, third_owner, 2) for block in third]
    is_near, is_second = chip == upper, core == upper
    flags = jnp.stack([is_near, ~is_near & is_second, ~is_near & ~is_second]).astype(jnp.int32)
    base = near_rows(flags, near, near_far, (third[1],))
    *outs, rest = finish_most(weight, flags, base, second, second_far, pair, pair_far, *third)
    return (y_next, *finish(weight, outs, rest, third_far))


def solution(mesh):
    placed = (
        P(("image", "dom"), "band"),
        P(("image", "dom"), "band"),
        P("dom", None),
        P("dom"),
        P("dom"),
        P(("image", "dom")),
    )
    return jax.shard_map(
        on_device,
        mesh=mesh,
        in_specs=placed,
        out_specs=(
            P(("image", "dom"), "band"),
            P(("image", "band"), "dom"),
            P(("image", "band"), "dom"),
        ),
        check_vma=False,
    )
```

```python
import functools

import jax
import jax.numpy as jnp
import numpy as np
from jax import lax
from jax.experimental import pallas as pl
from jax.experimental.pallas import tpu as pltpu
from jax.sharding import PartitionSpec as P

SIDE = 32
STATES_DEV = 512
BLOCK = 128
WINDOW = 256
MARGIN = (WINDOW - BLOCK) // 2

cheb_low = 1.0
cheb_high = 9.0
centre = 0.5 * (cheb_high + cheb_low)
half_width = 0.5 * (cheb_high - cheb_low)

OFFSETS = [(dj, dk) for dj in (-1, 0, 1) for dk in (-1, 0, 1)]
PARAMS = pltpu.CompilerParams(vmem_limit_bytes=32 * 1024 * 1024)


COST = pl.CostEstimate(flops=10**12, bytes_accessed=1, transcendentals=0)


def element_table():
    stiff_line = np.array([[1.0, -1.0], [-1.0, 1.0]])
    mass_line = np.array([[1.0 / 3.0, 1.0 / 6.0], [1.0 / 6.0, 1.0 / 3.0]])
    total = np.kron(stiff_line, np.kron(mass_line, mass_line))
    total = total + np.kron(mass_line, np.kron(stiff_line, mass_line))
    total = total + np.kron(mass_line, np.kron(mass_line, stiff_line))
    return total.astype(np.float32)


def halves(x):
    high = x.astype(jnp.bfloat16)
    low = (x - high.astype(jnp.float32)).astype(jnp.bfloat16)
    return high, low


def dot(a, b):
    return lax.dot_general(a, b, (((1,), (0,)), ((), ())), preferred_element_type=jnp.float32)


def corner(x):
    rows = 32 // x.dtype.itemsize
    return pl.BlockSpec((rows, 128), lambda *_: (0, 0))


def call(kernel, after, *, in_specs, out_specs, out_shape, name, into=(), passed=(), params=None, **options):
    count = len(in_specs)
    extra = [*[array for _, array in into], *after, *passed]
    aliases = {count + at: out for at, (out, _) in enumerate(into)}
    outs = len(out_shape) if isinstance(out_shape, (list, tuple)) else 1
    if passed:
        out_specs = [*out_specs, *map(corner, passed)]
        out_shape = [*out_shape, *[jax.ShapeDtypeStruct(x.shape, x.dtype) for x in passed]]
        aliases |= {count + len(extra) - len(passed) + at: outs + at for at in range(len(passed))}

    def body(*refs):
        rest = refs[count + len(extra) :]
        kernel(*refs[:count], *rest[:outs], *rest[outs + len(passed) :])
        first = count + len(extra) - len(passed)
        for x_ref, out_ref in zip(refs[first : first + len(passed)], rest[outs : outs + len(passed)]):
            out_ref[...] = x_ref[...]

    made = pl.pallas_call(
        body,
        in_specs=[*in_specs, *map(corner, extra)],
        out_specs=out_specs,
        out_shape=out_shape,
        input_output_aliases=aliases,
        compiler_params=params or PARAMS,
        cost_estimate=COST,
        name=name,
        **options,
    )
    return lambda *args: made(*args, *extra)


def gate(arrays, after):
    return call(lambda: None, after, passed=arrays, grid=(1,), in_specs=[], out_specs=[], out_shape=[], name="gate")()


def plus_kernel(left_ref, right_ref, out_ref):
    out_ref[...] = left_ref[...] + right_ref[...]


def plus(left, right, after, passed=()):
    rows = min(512, left.shape[0])
    part = pl.BlockSpec((rows, left.shape[1]), lambda i: (i, 0))
    return call(
        plus_kernel,
        after,
        grid=(left.shape[0] // rows,),
        in_specs=[part, part],
        out_specs=[part],
        out_shape=[jax.ShapeDtypeStruct(left.shape, left.dtype)],
        passed=passed,
        name="plus",
    )(left, right)


def to_grid_kernel(at, map_hbm, x_hbm, out_ref, whole_ref, map_ref, x_ref, high_ref, low_ref, sems):
    step = pl.program_id(0)
    width = x_ref.shape[1]

    @pl.when(step == 0)
    def _():
        copies = [
            pltpu.make_async_copy(x_hbm.at[:, pl.ds(at * width, width)], x_ref, sems.at[0]),
            pltpu.make_async_copy(map_hbm, map_ref, sems.at[1]),
        ]
        for copy in copies:
            copy.start()
        for copy in copies:
            copy.wait()
        high_ref[...], low_ref[...] = halves(x_ref[...])

    rows, nodes = out_ref.shape[0], x_ref.shape[0]
    place = lax.broadcasted_iota(jnp.int32, (BLOCK, nodes), 1)
    for part in range(rows // BLOCK):
        row = map_ref[pl.ds(step * (rows // BLOCK) + part, 1), :]
        column = jnp.broadcast_to(row, (BLOCK, BLOCK)).T
        column = jnp.concatenate([column] * (nodes // BLOCK), axis=1)
        pick = jnp.where(place == column, 1.0, 0.0).astype(jnp.bfloat16)
        moved = dot(pick, high_ref[...]) + dot(pick, low_ref[...])
        out = slice(part * BLOCK, (part + 1) * BLOCK)
        out_ref[out, :] = moved
        whole_ref[out, :] = moved


def to_grid(face_map, x, at, width, so_far, after):
    nodes, states = x.shape
    rows = 512
    places = (nodes // BLOCK, BLOCK)
    return call(
        functools.partial(to_grid_kernel, at),
        after,
        params=pltpu.CompilerParams(vmem_limit_bytes=(60 if at == 0 else 32) * 1024 * 1024),
        into=[(1, so_far)] if at else [],
        grid=(nodes // rows,),
        in_specs=[pl.BlockSpec(memory_space=pltpu.HBM)] * 2,
        out_specs=[pl.BlockSpec((rows, width), lambda i: (i, 0)), pl.BlockSpec((rows, width), lambda i: (i, at))],
        out_shape=[
            jax.ShapeDtypeStruct((nodes, width), jnp.float32),
            jax.ShapeDtypeStruct((nodes, states), jnp.float32),
        ],
        scratch_shapes=[pltpu.VMEM(places, jnp.int32), pltpu.VMEM((nodes, width), jnp.float32)]
        + [pltpu.VMEM((nodes, width), jnp.bfloat16)] * 2
        + [pltpu.SemaphoreType.DMA((2,))],
        name="to_grid",
    )(face_map.reshape(places), x)


def from_grid_kernel(map_ref, *refs):
    pieces, refs = refs[:-7], refs[-7:]
    out_ref, again_ref, half_ref, turned_high, turned_low, high_ref, low_ref = refs
    step = pl.program_id(0)

    @pl.when(step == 0)
    def _():
        split_columns([[x] for x in pieces], high_ref, low_ref, 0)

    rows, nodes = out_ref.shape[0], high_ref.shape[0]
    node = lax.broadcasted_iota(jnp.int32, (rows, nodes), 0) + step * rows
    pick = jnp.where(node == map_ref[...], 1.0, 0.0).astype(jnp.bfloat16)
    out_ref[...] = dot(pick, high_ref[...]) + dot(pick, low_ref[...])
    here = pl.ds(pl.multiple_of(step * rows, rows), rows)
    again = jnp.concatenate([x[here, :] for x in pieces], axis=1)
    again_ref[...] = again
    half_ref[...] = again[:, half_ref.shape[1] :]
    turned_high[...], turned_low[...] = halves(again.T)


def from_grid(face_map, pieces, after=(), passed=()):
    nodes = pieces[0].shape[0]
    states = sum(x.shape[1] for x in pieces)
    rows = 256
    part = pl.BlockSpec((rows, states), lambda i: (i, 0))
    turned = pl.BlockSpec((states, rows), lambda i: (0, i))
    sizes = (states, states, states // 2)
    return call(
        from_grid_kernel,
        after,
        passed=passed,
        grid=(nodes // rows,),
        in_specs=[pl.BlockSpec((1, nodes), lambda i: (0, 0))]
        + [pl.BlockSpec(x.shape, lambda i: (0, 0)) for x in pieces],
        out_specs=[part, part, pl.BlockSpec((rows, states // 2), lambda i: (i, 0)), turned, turned],
        out_shape=[jax.ShapeDtypeStruct((nodes, size), jnp.float32) for size in sizes]
        + [jax.ShapeDtypeStruct((states, nodes), jnp.bfloat16)] * 2,
        scratch_shapes=[pltpu.VMEM((nodes, states), jnp.bfloat16)] * 2,
        name="from_grid",
    )(face_map.reshape(1, nodes), *pieces)


def plane_terms(shifted, stiff, layer):
    terms = []
    for dj, dk in OFFSETS:
        total = None
        for b in (0, 1):
            for c in (0, 1):
                if b + dj in (0, 1) and c + dk in (0, 1):
                    weight = float(stiff[2 * b + c, 4 * layer + 2 * (b + dj) + c + dk])
                    term = weight * shifted[b][c]
                    total = term if total is None else total + term
        terms.append(total)
    return terms


def write_terms(stiff, odd, own_ref, before_ref, potential_ref, terms_ref):
    nodes = own_ref.shape[1]
    column = lax.broadcasted_iota(jnp.int32, (8, nodes), 1) & (SIDE - 1)
    here, layers = None, []
    for ref in (own_ref, before_ref):
        scale = jnp.broadcast_to(0.5 * ref[...], (8, nodes))
        back = jnp.where(column == 0, pltpu.roll(scale, nodes - SIDE + 1, 1), pltpu.roll(scale, 1, 1))
        shifted = [[x, pltpu.roll(x, SIDE, 1)] for x in (scale, back)]
        shifted = [[shifted[c][b] for c in (0, 1)] for b in (0, 1)]
        mine = plane_terms(shifted, stiff, 0)
        here = mine if here is None else [a + b for a, b in zip(here, mine)]
        layers.append(plane_terms(shifted, stiff, 1))
    here[4] = here[4] + potential_ref[...]
    after, back = layers
    paired = [jnp.where(odd, b, a) for a, b in zip(after, back)]
    far = [jnp.where(odd, a, b) for a, b in zip(after, back)]
    for at, term in enumerate(here + paired + far):
        terms_ref[at : at + 1, :] = term[:1]


def write_bands(terms, out_ref):
    row = lax.broadcasted_iota(jnp.int32, (SIDE, BLOCK), 0)
    lane = lax.broadcasted_iota(jnp.int32, (SIDE, BLOCK), 1)
    turn = (lane - row) & (SIDE - 1)
    for line in range(BLOCK // SIDE):
        rows = slice(line * SIDE, (line + 1) * SIDE)
        rest = slice(BLOCK + rows.start, BLOCK + rows.stop)
        masks = {}
        for dj, dk in OFFSETS:
            tile, group = divmod(line + MARGIN // SIDE + dj, BLOCK // SIDE)
            masks[dj, dk] = tile, (turn == dk % SIDE) & ((lane >> 5) == group)
        for plane in range(3):
            totals = [jnp.zeros((SIDE, BLOCK), jnp.float32) for _ in range(WINDOW // BLOCK)]
            for at, offset in enumerate(OFFSETS):
                term = terms[rows, plane * 9 + at : plane * 9 + at + 1]
                tile, mask = masks[offset]
                totals[tile] = jnp.where(mask, term, totals[tile])
            for tile, total in enumerate(totals):
                columns = slice(tile * BLOCK, (tile + 1) * BLOCK)
                out_ref[plane, 0, rows, columns], out_ref[plane, 0, rest, columns] = halves(total)


def prepare_kernel(stiff, odd_ref, own_ref, before_ref, potential_ref, map_ref, prev_ref, *refs):
    band_ref, last_ref, terms_ref, high_ref, low_ref = refs
    step = pl.program_id(0)
    nodes = prev_ref.shape[0]

    @pl.when(step == 0)
    def _():
        write_terms(stiff, odd_ref[0] == 1, own_ref, before_ref, potential_ref, terms_ref)
        split_columns([[prev_ref]], high_ref, low_ref, 0)

    write_bands(terms_ref[:, pl.ds(pl.multiple_of(step * BLOCK, BLOCK), BLOCK)].T, band_ref)
    place = lax.broadcasted_iota(jnp.int32, (BLOCK, nodes), 1)
    column = jnp.broadcast_to(map_ref[pl.ds(step, 1), :], (BLOCK, BLOCK)).T
    column = jnp.concatenate([column] * (nodes // BLOCK), axis=1)
    pick = jnp.where(place == column, 1.0, 0.0).astype(jnp.bfloat16)
    last_ref[...] = dot(pick, high_ref[...]) + dot(pick, low_ref[...])


def prepare(stiff, odd, own, before, potential, face_map, y_prev, after):
    nodes, states = y_prev.shape
    row = pl.BlockSpec((1, nodes), lambda i: (0, 0))
    return call(
        functools.partial(prepare_kernel, stiff),
        after,
        grid=(nodes // BLOCK,),
        in_specs=[pl.BlockSpec(memory_space=pltpu.SMEM), row, row, row]
        + [pl.BlockSpec((nodes // BLOCK, BLOCK), lambda i: (0, 0))]
        + [pl.BlockSpec((nodes, states), lambda i: (0, 0))],
        out_specs=[
            pl.BlockSpec((3, 1, 2 * BLOCK, WINDOW), lambda i: (0, i, 0, 0)),
            pl.BlockSpec((BLOCK, states), lambda i: (i, 0)),
        ],
        out_shape=[
            jax.ShapeDtypeStruct((3, nodes // BLOCK, 2 * BLOCK, WINDOW), jnp.bfloat16),
            jax.ShapeDtypeStruct((nodes, states), jnp.float32),
        ],
        scratch_shapes=[pltpu.VMEM((32, nodes), jnp.float32)]
        + [pltpu.VMEM((nodes, states), jnp.bfloat16)] * 2,
        name="prepare",
    )(
        odd,
        *[x.reshape(1, nodes) for x in (own, before, potential)],
        face_map.reshape(nodes // BLOCK, BLOCK),
        y_prev,
    )


def fill(wide, plane, ref, start, width):
    nodes = ref.shape[0]
    for first, part in zip((start, width + start), halves(ref[...])):
        columns = slice(first, first + part.shape[1])
        wide[plane, pl.ds(MARGIN, nodes), columns] = part
        wide[plane, pl.ds(0, MARGIN), columns] = part[nodes - MARGIN :]
        wide[plane, pl.ds(MARGIN + nodes, MARGIN), columns] = part[:MARGIN]


def applied_rows(band_ref, at, wide, first):
    total = None
    for plane in range(band_ref.shape[0]):
        term = dot(band_ref[plane, at], wide[plane, pl.ds(first, WINDOW), :])
        total = term if total is None else total + term
    total = total[:BLOCK] + total[BLOCK:]
    width = total.shape[1] // 2
    return total[:, :width] + total[:, width:]


def on_chip_kernel(filtered, band_ref, own_ref, paired_ref, *refs):
    last_ref, (out_ref, wide) = refs[0], refs[-2:]
    step = pl.program_id(0)
    width = own_ref.shape[1]

    @pl.when(step == 0)
    def _():
        for plane, ref in enumerate((own_ref, paired_ref)):
            fill(wide, plane, ref, 0, width)

    per_step = band_ref.shape[1]
    for at in range(per_step):
        first = pl.multiple_of((step * per_step + at) * BLOCK, BLOCK)
        total = applied_rows(band_ref, at, wide, first)
        rows = pl.ds(at * BLOCK, BLOCK)
        if filtered:
            total = (2.0 / half_width) * (total - centre * own_ref[pl.ds(first, BLOCK), :]) - last_ref[rows, :]
        out_ref[rows, :] = total


def across_kernel(filtered, pieces, band_ref, part_ref, *refs):
    far_refs, outs, wide = refs[:pieces], refs[pieces:-1], refs[-1]
    step = pl.program_id(0)
    width = part_ref.shape[1]

    @pl.when(step == 0)
    def _():
        for at, ref in enumerate(far_refs):
            fill(wide, 0, ref, at * width // pieces, width)

    per_step = band_ref.shape[1]
    for at in range(per_step):
        first = pl.multiple_of((step * per_step + at) * BLOCK, BLOCK)
        total = applied_rows(band_ref, at, wide, first)
        rows = pl.ds(at * BLOCK, BLOCK)
        if filtered:
            outs[0][rows, :] = part_ref[rows, :] + (2.0 / half_width) * total
        else:
            outs[0][:, rows], outs[1][:, rows] = halves((part_ref[rows, :] + total).T)


PER_STEP = 2


def on_chip(band, own, paired, last, first=0, width=None, after=()):
    nodes, states = own.shape
    rows, width = PER_STEP * BLOCK, width or states
    at = first // width
    column = pl.BlockSpec((nodes, width), lambda i: (0, at))
    part = pl.BlockSpec((rows, width), lambda i: (i, at))
    return call(
        functools.partial(on_chip_kernel, last is not None),
        after,
        grid=(nodes // rows,),
        in_specs=[pl.BlockSpec((2, PER_STEP, 2 * BLOCK, WINDOW), lambda i: (0, i, 0, 0)), column, column]
        + [part] * (last is not None),
        out_specs=pl.BlockSpec((rows, width), lambda i: (i, 0)),
        out_shape=jax.ShapeDtypeStruct((nodes, width), jnp.float32),
        scratch_shapes=[pltpu.VMEM((2, nodes + 2 * MARGIN, 2 * width), jnp.bfloat16)],
        name="on_chip",
    )(band, own, paired, *([] if last is None else [last]))


def across_specs(nodes, width):
    rows = PER_STEP * BLOCK
    return dict(
        grid=(nodes // rows,),
        scratch_shapes=[pltpu.VMEM((1, nodes + 2 * MARGIN, 2 * width), jnp.bfloat16)],
        name="across",
    ), pl.BlockSpec((1, PER_STEP, 2 * BLOCK, WINDOW), lambda i: (2, i, 0, 0))


def next_degree(band, terms, far, after):
    nodes, width = far.shape
    rows = PER_STEP * BLOCK
    options, band_spec = across_specs(nodes, width)
    part = pl.BlockSpec((rows, width), lambda i: (i, 0))
    return call(
        functools.partial(across_kernel, True, 1),
        after,
        in_specs=[band_spec, part, pl.BlockSpec((nodes, width), lambda i: (0, 0))],
        out_specs=part,
        out_shape=jax.ShapeDtypeStruct((nodes, width), jnp.float32),
        **options,
    )(band, terms, far)


def applied_next(band, terms, far, after=()):
    nodes, states = terms.shape
    rows = PER_STEP * BLOCK
    options, band_spec = across_specs(nodes, states)
    turned = pl.BlockSpec((states, rows), lambda i: (0, i))
    turned_shape = jax.ShapeDtypeStruct((states, nodes), jnp.bfloat16)
    return call(
        functools.partial(across_kernel, False, len(far)),
        after,
        in_specs=[band_spec, pl.BlockSpec((rows, states), lambda i: (i, 0))]
        + [pl.BlockSpec(x.shape, lambda i: (0, 0)) for x in far],
        out_specs=[turned, turned],
        out_shape=[turned_shape, turned_shape],
        **options,
    )(band, terms, *far)


def split_columns(pieces, high_ref, low_ref, first):
    for group in pieces:
        piece = group[0][...]
        for other in group[1:]:
            piece = piece + other[...]
        columns = slice(first, first + piece.shape[1])
        first += piece.shape[1]
        high_ref[:, columns], low_ref[:, columns] = halves(piece)


def rows_product(left_high, left_low, high_ref, low_ref):
    total = dot(left_high[...], high_ref[...]) + dot(left_high[...], low_ref[...])
    return total + dot(left_low[...], high_ref[...])


def sorted_kernel(count, keep_ref, left_high, left_low, *refs):
    own, first = [[x] for x in refs[:count]], [[x] for x in refs[count:-4]]
    kept_ref, sent_ref, high_ref, low_ref = refs[-4:]
    width = kept_ref.shape[1]

    @pl.when((pl.program_id(0) == 0) & (keep_ref[0] == 1))
    def _():
        split_columns(own, high_ref, low_ref, 0)
        split_columns(first, high_ref, low_ref, width)

    @pl.when((pl.program_id(0) == 0) & (keep_ref[0] != 1))
    def _():
        split_columns(own, high_ref, low_ref, width)
        split_columns(first, high_ref, low_ref, 0)

    total = rows_product(left_high, left_low, high_ref, low_ref)
    kept_ref[...] = total[:, :width]
    sent_ref[...] = total[:, width:]


def sorted_products(keep, turned, own, first, at, so_far, after=(), passed=()):
    states, nodes = turned[0].shape
    rows = 256
    steps = states // rows
    width = sum(piece.shape[1] for piece in own)
    left = pl.BlockSpec((rows, nodes), lambda i: (i, 0))
    out = pl.BlockSpec((rows, width), lambda i: (i + at * steps, 0))
    shape = jax.ShapeDtypeStruct((2 * states, width), jnp.float32)
    return call(
        functools.partial(sorted_kernel, len(own)),
        after,
        into=list(enumerate(so_far)) if at else [],
        passed=passed,
        grid=(steps,),
        in_specs=[pl.BlockSpec(memory_space=pltpu.SMEM), left, left]
        + [pl.BlockSpec(piece.shape, lambda i: (0, 0)) for piece in (*own, *first)],
        out_specs=[out, out],
        out_shape=[shape, shape],
        scratch_shapes=[pltpu.VMEM((nodes, 2 * width), jnp.bfloat16)] * 2,
        name="sorted_products",
    )(keep, *turned, *own, *first)


def both_kernel(summed, left_high, left_low, more_high, more_low, *refs):
    pieces, (out_ref, high_ref, low_ref) = refs[:-3], refs[-3:]
    step, half = pl.program_id(0), pl.num_programs(0) // 2

    @pl.when(step == 0)
    def _():
        groups = [pieces[at : at + summed] for at in range(0, len(pieces), summed)]
        split_columns(groups, high_ref, low_ref, 0)

    @pl.when(step < half)
    def _():
        out_ref[...] = rows_product(left_high, left_low, high_ref, low_ref)

    @pl.when(step >= half)
    def _():
        out_ref[...] = rows_product(more_high, more_low, high_ref, low_ref)


def both_products(y_turned, h_turned, pieces, summed=1, after=(), passed=()):
    states, nodes = y_turned[0].shape
    rows = 256
    steps = states // rows
    width = sum(piece.shape[1] for piece in pieces) // summed
    first = pl.BlockSpec((rows, nodes), lambda i: (jnp.minimum(i, steps - 1), 0))
    second = pl.BlockSpec((rows, nodes), lambda i: (jnp.maximum(i - steps, 0), 0))
    return call(
        functools.partial(both_kernel, summed),
        after,
        grid=(2 * steps,),
        in_specs=[first, first, second, second]
        + [pl.BlockSpec(piece.shape, lambda i: (0, 0)) for piece in pieces],
        out_specs=[pl.BlockSpec((rows, width), lambda i: (i, 0))],
        out_shape=[jax.ShapeDtypeStruct((2 * states, width), jnp.float32)],
        passed=passed,
        scratch_shapes=[pltpu.VMEM((nodes, width), jnp.bfloat16)] * 2,
        name="both_products",
    )(*y_turned, *h_turned, *pieces)


def pair_kernel(keep_ref, left_high, left_low, more_high, more_low, block_ref, piece_ref, other_ref, *refs):
    kept_ref, sent_ref, high_ref, low_ref = refs
    step, half = pl.program_id(0), pl.num_programs(0) // 2

    @pl.when(step == 0)
    def _():
        split_columns([[piece_ref, other_ref]], high_ref, low_ref, 0)

    def write(total):
        keeps = keep_ref[0] == 1
        kept_ref[...] = jnp.where(keeps, block_ref[...], total)
        sent_ref[...] = jnp.where(keeps, total, block_ref[...])

    @pl.when(step < half)
    def _():
        write(rows_product(left_high, left_low, high_ref, low_ref))

    @pl.when(step >= half)
    def _():
        write(rows_product(more_high, more_low, high_ref, low_ref))


def pair_products(keep, y_turned, h_turned, block, piece, other, after):
    states, nodes = y_turned[0].shape
    rows = 256
    steps = states // rows
    width = piece.shape[1]
    first = pl.BlockSpec((rows, nodes), lambda i: (jnp.minimum(i, steps - 1), 0))
    second = pl.BlockSpec((rows, nodes), lambda i: (jnp.maximum(i - steps, 0), 0))
    whole = pl.BlockSpec((nodes, width), lambda i: (0, 0))
    out = pl.BlockSpec((rows, width), lambda i: (i, 0))
    return call(
        pair_kernel,
        after,
        grid=(2 * steps,),
        in_specs=[pl.BlockSpec(memory_space=pltpu.SMEM), first, first, second, second, out, whole, whole],
        out_specs=[out, out],
        out_shape=[jax.ShapeDtypeStruct((2 * states, width), jnp.float32)] * 2,
        scratch_shapes=[pltpu.VMEM((nodes, width), jnp.bfloat16)] * 2,
        name="pair_products",
    )(keep, *y_turned, *h_turned, block, piece, other)


def near_kernel(flags_ref, mine_ref, arrived_ref, out_ref):
    out_ref[...] = jnp.where(flags_ref[0] == 1, 1.0, 0.0) * (mine_ref[...] + arrived_ref[...])


def near_rows(flags, mine, arrived, after):
    whole = pl.BlockSpec(mine.shape, lambda i: (0, 0))
    return call(
        near_kernel,
        after,
        grid=(1,),
        in_specs=[pl.BlockSpec(memory_space=pltpu.SMEM), whole, whole],
        out_specs=whole,
        out_shape=jax.ShapeDtypeStruct(mine.shape, jnp.float32),
        name="near_rows",
    )(flags, mine, arrived)


def mark(after):
    shape = jax.ShapeDtypeStruct((8, 128), jnp.float32)

    def kernel(out_ref):
        out_ref[...] = jnp.zeros_like(out_ref)

    return call(kernel, after, in_specs=[], grid=(1,), out_specs=corner(shape), out_shape=shape, name="mark")()


def most_kernel(weight, flags_ref, base_ref, one_ref, one_far, two_ref, two_far, *refs):
    third_refs, outs, rest_ref = refs[:-3], refs[-3:-1], refs[-1]
    one, two = [jnp.where(flags_ref[band] == 1, 1.0, 0.0) for band in (1, 2)]
    states, width = outs[0].shape
    for half, out_ref in enumerate(outs):
        rows = slice(half * states, (half + 1) * states)
        total = base_ref[rows, :width] + one * (one_ref[rows, :] + one_far[rows, :])
        pair = two_ref[rows, :] + two_far[rows, :]
        out_ref[...] = weight * (total + two * pair)
        rest = base_ref[rows, width:] + one * pair
        third = jnp.concatenate([x[rows, :] for x in third_refs], axis=1)
        rest_ref[rows, :] = weight * (rest + two * third)


def finish_most(weight, flags, base, one, one_far, two, two_far, *third):
    rows, width = one.shape
    states = rows // 2
    whole = pl.BlockSpec((rows, width), lambda i: (0, 0))
    shape = jax.ShapeDtypeStruct((states, base.shape[1]), jnp.float32)
    return call(
        functools.partial(most_kernel, weight),
        (),
        grid=(1,),
        in_specs=[pl.BlockSpec(memory_space=pltpu.SMEM), pl.BlockSpec(base.shape, lambda i: (0, 0))]
        + [whole] * 4
        + [pl.BlockSpec(x.shape, lambda i: (0, 0)) for x in third],
        out_specs=[pl.BlockSpec((states, width), lambda i: (0, 0))] * 2 + [whole],
        out_shape=[shape, shape, jax.ShapeDtypeStruct((rows, width), jnp.float32)],
        name="finish_most",
    )(flags, base, one, one_far, two, two_far, *third)


def finish_kernel(weight, upper_ref, lower_ref, *refs):
    far_refs, outs = refs[:-2], refs[-2:]
    far_refs = far_refs[: len(far_refs) // 2], far_refs[len(far_refs) // 2 :]
    for rest_ref, far, out_ref in zip((upper_ref, lower_ref), far_refs, outs):
        arrived = jnp.concatenate([x[...] for x in far], axis=1)
        out_ref[...] = rest_ref[...] + weight * arrived


def finish(weight, outs, rest, far):
    states, width = outs[0].shape
    steps, half = 2, width // 2
    rows = states // steps
    upper = lambda size: pl.BlockSpec((rows, size), lambda i: (i, 0))
    lower = lambda size: pl.BlockSpec((rows, size), lambda i: (i + steps, 0))
    return call(
        functools.partial(finish_kernel, weight),
        (),
        into=list(enumerate(outs)),
        grid=(steps,),
        in_specs=[upper(half), lower(half)]
        + [upper(x.shape[1]) for x in far]
        + [lower(x.shape[1]) for x in far],
        out_specs=[pl.BlockSpec((rows, half), lambda i: (i, 1))] * 2,
        out_shape=[jax.ShapeDtypeStruct((states, width), jnp.float32)] * 2,
        name="finish",
    )(rest, rest, *far, *far)


def exchange(block, axis, pairs):
    return lax.ppermute(block, axis, pairs + [(b, a) for a, b in pairs])


def paired(block):
    return exchange(block, "dom", [(i, i + 1) for i in range(0, lax.axis_size("dom"), 2)])


def crossed(block):
    size = lax.axis_size("dom")
    return exchange(block, "dom", [(i, (i + 1) % size) for i in range(1, size, 2)])


def to_owner(block, owners, step):
    size = len(owners)
    route = []
    for band, owner in enumerate(owners):
        for to in (owner, owner ^ 2) if step == 1 else (owner,):
            route.append(((to ^ step) * size + band, to * size + band))
    return lax.ppermute(block, ("dom", "band"), route)


def on_device(y_cur, y_prev, connect, face_map, elem_scale, potential):
    stiff = element_table()
    nodes, states = y_cur.shape
    domains, band_count = lax.axis_size("dom"), lax.axis_size("band")
    me, level = lax.axis_index("dom"), lax.axis_index("band")
    swaps = domains == 4 and band_count == 4 and states == STATES_DEV
    half = states // 2
    place = jnp.arange(nodes, dtype=jnp.int32)
    cell_place = connect[:, 4] - nodes
    own = jnp.sum(jnp.where(cell_place[:, None] == place[None, :], elem_scale[:, None], 0.0), axis=0)
    before = lax.ppermute(own, "dom", [(i, (i + 1) % domains) for i in range(domains)])
    at_grid = jnp.sum(jnp.where(place[:, None] == face_map[None, :], potential[:, None], 0.0), axis=0)
    odd = (me % 2).astype(jnp.int32).reshape(1)
    weight = 1.0 / (nodes * domains)

    far, current, waited = [], None, ()
    for at in (0, 1):
        chunk, current = to_grid(face_map, y_cur, at, half, current, waited)
        far.append(crossed(chunk))
        waited = (chunk,)
    current_paired = paired(current)
    band, last = prepare(stiff, odd, own, before, at_grid, face_map, y_prev, (current,))

    following = []
    for at, piece in enumerate(far):
        terms = on_chip(band, current, current_paired, last, at * half, half, following)
        following.append(next_degree(band, terms, piece, ()))
    next_far = [crossed(following[0])]

    if not swaps:
        y_next, whole, other, *y_turned = from_grid(face_map, following)
        next_far.append(crossed(other))
        h_turned = applied_next(band, on_chip(band, whole, paired(whole), None), next_far)
        piece = lax.all_gather(whole, "band", axis=1, tiled=True)
        (block,) = both_products(y_turned, h_turned, [piece])
        parts = [
            weight * lax.psum_scatter(rows, "dom", scatter_dimension=1, tiled=True)
            for rows in (block[:states], block[states:])
        ]
        return (y_next, *parts)

    outward = [(2, 3), (1, 0)]
    core, chip, upper = me % 2, me // 2, level // 2
    keep = jnp.where(core == level % 2, 1, 0).astype(jnp.int32).reshape(1)
    near_route = [
        (((b // 2 * 2 + c) ^ 2) * 4 + b, (b // 2 * 2 + c) * 4 + b) for b in range(4) for c in (0, 1)
    ]
    near_across = lambda x: lax.ppermute(x, ("dom", "band"), near_route)
    second_owner, third_owner = [2, 2, 1, 1], [3, 3, 0, 0]

    ends, middle = [(0, 1), (2, 3)], [(1, 2)]
    first = [exchange(x, "band", ends) for x in following]
    second_middle = [exchange(x, "band", middle) for x in following]
    waited = (first[0], next_far[0])
    y_next, whole, other, *y_turned, second_middle[0] = from_grid(face_map, following, waited, second_middle[:1])
    next_far.append(crossed(other))
    second_out = [lax.ppermute(second_middle[0], "band", outward)]
    whole_paired = paired(whole)
    (first[0],) = gate(first[:1], (mark((y_next,)), whole_paired, second_middle[1]))
    third_middle = [exchange(first[0], "band", middle)]
    *near, second_middle[1] = sorted_products(keep, y_turned, following, first, 0, (), (), second_middle[1:])
    second_out.append(lax.ppermute(second_middle[1], "band", outward))
    h_turned = applied_next(band, on_chip(band, whole, whole_paired, None, after=near[:1]), next_far)
    (first[1],) = gate(first[1:], (h_turned[0], third_middle[0]))
    third_middle.append(exchange(first[1], "band", middle))
    kept, sent, third_middle[0] = sorted_products(keep, h_turned, following, first, 1, near, (), third_middle[:1])
    third_out = [lax.ppermute(third_middle[0], "band", outward)]
    sent = paired(sent)

    blocks = [*both_products(y_turned, h_turned, [second_middle[0], second_out[0]], 2, (kept,))]
    cores = [to_owner(blocks[0], second_owner, 1)]
    (near,) = plus(kept, sent, (blocks[0],))
    near_far = near_across(near)
    pieces = [second_middle[1], second_out[1]]
    block, third_middle[1] = both_products(y_turned, h_turned, pieces, 2, (near,), third_middle[1:])
    blocks.append(block)
    tails = [third_middle[1][:, : half // 2], third_middle[1][:, half // 2 :]]
    (second,) = plus(blocks[0], cores[0], (blocks[1],))
    second_far = to_owner(second, second_owner, 2)
    tails_out = [lax.ppermute(tails[0], "band", outward)]
    keep = jnp.where(core == upper, 1, 0).astype(jnp.int32).reshape(1)
    pieces = (blocks[1], third_middle[0], third_out[0])
    kept, sent = pair_products(keep, y_turned, h_turned, *pieces, (second,))
    sent = paired(sent)
    (tails[1],) = gate(tails[1:], (kept, second_far))
    tails_out.append(lax.ppermute(tails[1], "band", outward))
    (pair,) = plus(kept, sent, tails[1:])
    pair_route = [
        (((2 - b // 2 * 2 + c) ^ 2) * 4 + b, (2 - b // 2 * 2 + c) * 4 + b) for b in range(4) for c in (0, 1)
    ]
    pair_far = lax.ppermute(pair, ("dom", "band"), pair_route)
    blocks, waited = [], (pair,)
    for piece in zip(tails, tails_out):
        blocks += both_products(y_turned, h_turned, list(piece), 2, waited)
        waited = blocks[-1:]
    cores = [to_owner(block, third_owner, 1) for block in blocks]
    third = [*plus(blocks[0], cores[0], blocks[1:])]
    third += plus(blocks[1], cores[1], third)
    third_far = [to_owner(block, third_owner, 2) for block in third]
    is_near, is_second = chip == upper, core == upper
    flags = jnp.stack([is_near, ~is_near & is_second, ~is_near & ~is_second]).astype(jnp.int32)
    base = near_rows(flags, near, near_far, (third[1],))
    *outs, rest = finish_most(weight, flags, base, second, second_far, pair, pair_far, *third)
    return (y_next, *finish(weight, outs, rest, third_far))


def solution(mesh):
    placed = (
        P(("image", "dom"), "band"),
        P(("image", "dom"), "band"),
        P("dom", None),
        P("dom"),
        P("dom"),
        P(("image", "dom")),
    )
    return jax.shard_map(
        on_device,
        mesh=mesh,
        in_specs=placed,
        out_specs=(
            P(("image", "dom"), "band"),
            P(("image", "band"), "dom"),
            P(("image", "band"), "dom"),
        ),
        check_vma=False,
    )
```

```python
import functools

import jax
import jax.numpy as jnp
import numpy as np
from jax import lax
from jax.experimental import pallas as pl
from jax.experimental.pallas import tpu as pltpu
from jax.sharding import PartitionSpec as P

SIDE = 32
STATES_DEV = 512
BLOCK = 128
WINDOW = 256
MARGIN = (WINDOW - BLOCK) // 2

cheb_low = 1.0
cheb_high = 9.0
centre = 0.5 * (cheb_high + cheb_low)
half_width = 0.5 * (cheb_high - cheb_low)

OFFSETS = [(dj, dk) for dj in (-1, 0, 1) for dk in (-1, 0, 1)]
PARAMS = pltpu.CompilerParams(vmem_limit_bytes=32 * 1024 * 1024)


COST = pl.CostEstimate(flops=10**12, bytes_accessed=1, transcendentals=0)


def element_table():
    stiff_line = np.array([[1.0, -1.0], [-1.0, 1.0]])
    mass_line = np.array([[1.0 / 3.0, 1.0 / 6.0], [1.0 / 6.0, 1.0 / 3.0]])
    total = np.kron(stiff_line, np.kron(mass_line, mass_line))
    total = total + np.kron(mass_line, np.kron(stiff_line, mass_line))
    total = total + np.kron(mass_line, np.kron(mass_line, stiff_line))
    return total.astype(np.float32)


def halves(x):
    high = x.astype(jnp.bfloat16)
    low = (x - high.astype(jnp.float32)).astype(jnp.bfloat16)
    return high, low


def dot(a, b):
    return lax.dot_general(a, b, (((1,), (0,)), ((), ())), preferred_element_type=jnp.float32)


def corner(x):
    rows = 32 // x.dtype.itemsize
    return pl.BlockSpec((rows, 128), lambda *_: (0, 0))


def call(kernel, after, *, in_specs, out_specs, out_shape, name, into=(), passed=(), params=None, **options):
    count = len(in_specs)
    extra = [*[array for _, array in into], *after, *passed]
    aliases = {count + at: out for at, (out, _) in enumerate(into)}
    outs = len(out_shape) if isinstance(out_shape, (list, tuple)) else 1
    if passed:
        out_specs = [*out_specs, *map(corner, passed)]
        out_shape = [*out_shape, *[jax.ShapeDtypeStruct(x.shape, x.dtype) for x in passed]]
        aliases |= {count + len(extra) - len(passed) + at: outs + at for at in range(len(passed))}

    def body(*refs):
        rest = refs[count + len(extra) :]
        kernel(*refs[:count], *rest[:outs], *rest[outs + len(passed) :])
        first = count + len(extra) - len(passed)
        for x_ref, out_ref in zip(refs[first : first + len(passed)], rest[outs : outs + len(passed)]):
            out_ref[...] = x_ref[...]

    made = pl.pallas_call(
        body,
        in_specs=[*in_specs, *map(corner, extra)],
        out_specs=out_specs,
        out_shape=out_shape,
        input_output_aliases=aliases,
        compiler_params=params or PARAMS,
        cost_estimate=COST,
        name=name,
        **options,
    )
    return lambda *args: made(*args, *extra)


def gate(arrays, after):
    return call(lambda: None, after, passed=arrays, grid=(1,), in_specs=[], out_specs=[], out_shape=[], name="gate")()


def plus_kernel(left_ref, right_ref, out_ref):
    out_ref[...] = left_ref[...] + right_ref[...]


def plus(left, right, after, passed=()):
    rows = min(512, left.shape[0])
    part = pl.BlockSpec((rows, left.shape[1]), lambda i: (i, 0))
    return call(
        plus_kernel,
        after,
        grid=(left.shape[0] // rows,),
        in_specs=[part, part],
        out_specs=[part],
        out_shape=[jax.ShapeDtypeStruct(left.shape, left.dtype)],
        passed=passed,
        name="plus",
    )(left, right)


def to_grid_kernel(at, map_hbm, x_hbm, out_ref, whole_ref, map_ref, x_ref, high_ref, low_ref, sems):
    step = pl.program_id(0)
    width = x_ref.shape[1]

    @pl.when(step == 0)
    def _():
        copies = [
            pltpu.make_async_copy(x_hbm.at[:, pl.ds(at * width, width)], x_ref, sems.at[0]),
            pltpu.make_async_copy(map_hbm, map_ref, sems.at[1]),
        ]
        for copy in copies:
            copy.start()
        for copy in copies:
            copy.wait()
        high_ref[...], low_ref[...] = halves(x_ref[...])

    rows, nodes = out_ref.shape[0], x_ref.shape[0]
    place = lax.broadcasted_iota(jnp.int32, (BLOCK, nodes), 1)
    for part in range(rows // BLOCK):
        row = map_ref[pl.ds(step * (rows // BLOCK) + part, 1), :]
        column = jnp.broadcast_to(row, (BLOCK, BLOCK)).T
        column = jnp.concatenate([column] * (nodes // BLOCK), axis=1)
        pick = jnp.where(place == column, 1.0, 0.0).astype(jnp.bfloat16)
        moved = dot(pick, high_ref[...]) + dot(pick, low_ref[...])
        out = slice(part * BLOCK, (part + 1) * BLOCK)
        out_ref[out, :] = moved
        whole_ref[out, :] = moved


def to_grid(face_map, x, at, width, so_far, after):
    nodes, states = x.shape
    rows = 512
    places = (nodes // BLOCK, BLOCK)
    return call(
        functools.partial(to_grid_kernel, at),
        after,
        params=pltpu.CompilerParams(vmem_limit_bytes=(60 if at == 0 else 32) * 1024 * 1024),
        into=[(1, so_far)] if at else [],
        grid=(nodes // rows,),
        in_specs=[pl.BlockSpec(memory_space=pltpu.HBM)] * 2,
        out_specs=[pl.BlockSpec((rows, width), lambda i: (i, 0)), pl.BlockSpec((rows, width), lambda i: (i, at))],
        out_shape=[
            jax.ShapeDtypeStruct((nodes, width), jnp.float32),
            jax.ShapeDtypeStruct((nodes, states), jnp.float32),
        ],
        scratch_shapes=[pltpu.VMEM(places, jnp.int32), pltpu.VMEM((nodes, width), jnp.float32)]
        + [pltpu.VMEM((nodes, width), jnp.bfloat16)] * 2
        + [pltpu.SemaphoreType.DMA((2,))],
        name="to_grid",
    )(face_map.reshape(places), x)


def from_grid_kernel(map_ref, *refs):
    pieces, refs = refs[:-7], refs[-7:]
    out_ref, again_ref, half_ref, turned_high, turned_low, high_ref, low_ref = refs
    step = pl.program_id(0)

    @pl.when(step == 0)
    def _():
        split_columns([[x] for x in pieces], high_ref, low_ref, 0)

    rows, nodes = out_ref.shape[0], high_ref.shape[0]
    node = lax.broadcasted_iota(jnp.int32, (rows, nodes), 0) + step * rows
    pick = jnp.where(node == map_ref[...], 1.0, 0.0).astype(jnp.bfloat16)
    out_ref[...] = dot(pick, high_ref[...]) + dot(pick, low_ref[...])
    here = pl.ds(pl.multiple_of(step * rows, rows), rows)
    again = jnp.concatenate([x[here, :] for x in pieces], axis=1)
    again_ref[...] = again
    half_ref[...] = again[:, half_ref.shape[1] :]
    turned_high[...], turned_low[...] = halves(again.T)


def from_grid(face_map, pieces, after=(), passed=()):
    nodes = pieces[0].shape[0]
    states = sum(x.shape[1] for x in pieces)
    rows = 256
    part = pl.BlockSpec((rows, states), lambda i: (i, 0))
    turned = pl.BlockSpec((states, rows), lambda i: (0, i))
    sizes = (states, states, states // 2)
    return call(
        from_grid_kernel,
        after,
        passed=passed,
        grid=(nodes // rows,),
        in_specs=[pl.BlockSpec((1, nodes), lambda i: (0, 0))]
        + [pl.BlockSpec(x.shape, lambda i: (0, 0)) for x in pieces],
        out_specs=[part, part, pl.BlockSpec((rows, states // 2), lambda i: (i, 0)), turned, turned],
        out_shape=[jax.ShapeDtypeStruct((nodes, size), jnp.float32) for size in sizes]
        + [jax.ShapeDtypeStruct((states, nodes), jnp.bfloat16)] * 2,
        scratch_shapes=[pltpu.VMEM((nodes, states), jnp.bfloat16)] * 2,
        name="from_grid",
    )(face_map.reshape(1, nodes), *pieces)


def plane_terms(shifted, stiff, layer):
    terms = []
    for dj, dk in OFFSETS:
        total = None
        for b in (0, 1):
            for c in (0, 1):
                if b + dj in (0, 1) and c + dk in (0, 1):
                    weight = float(stiff[2 * b + c, 4 * layer + 2 * (b + dj) + c + dk])
                    term = weight * shifted[b][c]
                    total = term if total is None else total + term
        terms.append(total)
    return terms


def write_terms(stiff, odd, own_ref, before_ref, potential_ref, terms_ref):
    nodes = own_ref.shape[1]
    column = lax.broadcasted_iota(jnp.int32, (8, nodes), 1) & (SIDE - 1)
    here, layers = None, []
    for ref in (own_ref, before_ref):
        scale = jnp.broadcast_to(0.5 * ref[...], (8, nodes))
        back = jnp.where(column == 0, pltpu.roll(scale, nodes - SIDE + 1, 1), pltpu.roll(scale, 1, 1))
        shifted = [[x, pltpu.roll(x, SIDE, 1)] for x in (scale, back)]
        shifted = [[shifted[c][b] for c in (0, 1)] for b in (0, 1)]
        mine = plane_terms(shifted, stiff, 0)
        here = mine if here is None else [a + b for a, b in zip(here, mine)]
        layers.append(plane_terms(shifted, stiff, 1))
    here[4] = here[4] + potential_ref[...]
    after, back = layers
    paired = [jnp.where(odd, b, a) for a, b in zip(after, back)]
    far = [jnp.where(odd, a, b) for a, b in zip(after, back)]
    for at, term in enumerate(here + paired + far):
        terms_ref[at : at + 1, :] = term[:1]


def write_bands(terms, out_ref):
    row = lax.broadcasted_iota(jnp.int32, (SIDE, BLOCK), 0)
    lane = lax.broadcasted_iota(jnp.int32, (SIDE, BLOCK), 1)
    turn = (lane - row) & (SIDE - 1)
    for line in range(BLOCK // SIDE):
        rows = slice(line * SIDE, (line + 1) * SIDE)
        rest = slice(BLOCK + rows.start, BLOCK + rows.stop)
        masks = {}
        for dj, dk in OFFSETS:
            tile, group = divmod(line + MARGIN // SIDE + dj, BLOCK // SIDE)
            masks[dj, dk] = tile, (turn == dk % SIDE) & ((lane >> 5) == group)
        for plane in range(3):
            totals = [jnp.zeros((SIDE, BLOCK), jnp.float32) for _ in range(WINDOW // BLOCK)]
            for at, offset in enumerate(OFFSETS):
                term = terms[rows, plane * 9 + at : plane * 9 + at + 1]
                tile, mask = masks[offset]
                totals[tile] = jnp.where(mask, term, totals[tile])
            for tile, total in enumerate(totals):
                columns = slice(tile * BLOCK, (tile + 1) * BLOCK)
                out_ref[plane, 0, rows, columns], out_ref[plane, 0, rest, columns] = halves(total)


def prepare_kernel(stiff, odd_ref, own_ref, before_ref, potential_ref, map_ref, prev_ref, *refs):
    band_ref, last_ref, terms_ref, high_ref, low_ref = refs
    step = pl.program_id(0)
    nodes = prev_ref.shape[0]

    @pl.when(step == 0)
    def _():
        write_terms(stiff, odd_ref[0] == 1, own_ref, before_ref, potential_ref, terms_ref)
        split_columns([[prev_ref]], high_ref, low_ref, 0)

    write_bands(terms_ref[:, pl.ds(pl.multiple_of(step * BLOCK, BLOCK), BLOCK)].T, band_ref)
    place = lax.broadcasted_iota(jnp.int32, (BLOCK, nodes), 1)
    column = jnp.broadcast_to(map_ref[pl.ds(step, 1), :], (BLOCK, BLOCK)).T
    column = jnp.concatenate([column] * (nodes // BLOCK), axis=1)
    pick = jnp.where(place == column, 1.0, 0.0).astype(jnp.bfloat16)
    last_ref[...] = dot(pick, high_ref[...]) + dot(pick, low_ref[...])


def prepare(stiff, odd, own, before, potential, face_map, y_prev, after):
    nodes, states = y_prev.shape
    row = pl.BlockSpec((1, nodes), lambda i: (0, 0))
    return call(
        functools.partial(prepare_kernel, stiff),
        after,
        grid=(nodes // BLOCK,),
        in_specs=[pl.BlockSpec(memory_space=pltpu.SMEM), row, row, row]
        + [pl.BlockSpec((nodes // BLOCK, BLOCK), lambda i: (0, 0))]
        + [pl.BlockSpec((nodes, states), lambda i: (0, 0))],
        out_specs=[
            pl.BlockSpec((3, 1, 2 * BLOCK, WINDOW), lambda i: (0, i, 0, 0)),
            pl.BlockSpec((BLOCK, states), lambda i: (i, 0)),
        ],
        out_shape=[
            jax.ShapeDtypeStruct((3, nodes // BLOCK, 2 * BLOCK, WINDOW), jnp.bfloat16),
            jax.ShapeDtypeStruct((nodes, states), jnp.float32),
        ],
        scratch_shapes=[pltpu.VMEM((32, nodes), jnp.float32)]
        + [pltpu.VMEM((nodes, states), jnp.bfloat16)] * 2,
        name="prepare",
    )(
        odd,
        *[x.reshape(1, nodes) for x in (own, before, potential)],
        face_map.reshape(nodes // BLOCK, BLOCK),
        y_prev,
    )


def fill(wide, plane, ref, start, width):
    nodes = ref.shape[0]
    for first, part in zip((start, width + start), halves(ref[...])):
        columns = slice(first, first + part.shape[1])
        wide[plane, pl.ds(MARGIN, nodes), columns] = part
        wide[plane, pl.ds(0, MARGIN), columns] = part[nodes - MARGIN :]
        wide[plane, pl.ds(MARGIN + nodes, MARGIN), columns] = part[:MARGIN]


def applied_rows(band_ref, at, wide, first):
    total = None
    for plane in range(band_ref.shape[0]):
        term = dot(band_ref[plane, at], wide[plane, pl.ds(first, WINDOW), :])
        total = term if total is None else total + term
    total = total[:BLOCK] + total[BLOCK:]
    width = total.shape[1] // 2
    return total[:, :width] + total[:, width:]


def on_chip_kernel(filtered, band_ref, own_ref, paired_ref, *refs):
    last_ref, (out_ref, wide) = refs[0], refs[-2:]
    step = pl.program_id(0)
    width = own_ref.shape[1]

    @pl.when(step == 0)
    def _():
        for plane, ref in enumerate((own_ref, paired_ref)):
            fill(wide, plane, ref, 0, width)

    per_step = band_ref.shape[1]
    for at in range(per_step):
        first = pl.multiple_of((step * per_step + at) * BLOCK, BLOCK)
        total = applied_rows(band_ref, at, wide, first)
        rows = pl.ds(at * BLOCK, BLOCK)
        if filtered:
            total = (2.0 / half_width) * (total - centre * own_ref[pl.ds(first, BLOCK), :]) - last_ref[rows, :]
        out_ref[rows, :] = total


def across_kernel(filtered, pieces, band_ref, part_ref, *refs):
    far_refs, outs, wide = refs[:pieces], refs[pieces:-1], refs[-1]
    step = pl.program_id(0)
    width = part_ref.shape[1]

    @pl.when(step == 0)
    def _():
        for at, ref in enumerate(far_refs):
            fill(wide, 0, ref, at * width // pieces, width)

    per_step = band_ref.shape[1]
    for at in range(per_step):
        first = pl.multiple_of((step * per_step + at) * BLOCK, BLOCK)
        total = applied_rows(band_ref, at, wide, first)
        rows = pl.ds(at * BLOCK, BLOCK)
        if filtered:
            outs[0][rows, :] = part_ref[rows, :] + (2.0 / half_width) * total
        else:
            outs[0][:, rows], outs[1][:, rows] = halves((part_ref[rows, :] + total).T)


PER_STEP = 2


def on_chip(band, own, paired, last, first=0, width=None, after=()):
    nodes, states = own.shape
    rows, width = PER_STEP * BLOCK, width or states
    at = first // width
    column = pl.BlockSpec((nodes, width), lambda i: (0, at))
    part = pl.BlockSpec((rows, width), lambda i: (i, at))
    return call(
        functools.partial(on_chip_kernel, last is not None),
        after,
        grid=(nodes // rows,),
        in_specs=[pl.BlockSpec((2, PER_STEP, 2 * BLOCK, WINDOW), lambda i: (0, i, 0, 0)), column, column]
        + [part] * (last is not None),
        out_specs=pl.BlockSpec((rows, width), lambda i: (i, 0)),
        out_shape=jax.ShapeDtypeStruct((nodes, width), jnp.float32),
        scratch_shapes=[pltpu.VMEM((2, nodes + 2 * MARGIN, 2 * width), jnp.bfloat16)],
        name="on_chip",
    )(band, own, paired, *([] if last is None else [last]))


def across_specs(nodes, width):
    rows = PER_STEP * BLOCK
    return dict(
        grid=(nodes // rows,),
        scratch_shapes=[pltpu.VMEM((1, nodes + 2 * MARGIN, 2 * width), jnp.bfloat16)],
        name="across",
    ), pl.BlockSpec((1, PER_STEP, 2 * BLOCK, WINDOW), lambda i: (2, i, 0, 0))


def next_degree(band, terms, far, after):
    nodes, width = far.shape
    rows = PER_STEP * BLOCK
    options, band_spec = across_specs(nodes, width)
    part = pl.BlockSpec((rows, width), lambda i: (i, 0))
    return call(
        functools.partial(across_kernel, True, 1),
        after,
        in_specs=[band_spec, part, pl.BlockSpec((nodes, width), lambda i: (0, 0))],
        out_specs=part,
        out_shape=jax.ShapeDtypeStruct((nodes, width), jnp.float32),
        **options,
    )(band, terms, far)


def applied_next(band, terms, far, after=()):
    nodes, states = terms.shape
    rows = PER_STEP * BLOCK
    options, band_spec = across_specs(nodes, states)
    turned = pl.BlockSpec((states, rows), lambda i: (0, i))
    turned_shape = jax.ShapeDtypeStruct((states, nodes), jnp.bfloat16)
    return call(
        functools.partial(across_kernel, False, len(far)),
        after,
        in_specs=[band_spec, pl.BlockSpec((rows, states), lambda i: (i, 0))]
        + [pl.BlockSpec(x.shape, lambda i: (0, 0)) for x in far],
        out_specs=[turned, turned],
        out_shape=[turned_shape, turned_shape],
        **options,
    )(band, terms, *far)


def split_columns(pieces, high_ref, low_ref, first):
    for group in pieces:
        piece = group[0][...]
        for other in group[1:]:
            piece = piece + other[...]
        columns = slice(first, first + piece.shape[1])
        first += piece.shape[1]
        high_ref[:, columns], low_ref[:, columns] = halves(piece)


def rows_product(left_high, left_low, high_ref, low_ref):
    total = dot(left_high[...], high_ref[...]) + dot(left_high[...], low_ref[...])
    return total + dot(left_low[...], high_ref[...])


def sorted_kernel(count, keep_ref, left_high, left_low, *refs):
    own, first = [[x] for x in refs[:count]], [[x] for x in refs[count:-4]]
    kept_ref, sent_ref, high_ref, low_ref = refs[-4:]
    width = kept_ref.shape[1]

    @pl.when((pl.program_id(0) == 0) & (keep_ref[0] == 1))
    def _():
        split_columns(own, high_ref, low_ref, 0)
        split_columns(first, high_ref, low_ref, width)

    @pl.when((pl.program_id(0) == 0) & (keep_ref[0] != 1))
    def _():
        split_columns(own, high_ref, low_ref, width)
        split_columns(first, high_ref, low_ref, 0)

    total = rows_product(left_high, left_low, high_ref, low_ref)
    kept_ref[...] = total[:, :width]
    sent_ref[...] = total[:, width:]


def sorted_products(keep, turned, own, first, at, so_far, after=(), passed=()):
    states, nodes = turned[0].shape
    rows = 512 if turned[0].shape[0] % 512 == 0 else 256
    steps = states // rows
    width = sum(piece.shape[1] for piece in own)
    left = pl.BlockSpec((rows, nodes), lambda i: (i, 0))
    out = pl.BlockSpec((rows, width), lambda i: (i + at * steps, 0))
    shape = jax.ShapeDtypeStruct((2 * states, width), jnp.float32)
    return call(
        functools.partial(sorted_kernel, len(own)),
        after,
        into=list(enumerate(so_far)) if at else [],
        passed=passed,
        grid=(steps,),
        in_specs=[pl.BlockSpec(memory_space=pltpu.SMEM), left, left]
        + [pl.BlockSpec(piece.shape, lambda i: (0, 0)) for piece in (*own, *first)],
        out_specs=[out, out],
        out_shape=[shape, shape],
        scratch_shapes=[pltpu.VMEM((nodes, 2 * width), jnp.bfloat16)] * 2,
        name="sorted_products",
    )(keep, *turned, *own, *first)


def both_kernel(summed, left_high, left_low, more_high, more_low, *refs):
    pieces, (out_ref, high_ref, low_ref) = refs[:-3], refs[-3:]
    step, half = pl.program_id(0), pl.num_programs(0) // 2

    @pl.when(step == 0)
    def _():
        groups = [pieces[at : at + summed] for at in range(0, len(pieces), summed)]
        split_columns(groups, high_ref, low_ref, 0)

    @pl.when(step < half)
    def _():
        out_ref[...] = rows_product(left_high, left_low, high_ref, low_ref)

    @pl.when(step >= half)
    def _():
        out_ref[...] = rows_product(more_high, more_low, high_ref, low_ref)


def both_products(y_turned, h_turned, pieces, summed=1, after=(), passed=()):
    states, nodes = y_turned[0].shape
    rows = 512 if y_turned[0].shape[0] % 512 == 0 else 256
    steps = states // rows
    width = sum(piece.shape[1] for piece in pieces) // summed
    first = pl.BlockSpec((rows, nodes), lambda i: (jnp.minimum(i, steps - 1), 0))
    second = pl.BlockSpec((rows, nodes), lambda i: (jnp.maximum(i - steps, 0), 0))
    return call(
        functools.partial(both_kernel, summed),
        after,
        grid=(2 * steps,),
        in_specs=[first, first, second, second]
        + [pl.BlockSpec(piece.shape, lambda i: (0, 0)) for piece in pieces],
        out_specs=[pl.BlockSpec((rows, width), lambda i: (i, 0))],
        out_shape=[jax.ShapeDtypeStruct((2 * states, width), jnp.float32)],
        passed=passed,
        scratch_shapes=[pltpu.VMEM((nodes, width), jnp.bfloat16)] * 2,
        name="both_products",
    )(*y_turned, *h_turned, *pieces)


def pair_kernel(keep_ref, left_high, left_low, more_high, more_low, block_ref, piece_ref, other_ref, *refs):
    kept_ref, sent_ref, high_ref, low_ref = refs
    step, half = pl.program_id(0), pl.num_programs(0) // 2

    @pl.when(step == 0)
    def _():
        split_columns([[piece_ref, other_ref]], high_ref, low_ref, 0)

    def write(total):
        keeps = keep_ref[0] == 1
        kept_ref[...] = jnp.where(keeps, block_ref[...], total)
        sent_ref[...] = jnp.where(keeps, total, block_ref[...])

    @pl.when(step < half)
    def _():
        write(rows_product(left_high, left_low, high_ref, low_ref))

    @pl.when(step >= half)
    def _():
        write(rows_product(more_high, more_low, high_ref, low_ref))


def pair_products(keep, y_turned, h_turned, block, piece, other, after):
    states, nodes = y_turned[0].shape
    rows = 512 if y_turned[0].shape[0] % 512 == 0 else 256
    steps = states // rows
    width = piece.shape[1]
    first = pl.BlockSpec((rows, nodes), lambda i: (jnp.minimum(i, steps - 1), 0))
    second = pl.BlockSpec((rows, nodes), lambda i: (jnp.maximum(i - steps, 0), 0))
    whole = pl.BlockSpec((nodes, width), lambda i: (0, 0))
    out = pl.BlockSpec((rows, width), lambda i: (i, 0))
    return call(
        pair_kernel,
        after,
        grid=(2 * steps,),
        in_specs=[pl.BlockSpec(memory_space=pltpu.SMEM), first, first, second, second, out, whole, whole],
        out_specs=[out, out],
        out_shape=[jax.ShapeDtypeStruct((2 * states, width), jnp.float32)] * 2,
        scratch_shapes=[pltpu.VMEM((nodes, width), jnp.bfloat16)] * 2,
        name="pair_products",
    )(keep, *y_turned, *h_turned, block, piece, other)


def near_kernel(flags_ref, mine_ref, arrived_ref, out_ref):
    out_ref[...] = jnp.where(flags_ref[0] == 1, 1.0, 0.0) * (mine_ref[...] + arrived_ref[...])


def near_rows(flags, mine, arrived, after):
    whole = pl.BlockSpec(mine.shape, lambda i: (0, 0))
    return call(
        near_kernel,
        after,
        grid=(1,),
        in_specs=[pl.BlockSpec(memory_space=pltpu.SMEM), whole, whole],
        out_specs=whole,
        out_shape=jax.ShapeDtypeStruct(mine.shape, jnp.float32),
        name="near_rows",
    )(flags, mine, arrived)


def mark(after):
    shape = jax.ShapeDtypeStruct((8, 128), jnp.float32)

    def kernel(out_ref):
        out_ref[...] = jnp.zeros_like(out_ref)

    return call(kernel, after, in_specs=[], grid=(1,), out_specs=corner(shape), out_shape=shape, name="mark")()


def most_kernel(weight, flags_ref, base_ref, one_ref, one_far, two_ref, two_far, *refs):
    third_refs, outs, rest_ref = refs[:-3], refs[-3:-1], refs[-1]
    one, two = [jnp.where(flags_ref[band] == 1, 1.0, 0.0) for band in (1, 2)]
    states, width = outs[0].shape
    for half, out_ref in enumerate(outs):
        rows = slice(half * states, (half + 1) * states)
        total = base_ref[rows, :width] + one * (one_ref[rows, :] + one_far[rows, :])
        pair = two_ref[rows, :] + two_far[rows, :]
        out_ref[...] = weight * (total + two * pair)
        rest = base_ref[rows, width:] + one * pair
        third = jnp.concatenate([x[rows, :] for x in third_refs], axis=1)
        rest_ref[rows, :] = weight * (rest + two * third)


def finish_most(weight, flags, base, one, one_far, two, two_far, *third):
    rows, width = one.shape
    states = rows // 2
    whole = pl.BlockSpec((rows, width), lambda i: (0, 0))
    shape = jax.ShapeDtypeStruct((states, base.shape[1]), jnp.float32)
    return call(
        functools.partial(most_kernel, weight),
        (),
        grid=(1,),
        in_specs=[pl.BlockSpec(memory_space=pltpu.SMEM), pl.BlockSpec(base.shape, lambda i: (0, 0))]
        + [whole] * 4
        + [pl.BlockSpec(x.shape, lambda i: (0, 0)) for x in third],
        out_specs=[pl.BlockSpec((states, width), lambda i: (0, 0))] * 2 + [whole],
        out_shape=[shape, shape, jax.ShapeDtypeStruct((rows, width), jnp.float32)],
        name="finish_most",
    )(flags, base, one, one_far, two, two_far, *third)


def finish_kernel(weight, upper_ref, lower_ref, *refs):
    far_refs, outs = refs[:-2], refs[-2:]
    far_refs = far_refs[: len(far_refs) // 2], far_refs[len(far_refs) // 2 :]
    for rest_ref, far, out_ref in zip((upper_ref, lower_ref), far_refs, outs):
        arrived = jnp.concatenate([x[...] for x in far], axis=1)
        out_ref[...] = rest_ref[...] + weight * arrived


def finish(weight, outs, rest, far):
    states, width = outs[0].shape
    steps, half = 2, width // 2
    rows = states // steps
    upper = lambda size: pl.BlockSpec((rows, size), lambda i: (i, 0))
    lower = lambda size: pl.BlockSpec((rows, size), lambda i: (i + steps, 0))
    return call(
        functools.partial(finish_kernel, weight),
        (),
        into=list(enumerate(outs)),
        grid=(steps,),
        in_specs=[upper(half), lower(half)]
        + [upper(x.shape[1]) for x in far]
        + [lower(x.shape[1]) for x in far],
        out_specs=[pl.BlockSpec((rows, half), lambda i: (i, 1))] * 2,
        out_shape=[jax.ShapeDtypeStruct((states, width), jnp.float32)] * 2,
        name="finish",
    )(rest, rest, *far, *far)


def exchange(block, axis, pairs):
    return lax.ppermute(block, axis, pairs + [(b, a) for a, b in pairs])


def paired(block):
    return exchange(block, "dom", [(i, i + 1) for i in range(0, lax.axis_size("dom"), 2)])


def crossed(block):
    size = lax.axis_size("dom")
    return exchange(block, "dom", [(i, (i + 1) % size) for i in range(1, size, 2)])


def to_owner(block, owners, step):
    size = len(owners)
    route = []
    for band, owner in enumerate(owners):
        for to in (owner, owner ^ 2) if step == 1 else (owner,):
            route.append(((to ^ step) * size + band, to * size + band))
    return lax.ppermute(block, ("dom", "band"), route)


def on_device(y_cur, y_prev, connect, face_map, elem_scale, potential):
    stiff = element_table()
    nodes, states = y_cur.shape
    domains, band_count = lax.axis_size("dom"), lax.axis_size("band")
    me, level = lax.axis_index("dom"), lax.axis_index("band")
    swaps = domains == 4 and band_count == 4 and states == STATES_DEV
    half = states // 2
    place = jnp.arange(nodes, dtype=jnp.int32)
    cell_place = connect[:, 4] - nodes
    own = jnp.sum(jnp.where(cell_place[:, None] == place[None, :], elem_scale[:, None], 0.0), axis=0)
    before = lax.ppermute(own, "dom", [(i, (i + 1) % domains) for i in range(domains)])
    at_grid = jnp.sum(jnp.where(place[:, None] == face_map[None, :], potential[:, None], 0.0), axis=0)
    odd = (me % 2).astype(jnp.int32).reshape(1)
    weight = 1.0 / (nodes * domains)

    far, current, waited = [], None, ()
    for at in (0, 1):
        chunk, current = to_grid(face_map, y_cur, at, half, current, waited)
        far.append(crossed(chunk))
        waited = (chunk,)
    current_paired = paired(current)
    band, last = prepare(stiff, odd, own, before, at_grid, face_map, y_prev, (current,))

    following = []
    for at, piece in enumerate(far):
        terms = on_chip(band, current, current_paired, last, at * half, half, following)
        following.append(next_degree(band, terms, piece, ()))
    next_far = [crossed(following[0])]

    if not swaps:
        y_next, whole, other, *y_turned = from_grid(face_map, following)
        next_far.append(crossed(other))
        h_turned = applied_next(band, on_chip(band, whole, paired(whole), None), next_far)
        piece = lax.all_gather(whole, "band", axis=1, tiled=True)
        (block,) = both_products(y_turned, h_turned, [piece])
        parts = [
            weight * lax.psum_scatter(rows, "dom", scatter_dimension=1, tiled=True)
            for rows in (block[:states], block[states:])
        ]
        return (y_next, *parts)

    outward = [(2, 3), (1, 0)]
    core, chip, upper = me % 2, me // 2, level // 2
    keep = jnp.where(core == level % 2, 1, 0).astype(jnp.int32).reshape(1)
    near_route = [
        (((b // 2 * 2 + c) ^ 2) * 4 + b, (b // 2 * 2 + c) * 4 + b) for b in range(4) for c in (0, 1)
    ]
    near_across = lambda x: lax.ppermute(x, ("dom", "band"), near_route)
    second_owner, third_owner = [2, 2, 1, 1], [3, 3, 0, 0]

    ends, middle = [(0, 1), (2, 3)], [(1, 2)]
    first = [exchange(x, "band", ends) for x in following]
    second_middle = [exchange(x, "band", middle) for x in following]
    waited = (first[0], next_far[0])
    y_next, whole, other, *y_turned, second_middle[0] = from_grid(face_map, following, waited, second_middle[:1])
    next_far.append(crossed(other))
    second_out = [lax.ppermute(second_middle[0], "band", outward)]
    whole_paired = paired(whole)
    (first[0],) = gate(first[:1], (mark((y_next,)), whole_paired, second_middle[1]))
    third_middle = [exchange(first[0], "band", middle)]
    *near, second_middle[1] = sorted_products(keep, y_turned, following, first, 0, (), (), second_middle[1:])
    second_out.append(lax.ppermute(second_middle[1], "band", outward))
    h_turned = applied_next(band, on_chip(band, whole, whole_paired, None, after=near[:1]), next_far)
    (first[1],) = gate(first[1:], (h_turned[0], third_middle[0]))
    third_middle.append(exchange(first[1], "band", middle))
    kept, sent, third_middle[0] = sorted_products(keep, h_turned, following, first, 1, near, (), third_middle[:1])
    third_out = [lax.ppermute(third_middle[0], "band", outward)]
    sent = paired(sent)

    blocks = [*both_products(y_turned, h_turned, [second_middle[0], second_out[0]], 2, (kept,))]
    cores = [to_owner(blocks[0], second_owner, 1)]
    (near,) = plus(kept, sent, (blocks[0],))
    near_far = near_across(near)
    pieces = [second_middle[1], second_out[1]]
    block, third_middle[1] = both_products(y_turned, h_turned, pieces, 2, (near,), third_middle[1:])
    blocks.append(block)
    tails = [third_middle[1][:, : half // 2], third_middle[1][:, half // 2 :]]
    (second,) = plus(blocks[0], cores[0], (blocks[1],))
    second_far = to_owner(second, second_owner, 2)
    tails_out = [lax.ppermute(tails[0], "band", outward)]
    keep = jnp.where(core == upper, 1, 0).astype(jnp.int32).reshape(1)
    pieces = (blocks[1], third_middle[0], third_out[0])
    kept, sent = pair_products(keep, y_turned, h_turned, *pieces, (second,))
    sent = paired(sent)
    (tails[1],) = gate(tails[1:], (kept, second_far))
    tails_out.append(lax.ppermute(tails[1], "band", outward))
    (pair,) = plus(kept, sent, tails[1:])
    pair_route = [
        (((2 - b // 2 * 2 + c) ^ 2) * 4 + b, (2 - b // 2 * 2 + c) * 4 + b) for b in range(4) for c in (0, 1)
    ]
    pair_far = lax.ppermute(pair, ("dom", "band"), pair_route)
    blocks, waited = [], (pair,)
    for piece in zip(tails, tails_out):
        blocks += both_products(y_turned, h_turned, list(piece), 2, waited)
        waited = blocks[-1:]
    cores = [to_owner(block, third_owner, 1) for block in blocks]
    third = [*plus(blocks[0], cores[0], blocks[1:])]
    third += plus(blocks[1], cores[1], third)
    third_far = [to_owner(block, third_owner, 2) for block in third]
    is_near, is_second = chip == upper, core == upper
    flags = jnp.stack([is_near, ~is_near & is_second, ~is_near & ~is_second]).astype(jnp.int32)
    base = near_rows(flags, near, near_far, (third[1],))
    *outs, rest = finish_most(weight, flags, base, second, second_far, pair, pair_far, *third)
    return (y_next, *finish(weight, outs, rest, third_far))


def solution(mesh):
    placed = (
        P(("image", "dom"), "band"),
        P(("image", "dom"), "band"),
        P("dom", None),
        P("dom"),
        P("dom"),
        P(("image", "dom")),
    )
    return jax.shard_map(
        on_device,
        mesh=mesh,
        in_specs=placed,
        out_specs=(
            P(("image", "dom"), "band"),
            P(("image", "band"), "dom"),
            P(("image", "band"), "dom"),
        ),
        check_vma=False,
    )
```

```python
import functools

import jax
import jax.numpy as jnp
import numpy as np
from jax import lax
from jax.experimental import pallas as pl
from jax.experimental.pallas import tpu as pltpu
from jax.sharding import PartitionSpec as P

SIDE = 32
STATES_DEV = 512
BLOCK = 128
WINDOW = 256
MARGIN = (WINDOW - BLOCK) // 2

cheb_low = 1.0
cheb_high = 9.0
centre = 0.5 * (cheb_high + cheb_low)
half_width = 0.5 * (cheb_high - cheb_low)

OFFSETS = [(dj, dk) for dj in (-1, 0, 1) for dk in (-1, 0, 1)]
PARAMS = pltpu.CompilerParams(vmem_limit_bytes=32 * 1024 * 1024)


COST = pl.CostEstimate(flops=10**12, bytes_accessed=1, transcendentals=0)


def element_table():
    stiff_line = np.array([[1.0, -1.0], [-1.0, 1.0]])
    mass_line = np.array([[1.0 / 3.0, 1.0 / 6.0], [1.0 / 6.0, 1.0 / 3.0]])
    total = np.kron(stiff_line, np.kron(mass_line, mass_line))
    total = total + np.kron(mass_line, np.kron(stiff_line, mass_line))
    total = total + np.kron(mass_line, np.kron(mass_line, stiff_line))
    return total.astype(np.float32)


def halves(x):
    high = x.astype(jnp.bfloat16)
    low = (x - high.astype(jnp.float32)).astype(jnp.bfloat16)
    return high, low


def dot(a, b):
    return lax.dot_general(a, b, (((1,), (0,)), ((), ())), preferred_element_type=jnp.float32)


def corner(x):
    rows = 32 // x.dtype.itemsize
    return pl.BlockSpec((rows, 128), lambda *_: (0, 0))


def call(kernel, after, *, in_specs, out_specs, out_shape, name, into=(), passed=(), params=None, **options):
    count = len(in_specs)
    extra = [*[array for _, array in into], *after, *passed]
    aliases = {count + at: out for at, (out, _) in enumerate(into)}
    outs = len(out_shape) if isinstance(out_shape, (list, tuple)) else 1
    if passed:
        out_specs = [*out_specs, *map(corner, passed)]
        out_shape = [*out_shape, *[jax.ShapeDtypeStruct(x.shape, x.dtype) for x in passed]]
        aliases |= {count + len(extra) - len(passed) + at: outs + at for at in range(len(passed))}

    def body(*refs):
        rest = refs[count + len(extra) :]
        kernel(*refs[:count], *rest[:outs], *rest[outs + len(passed) :])
        first = count + len(extra) - len(passed)
        for x_ref, out_ref in zip(refs[first : first + len(passed)], rest[outs : outs + len(passed)]):
            out_ref[...] = x_ref[...]

    made = pl.pallas_call(
        body,
        in_specs=[*in_specs, *map(corner, extra)],
        out_specs=out_specs,
        out_shape=out_shape,
        input_output_aliases=aliases,
        compiler_params=params or PARAMS,
        cost_estimate=COST,
        name=name,
        **options,
    )
    return lambda *args: made(*args, *extra)


def gate(arrays, after):
    return call(lambda: None, after, passed=arrays, grid=(1,), in_specs=[], out_specs=[], out_shape=[], name="gate")()


def plus_kernel(left_ref, right_ref, out_ref):
    out_ref[...] = left_ref[...] + right_ref[...]


def plus(left, right, after, passed=()):
    rows = min(256 if left.shape[1] <= 128 else 512, left.shape[0])
    part = pl.BlockSpec((rows, left.shape[1]), lambda i: (i, 0))
    return call(
        plus_kernel,
        after,
        grid=(left.shape[0] // rows,),
        in_specs=[part, part],
        out_specs=[part],
        out_shape=[jax.ShapeDtypeStruct(left.shape, left.dtype)],
        passed=passed,
        name="plus",
    )(left, right)


def to_grid_kernel(at, map_hbm, x_hbm, out_ref, whole_ref, map_ref, x_ref, high_ref, low_ref, sems):
    step = pl.program_id(0)
    width = x_ref.shape[1]

    @pl.when(step == 0)
    def _():
        copies = [
            pltpu.make_async_copy(x_hbm.at[:, pl.ds(at * width, width)], x_ref, sems.at[0]),
            pltpu.make_async_copy(map_hbm, map_ref, sems.at[1]),
        ]
        for copy in copies:
            copy.start()
        for copy in copies:
            copy.wait()
        high_ref[...], low_ref[...] = halves(x_ref[...])

    rows, nodes = out_ref.shape[0], x_ref.shape[0]
    place = lax.broadcasted_iota(jnp.int32, (BLOCK, nodes), 1)
    for part in range(rows // BLOCK):
        row = map_ref[pl.ds(step * (rows // BLOCK) + part, 1), :]
        column = jnp.broadcast_to(row, (BLOCK, BLOCK)).T
        column = jnp.concatenate([column] * (nodes // BLOCK), axis=1)
        pick = jnp.where(place == column, 1.0, 0.0).astype(jnp.bfloat16)
        moved = dot(pick, high_ref[...]) + dot(pick, low_ref[...])
        out = slice(part * BLOCK, (part + 1) * BLOCK)
        out_ref[out, :] = moved
        whole_ref[out, :] = moved


def to_grid(face_map, x, at, width, so_far, after):
    nodes, states = x.shape
    rows = 512
    places = (nodes // BLOCK, BLOCK)
    return call(
        functools.partial(to_grid_kernel, at),
        after,
        params=pltpu.CompilerParams(vmem_limit_bytes=(60 if at == 0 else 32) * 1024 * 1024),
        into=[(1, so_far)] if at else [],
        grid=(nodes // rows,),
        in_specs=[pl.BlockSpec(memory_space=pltpu.HBM)] * 2,
        out_specs=[pl.BlockSpec((rows, width), lambda i: (i, 0)), pl.BlockSpec((rows, width), lambda i: (i, at))],
        out_shape=[
            jax.ShapeDtypeStruct((nodes, width), jnp.float32),
            jax.ShapeDtypeStruct((nodes, states), jnp.float32),
        ],
        scratch_shapes=[pltpu.VMEM(places, jnp.int32), pltpu.VMEM((nodes, width), jnp.float32)]
        + [pltpu.VMEM((nodes, width), jnp.bfloat16)] * 2
        + [pltpu.SemaphoreType.DMA((2,))],
        name="to_grid",
    )(face_map.reshape(places), x)


def from_grid_kernel(map_ref, *refs):
    pieces, refs = refs[:-7], refs[-7:]
    out_ref, again_ref, half_ref, turned_high, turned_low, high_ref, low_ref = refs
    step = pl.program_id(0)

    @pl.when(step == 0)
    def _():
        split_columns([[x] for x in pieces], high_ref, low_ref, 0)

    rows, nodes = out_ref.shape[0], high_ref.shape[0]
    node = lax.broadcasted_iota(jnp.int32, (rows, nodes), 0) + step * rows
    pick = jnp.where(node == map_ref[...], 1.0, 0.0).astype(jnp.bfloat16)
    out_ref[...] = dot(pick, high_ref[...]) + dot(pick, low_ref[...])
    here = pl.ds(pl.multiple_of(step * rows, rows), rows)
    again = jnp.concatenate([x[here, :] for x in pieces], axis=1)
    again_ref[...] = again
    half_ref[...] = again[:, half_ref.shape[1] :]
    turned_high[...], turned_low[...] = halves(again.T)


def from_grid(face_map, pieces, after=(), passed=()):
    nodes = pieces[0].shape[0]
    states = sum(x.shape[1] for x in pieces)
    rows = 256
    part = pl.BlockSpec((rows, states), lambda i: (i, 0))
    turned = pl.BlockSpec((states, rows), lambda i: (0, i))
    sizes = (states, states, states // 2)
    return call(
        from_grid_kernel,
        after,
        passed=passed,
        grid=(nodes // rows,),
        in_specs=[pl.BlockSpec((1, nodes), lambda i: (0, 0))]
        + [pl.BlockSpec(x.shape, lambda i: (0, 0)) for x in pieces],
        out_specs=[part, part, pl.BlockSpec((rows, states // 2), lambda i: (i, 0)), turned, turned],
        out_shape=[jax.ShapeDtypeStruct((nodes, size), jnp.float32) for size in sizes]
        + [jax.ShapeDtypeStruct((states, nodes), jnp.bfloat16)] * 2,
        scratch_shapes=[pltpu.VMEM((nodes, states), jnp.bfloat16)] * 2,
        name="from_grid",
    )(face_map.reshape(1, nodes), *pieces)


def plane_terms(shifted, stiff, layer):
    terms = []
    for dj, dk in OFFSETS:
        total = None
        for b in (0, 1):
            for c in (0, 1):
                if b + dj in (0, 1) and c + dk in (0, 1):
                    weight = float(stiff[2 * b + c, 4 * layer + 2 * (b + dj) + c + dk])
                    term = weight * shifted[b][c]
                    total = term if total is None else total + term
        terms.append(total)
    return terms


def write_terms(stiff, odd, own_ref, before_ref, potential_ref, terms_ref):
    nodes = own_ref.shape[1]
    column = lax.broadcasted_iota(jnp.int32, (8, nodes), 1) & (SIDE - 1)
    here, layers = None, []
    for ref in (own_ref, before_ref):
        scale = jnp.broadcast_to(0.5 * ref[...], (8, nodes))
        back = jnp.where(column == 0, pltpu.roll(scale, nodes - SIDE + 1, 1), pltpu.roll(scale, 1, 1))
        shifted = [[x, pltpu.roll(x, SIDE, 1)] for x in (scale, back)]
        shifted = [[shifted[c][b] for c in (0, 1)] for b in (0, 1)]
        mine = plane_terms(shifted, stiff, 0)
        here = mine if here is None else [a + b for a, b in zip(here, mine)]
        layers.append(plane_terms(shifted, stiff, 1))
    here[4] = here[4] + potential_ref[...]
    after, back = layers
    paired = [jnp.where(odd, b, a) for a, b in zip(after, back)]
    far = [jnp.where(odd, a, b) for a, b in zip(after, back)]
    for at, term in enumerate(here + paired + far):
        terms_ref[at : at + 1, :] = term[:1]


def write_bands(terms, out_ref):
    row = lax.broadcasted_iota(jnp.int32, (SIDE, BLOCK), 0)
    lane = lax.broadcasted_iota(jnp.int32, (SIDE, BLOCK), 1)
    turn = (lane - row) & (SIDE - 1)
    for line in range(BLOCK // SIDE):
        rows = slice(line * SIDE, (line + 1) * SIDE)
        rest = slice(BLOCK + rows.start, BLOCK + rows.stop)
        masks = {}
        for dj, dk in OFFSETS:
            tile, group = divmod(line + MARGIN // SIDE + dj, BLOCK // SIDE)
            masks[dj, dk] = tile, (turn == dk % SIDE) & ((lane >> 5) == group)
        for plane in range(3):
            totals = [jnp.zeros((SIDE, BLOCK), jnp.float32) for _ in range(WINDOW // BLOCK)]
            for at, offset in enumerate(OFFSETS):
                term = terms[rows, plane * 9 + at : plane * 9 + at + 1]
                tile, mask = masks[offset]
                totals[tile] = jnp.where(mask, term, totals[tile])
            for tile, total in enumerate(totals):
                columns = slice(tile * BLOCK, (tile + 1) * BLOCK)
                out_ref[plane, 0, rows, columns], out_ref[plane, 0, rest, columns] = halves(total)


def prepare_kernel(stiff, odd_ref, own_ref, before_ref, potential_ref, map_ref, prev_ref, *refs):
    band_ref, last_ref, terms_ref, high_ref, low_ref = refs
    step = pl.program_id(0)
    nodes = prev_ref.shape[0]

    @pl.when(step == 0)
    def _():
        write_terms(stiff, odd_ref[0] == 1, own_ref, before_ref, potential_ref, terms_ref)
        split_columns([[prev_ref]], high_ref, low_ref, 0)

    write_bands(terms_ref[:, pl.ds(pl.multiple_of(step * BLOCK, BLOCK), BLOCK)].T, band_ref)
    place = lax.broadcasted_iota(jnp.int32, (BLOCK, nodes), 1)
    column = jnp.broadcast_to(map_ref[pl.ds(step, 1), :], (BLOCK, BLOCK)).T
    column = jnp.concatenate([column] * (nodes // BLOCK), axis=1)
    pick = jnp.where(place == column, 1.0, 0.0).astype(jnp.bfloat16)
    last_ref[...] = dot(pick, high_ref[...]) + dot(pick, low_ref[...])


def prepare(stiff, odd, own, before, potential, face_map, y_prev, after):
    nodes, states = y_prev.shape
    row = pl.BlockSpec((1, nodes), lambda i: (0, 0))
    return call(
        functools.partial(prepare_kernel, stiff),
        after,
        grid=(nodes // BLOCK,),
        in_specs=[pl.BlockSpec(memory_space=pltpu.SMEM), row, row, row]
        + [pl.BlockSpec((nodes // BLOCK, BLOCK), lambda i: (0, 0))]
        + [pl.BlockSpec((nodes, states), lambda i: (0, 0))],
        out_specs=[
            pl.BlockSpec((3, 1, 2 * BLOCK, WINDOW), lambda i: (0, i, 0, 0)),
            pl.BlockSpec((BLOCK, states), lambda i: (i, 0)),
        ],
        out_shape=[
            jax.ShapeDtypeStruct((3, nodes // BLOCK, 2 * BLOCK, WINDOW), jnp.bfloat16),
            jax.ShapeDtypeStruct((nodes, states), jnp.float32),
        ],
        scratch_shapes=[pltpu.VMEM((32, nodes), jnp.float32)]
        + [pltpu.VMEM((nodes, states), jnp.bfloat16)] * 2,
        name="prepare",
    )(
        odd,
        *[x.reshape(1, nodes) for x in (own, before, potential)],
        face_map.reshape(nodes // BLOCK, BLOCK),
        y_prev,
    )


def fill(wide, plane, ref, start, width):
    nodes = ref.shape[0]
    for first, part in zip((start, width + start), halves(ref[...])):
        columns = slice(first, first + part.shape[1])
        wide[plane, pl.ds(MARGIN, nodes), columns] = part
        wide[plane, pl.ds(0, MARGIN), columns] = part[nodes - MARGIN :]
        wide[plane, pl.ds(MARGIN + nodes, MARGIN), columns] = part[:MARGIN]


def applied_rows(band_ref, at, wide, first):
    total = None
    for plane in range(band_ref.shape[0]):
        term = dot(band_ref[plane, at], wide[plane, pl.ds(first, WINDOW), :])
        total = term if total is None else total + term
    total = total[:BLOCK] + total[BLOCK:]
    width = total.shape[1] // 2
    return total[:, :width] + total[:, width:]


def on_chip_kernel(filtered, band_ref, own_ref, paired_ref, *refs):
    last_ref, (out_ref, wide) = refs[0], refs[-2:]
    step = pl.program_id(0)
    width = own_ref.shape[1]

    @pl.when(step == 0)
    def _():
        for plane, ref in enumerate((own_ref, paired_ref)):
            fill(wide, plane, ref, 0, width)

    per_step = band_ref.shape[1]
    for at in range(per_step):
        first = pl.multiple_of((step * per_step + at) * BLOCK, BLOCK)
        total = applied_rows(band_ref, at, wide, first)
        rows = pl.ds(at * BLOCK, BLOCK)
        if filtered:
            total = (2.0 / half_width) * (total - centre * own_ref[pl.ds(first, BLOCK), :]) - last_ref[rows, :]
        out_ref[rows, :] = total


def across_kernel(filtered, pieces, band_ref, part_ref, *refs):
    far_refs, outs, wide = refs[:pieces], refs[pieces:-1], refs[-1]
    step = pl.program_id(0)
    width = part_ref.shape[1]

    @pl.when(step == 0)
    def _():
        for at, ref in enumerate(far_refs):
            fill(wide, 0, ref, at * width // pieces, width)

    per_step = band_ref.shape[1]
    for at in range(per_step):
        first = pl.multiple_of((step * per_step + at) * BLOCK, BLOCK)
        total = applied_rows(band_ref, at, wide, first)
        rows = pl.ds(at * BLOCK, BLOCK)
        if filtered:
            outs[0][rows, :] = part_ref[rows, :] + (2.0 / half_width) * total
        else:
            outs[0][:, rows], outs[1][:, rows] = halves((part_ref[rows, :] + total).T)


PER_STEP = 2


def on_chip(band, own, paired, last, first=0, width=None, after=()):
    nodes, states = own.shape
    rows, width = PER_STEP * BLOCK, width or states
    at = first // width
    column = pl.BlockSpec((nodes, width), lambda i: (0, at))
    part = pl.BlockSpec((rows, width), lambda i: (i, at))
    return call(
        functools.partial(on_chip_kernel, last is not None),
        after,
        grid=(nodes // rows,),
        in_specs=[pl.BlockSpec((2, PER_STEP, 2 * BLOCK, WINDOW), lambda i: (0, i, 0, 0)), column, column]
        + [part] * (last is not None),
        out_specs=pl.BlockSpec((rows, width), lambda i: (i, 0)),
        out_shape=jax.ShapeDtypeStruct((nodes, width), jnp.float32),
        scratch_shapes=[pltpu.VMEM((2, nodes + 2 * MARGIN, 2 * width), jnp.bfloat16)],
        name="on_chip",
    )(band, own, paired, *([] if last is None else [last]))


def across_specs(nodes, width):
    rows = PER_STEP * BLOCK
    return dict(
        grid=(nodes // rows,),
        scratch_shapes=[pltpu.VMEM((1, nodes + 2 * MARGIN, 2 * width), jnp.bfloat16)],
        name="across",
    ), pl.BlockSpec((1, PER_STEP, 2 * BLOCK, WINDOW), lambda i: (2, i, 0, 0))


def next_degree(band, terms, far, after):
    nodes, width = far.shape
    rows = PER_STEP * BLOCK
    options, band_spec = across_specs(nodes, width)
    part = pl.BlockSpec((rows, width), lambda i: (i, 0))
    return call(
        functools.partial(across_kernel, True, 1),
        after,
        in_specs=[band_spec, part, pl.BlockSpec((nodes, width), lambda i: (0, 0))],
        out_specs=part,
        out_shape=jax.ShapeDtypeStruct((nodes, width), jnp.float32),
        **options,
    )(band, terms, far)


def applied_next(band, terms, far, after=()):
    nodes, states = terms.shape
    rows = PER_STEP * BLOCK
    options, band_spec = across_specs(nodes, states)
    turned = pl.BlockSpec((states, rows), lambda i: (0, i))
    turned_shape = jax.ShapeDtypeStruct((states, nodes), jnp.bfloat16)
    return call(
        functools.partial(across_kernel, False, len(far)),
        after,
        in_specs=[band_spec, pl.BlockSpec((rows, states), lambda i: (i, 0))]
        + [pl.BlockSpec(x.shape, lambda i: (0, 0)) for x in far],
        out_specs=[turned, turned],
        out_shape=[turned_shape, turned_shape],
        **options,
    )(band, terms, *far)


def split_columns(pieces, high_ref, low_ref, first):
    for group in pieces:
        piece = group[0][...]
        for other in group[1:]:
            piece = piece + other[...]
        columns = slice(first, first + piece.shape[1])
        first += piece.shape[1]
        high_ref[:, columns], low_ref[:, columns] = halves(piece)


def rows_product(left_high, left_low, high_ref, low_ref):
    total = dot(left_high[...], high_ref[...]) + dot(left_high[...], low_ref[...])
    return total + dot(left_low[...], high_ref[...])


def sorted_kernel(count, keep_ref, left_high, left_low, *refs):
    own, first = [[x] for x in refs[:count]], [[x] for x in refs[count:-4]]
    kept_ref, sent_ref, high_ref, low_ref = refs[-4:]
    width = kept_ref.shape[1]

    @pl.when((pl.program_id(0) == 0) & (keep_ref[0] == 1))
    def _():
        split_columns(own, high_ref, low_ref, 0)
        split_columns(first, high_ref, low_ref, width)

    @pl.when((pl.program_id(0) == 0) & (keep_ref[0] != 1))
    def _():
        split_columns(own, high_ref, low_ref, width)
        split_columns(first, high_ref, low_ref, 0)

    total = rows_product(left_high, left_low, high_ref, low_ref)
    kept_ref[...] = total[:, :width]
    sent_ref[...] = total[:, width:]


def sorted_products(keep, turned, own, first, at, so_far, after=(), passed=()):
    states, nodes = turned[0].shape
    rows = 512 if turned[0].shape[0] % 512 == 0 else 256
    steps = states // rows
    width = sum(piece.shape[1] for piece in own)
    left = pl.BlockSpec((rows, nodes), lambda i: (i, 0))
    out = pl.BlockSpec((rows, width), lambda i: (i + at * steps, 0))
    shape = jax.ShapeDtypeStruct((2 * states, width), jnp.float32)
    return call(
        functools.partial(sorted_kernel, len(own)),
        after,
        into=list(enumerate(so_far)) if at else [],
        passed=passed,
        grid=(steps,),
        in_specs=[pl.BlockSpec(memory_space=pltpu.SMEM), left, left]
        + [pl.BlockSpec(piece.shape, lambda i: (0, 0)) for piece in (*own, *first)],
        out_specs=[out, out],
        out_shape=[shape, shape],
        scratch_shapes=[pltpu.VMEM((nodes, 2 * width), jnp.bfloat16)] * 2,
        name="sorted_products",
    )(keep, *turned, *own, *first)


def both_kernel(summed, left_high, left_low, more_high, more_low, *refs):
    pieces, (out_ref, high_ref, low_ref) = refs[:-3], refs[-3:]
    step, half = pl.program_id(0), pl.num_programs(0) // 2

    @pl.when(step == 0)
    def _():
        groups = [pieces[at : at + summed] for at in range(0, len(pieces), summed)]
        split_columns(groups, high_ref, low_ref, 0)

    @pl.when(step < half)
    def _():
        out_ref[...] = rows_product(left_high, left_low, high_ref, low_ref)

    @pl.when(step >= half)
    def _():
        out_ref[...] = rows_product(more_high, more_low, high_ref, low_ref)


def both_products(y_turned, h_turned, pieces, summed=1, after=(), passed=()):
    states, nodes = y_turned[0].shape
    rows = 512 if y_turned[0].shape[0] % 512 == 0 else 256
    steps = states // rows
    width = sum(piece.shape[1] for piece in pieces) // summed
    first = pl.BlockSpec((rows, nodes), lambda i: (jnp.minimum(i, steps - 1), 0))
    second = pl.BlockSpec((rows, nodes), lambda i: (jnp.maximum(i - steps, 0), 0))
    return call(
        functools.partial(both_kernel, summed),
        after,
        grid=(2 * steps,),
        in_specs=[first, first, second, second]
        + [pl.BlockSpec(piece.shape, lambda i: (0, 0)) for piece in pieces],
        out_specs=[pl.BlockSpec((rows, width), lambda i: (i, 0))],
        out_shape=[jax.ShapeDtypeStruct((2 * states, width), jnp.float32)],
        passed=passed,
        scratch_shapes=[pltpu.VMEM((nodes, width), jnp.bfloat16)] * 2,
        name="both_products",
    )(*y_turned, *h_turned, *pieces)


def pair_kernel(keep_ref, left_high, left_low, more_high, more_low, block_ref, piece_ref, other_ref, *refs):
    kept_ref, sent_ref, high_ref, low_ref = refs
    step, half = pl.program_id(0), pl.num_programs(0) // 2

    @pl.when(step == 0)
    def _():
        split_columns([[piece_ref, other_ref]], high_ref, low_ref, 0)

    def write(total):
        keeps = keep_ref[0] == 1
        kept_ref[...] = jnp.where(keeps, block_ref[...], total)
        sent_ref[...] = jnp.where(keeps, total, block_ref[...])

    @pl.when(step < half)
    def _():
        write(rows_product(left_high, left_low, high_ref, low_ref))

    @pl.when(step >= half)
    def _():
        write(rows_product(more_high, more_low, high_ref, low_ref))


def pair_products(keep, y_turned, h_turned, block, piece, other, after):
    states, nodes = y_turned[0].shape
    rows = 512 if y_turned[0].shape[0] % 512 == 0 else 256
    steps = states // rows
    width = piece.shape[1]
    first = pl.BlockSpec((rows, nodes), lambda i: (jnp.minimum(i, steps - 1), 0))
    second = pl.BlockSpec((rows, nodes), lambda i: (jnp.maximum(i - steps, 0), 0))
    whole = pl.BlockSpec((nodes, width), lambda i: (0, 0))
    out = pl.BlockSpec((rows, width), lambda i: (i, 0))
    return call(
        pair_kernel,
        after,
        grid=(2 * steps,),
        in_specs=[pl.BlockSpec(memory_space=pltpu.SMEM), first, first, second, second, out, whole, whole],
        out_specs=[out, out],
        out_shape=[jax.ShapeDtypeStruct((2 * states, width), jnp.float32)] * 2,
        scratch_shapes=[pltpu.VMEM((nodes, width), jnp.bfloat16)] * 2,
        name="pair_products",
    )(keep, *y_turned, *h_turned, block, piece, other)


def near_kernel(flags_ref, mine_ref, arrived_ref, out_ref):
    out_ref[...] = jnp.where(flags_ref[0] == 1, 1.0, 0.0) * (mine_ref[...] + arrived_ref[...])


def near_rows(flags, mine, arrived, after):
    whole = pl.BlockSpec(mine.shape, lambda i: (0, 0))
    return call(
        near_kernel,
        after,
        grid=(1,),
        in_specs=[pl.BlockSpec(memory_space=pltpu.SMEM), whole, whole],
        out_specs=whole,
        out_shape=jax.ShapeDtypeStruct(mine.shape, jnp.float32),
        name="near_rows",
    )(flags, mine, arrived)


def mark(after):
    shape = jax.ShapeDtypeStruct((8, 128), jnp.float32)

    def kernel(out_ref):
        out_ref[...] = jnp.zeros_like(out_ref)

    return call(kernel, after, in_specs=[], grid=(1,), out_specs=corner(shape), out_shape=shape, name="mark")()


def most_kernel(weight, flags_ref, base_ref, one_ref, one_far, two_ref, two_far, *refs):
    third_refs, outs, rest_ref = refs[:-3], refs[-3:-1], refs[-1]
    one, two = [jnp.where(flags_ref[band] == 1, 1.0, 0.0) for band in (1, 2)]
    states, width = outs[0].shape
    for half, out_ref in enumerate(outs):
        rows = slice(half * states, (half + 1) * states)
        total = base_ref[rows, :width] + one * (one_ref[rows, :] + one_far[rows, :])
        pair = two_ref[rows, :] + two_far[rows, :]
        out_ref[...] = weight * (total + two * pair)
        rest = base_ref[rows, width:] + one * pair
        third = jnp.concatenate([x[rows, :] for x in third_refs], axis=1)
        rest_ref[rows, :] = weight * (rest + two * third)


def finish_most(weight, flags, base, one, one_far, two, two_far, *third):
    rows, width = one.shape
    states = rows // 2
    whole = pl.BlockSpec((rows, width), lambda i: (0, 0))
    shape = jax.ShapeDtypeStruct((states, base.shape[1]), jnp.float32)
    return call(
        functools.partial(most_kernel, weight),
        (),
        grid=(1,),
        in_specs=[pl.BlockSpec(memory_space=pltpu.SMEM), pl.BlockSpec(base.shape, lambda i: (0, 0))]
        + [whole] * 4
        + [pl.BlockSpec(x.shape, lambda i: (0, 0)) for x in third],
        out_specs=[pl.BlockSpec((states, width), lambda i: (0, 0))] * 2 + [whole],
        out_shape=[shape, shape, jax.ShapeDtypeStruct((rows, width), jnp.float32)],
        name="finish_most",
    )(flags, base, one, one_far, two, two_far, *third)


def finish_kernel(weight, upper_ref, lower_ref, *refs):
    far_refs, outs = refs[:-2], refs[-2:]
    far_refs = far_refs[: len(far_refs) // 2], far_refs[len(far_refs) // 2 :]
    for rest_ref, far, out_ref in zip((upper_ref, lower_ref), far_refs, outs):
        arrived = jnp.concatenate([x[...] for x in far], axis=1)
        out_ref[...] = rest_ref[...] + weight * arrived


def finish(weight, outs, rest, far):
    states, width = outs[0].shape
    steps, half = 2, width // 2
    rows = states // steps
    upper = lambda size: pl.BlockSpec((rows, size), lambda i: (i, 0))
    lower = lambda size: pl.BlockSpec((rows, size), lambda i: (i + steps, 0))
    return call(
        functools.partial(finish_kernel, weight),
        (),
        into=list(enumerate(outs)),
        grid=(steps,),
        in_specs=[upper(half), lower(half)]
        + [upper(x.shape[1]) for x in far]
        + [lower(x.shape[1]) for x in far],
        out_specs=[pl.BlockSpec((rows, half), lambda i: (i, 1))] * 2,
        out_shape=[jax.ShapeDtypeStruct((states, width), jnp.float32)] * 2,
        name="finish",
    )(rest, rest, *far, *far)


def exchange(block, axis, pairs):
    return lax.ppermute(block, axis, pairs + [(b, a) for a, b in pairs])


def paired(block):
    return exchange(block, "dom", [(i, i + 1) for i in range(0, lax.axis_size("dom"), 2)])


def crossed(block):
    size = lax.axis_size("dom")
    return exchange(block, "dom", [(i, (i + 1) % size) for i in range(1, size, 2)])


def to_owner(block, owners, step):
    size = len(owners)
    route = []
    for band, owner in enumerate(owners):
        for to in (owner, owner ^ 2) if step == 1 else (owner,):
            route.append(((to ^ step) * size + band, to * size + band))
    return lax.ppermute(block, ("dom", "band"), route)


def on_device(y_cur, y_prev, connect, face_map, elem_scale, potential):
    stiff = element_table()
    nodes, states = y_cur.shape
    domains, band_count = lax.axis_size("dom"), lax.axis_size("band")
    me, level = lax.axis_index("dom"), lax.axis_index("band")
    swaps = domains == 4 and band_count == 4 and states == STATES_DEV
    half = states // 2
    place = jnp.arange(nodes, dtype=jnp.int32)
    cell_place = connect[:, 4] - nodes
    own = jnp.sum(jnp.where(cell_place[:, None] == place[None, :], elem_scale[:, None], 0.0), axis=0)
    before = lax.ppermute(own, "dom", [(i, (i + 1) % domains) for i in range(domains)])
    at_grid = jnp.sum(jnp.where(place[:, None] == face_map[None, :], potential[:, None], 0.0), axis=0)
    odd = (me % 2).astype(jnp.int32).reshape(1)
    weight = 1.0 / (nodes * domains)

    far, current, waited = [], None, ()
    for at in (0, 1):
        chunk, current = to_grid(face_map, y_cur, at, half, current, waited)
        far.append(crossed(chunk))
        waited = (chunk,)
    current_paired = paired(current)
    band, last = prepare(stiff, odd, own, before, at_grid, face_map, y_prev, (current,))

    following = []
    for at, piece in enumerate(far):
        terms = on_chip(band, current, current_paired, last, at * half, half, following)
        following.append(next_degree(band, terms, piece, ()))
    next_far = [crossed(following[0])]

    if not swaps:
        y_next, whole, other, *y_turned = from_grid(face_map, following)
        next_far.append(crossed(other))
        h_turned = applied_next(band, on_chip(band, whole, paired(whole), None), next_far)
        piece = lax.all_gather(whole, "band", axis=1, tiled=True)
        (block,) = both_products(y_turned, h_turned, [piece])
        parts = [
            weight * lax.psum_scatter(rows, "dom", scatter_dimension=1, tiled=True)
            for rows in (block[:states], block[states:])
        ]
        return (y_next, *parts)

    outward = [(2, 3), (1, 0)]
    core, chip, upper = me % 2, me // 2, level // 2
    keep = jnp.where(core == level % 2, 1, 0).astype(jnp.int32).reshape(1)
    near_route = [
        (((b // 2 * 2 + c) ^ 2) * 4 + b, (b // 2 * 2 + c) * 4 + b) for b in range(4) for c in (0, 1)
    ]
    near_across = lambda x: lax.ppermute(x, ("dom", "band"), near_route)
    second_owner, third_owner = [2, 2, 1, 1], [3, 3, 0, 0]

    ends, middle = [(0, 1), (2, 3)], [(1, 2)]
    first = [exchange(x, "band", ends) for x in following]
    second_middle = [exchange(x, "band", middle) for x in following]
    waited = (first[0], next_far[0])
    y_next, whole, other, *y_turned, second_middle[0] = from_grid(face_map, following, waited, second_middle[:1])
    next_far.append(crossed(other))
    second_out = [lax.ppermute(second_middle[0], "band", outward)]
    whole_paired = paired(whole)
    (first[0],) = gate(first[:1], (mark((y_next,)), whole_paired, second_middle[1]))
    third_middle = [exchange(first[0], "band", middle)]
    *near, second_middle[1] = sorted_products(keep, y_turned, following, first, 0, (), (), second_middle[1:])
    second_out.append(lax.ppermute(second_middle[1], "band", outward))
    h_turned = applied_next(band, on_chip(band, whole, whole_paired, None, after=near[:1]), next_far)
    (first[1],) = gate(first[1:], (h_turned[0], third_middle[0]))
    third_middle.append(exchange(first[1], "band", middle))
    kept, sent, third_middle[0] = sorted_products(keep, h_turned, following, first, 1, near, (), third_middle[:1])
    third_out = [lax.ppermute(third_middle[0], "band", outward)]
    sent = paired(sent)

    blocks = [*both_products(y_turned, h_turned, [second_middle[0], second_out[0]], 2, (kept,))]
    cores = [to_owner(blocks[0], second_owner, 1)]
    (near,) = plus(kept, sent, (blocks[0],))
    near_far = near_across(near)
    pieces = [second_middle[1], second_out[1]]
    block, third_middle[1] = both_products(y_turned, h_turned, pieces, 2, (near,), third_middle[1:])
    blocks.append(block)
    tails = [third_middle[1][:, : half // 2], third_middle[1][:, half // 2 :]]
    (second,) = plus(blocks[0], cores[0], (blocks[1],))
    second_far = to_owner(second, second_owner, 2)
    tails_out = [lax.ppermute(tails[0], "band", outward)]
    keep = jnp.where(core == upper, 1, 0).astype(jnp.int32).reshape(1)
    pieces = (blocks[1], third_middle[0], third_out[0])
    kept, sent = pair_products(keep, y_turned, h_turned, *pieces, (second,))
    sent = paired(sent)
    (tails[1],) = gate(tails[1:], (kept, second_far))
    tails_out.append(lax.ppermute(tails[1], "band", outward))
    (pair,) = plus(kept, sent, tails[1:])
    pair_route = [
        (((2 - b // 2 * 2 + c) ^ 2) * 4 + b, (2 - b // 2 * 2 + c) * 4 + b) for b in range(4) for c in (0, 1)
    ]
    pair_far = lax.ppermute(pair, ("dom", "band"), pair_route)
    blocks, waited = [], (pair,)
    for piece in zip(tails, tails_out):
        blocks += both_products(y_turned, h_turned, list(piece), 2, waited)
        waited = blocks[-1:]
    cores = [to_owner(block, third_owner, 1) for block in blocks]
    third = [*plus(blocks[0], cores[0], blocks[1:])]
    third += plus(blocks[1], cores[1], third)
    third_far = [to_owner(block, third_owner, 2) for block in third]
    is_near, is_second = chip == upper, core == upper
    flags = jnp.stack([is_near, ~is_near & is_second, ~is_near & ~is_second]).astype(jnp.int32)
    base = near_rows(flags, near, near_far, (third[1],))
    *outs, rest = finish_most(weight, flags, base, second, second_far, pair, pair_far, *third)
    return (y_next, *finish(weight, outs, rest, third_far))


def solution(mesh):
    placed = (
        P(("image", "dom"), "band"),
        P(("image", "dom"), "band"),
        P("dom", None),
        P("dom"),
        P("dom"),
        P(("image", "dom")),
    )
    return jax.shard_map(
        on_device,
        mesh=mesh,
        in_specs=placed,
        out_specs=(
            P(("image", "dom"), "band"),
            P(("image", "band"), "dom"),
            P(("image", "band"), "dom"),
        ),
        check_vma=False,
    )
```
